32 devices in a mesh: dp: 4 (over x, core), context: 2 (over y), expert: 4 (over z).
Axes of the slice: x: 2, y: 2, z: 4, core: 2. Of those that a mesh axis runs over, the one named last changes fastest.
Arguments:
- tokens: bfloat16 [4, 1024, 768], P('dp', ('context', 'expert')), may hold values from -6 to 6
- w_query: bfloat16 [2, 768, 768], replicated, may hold values from -0.02734375 to 0.02734375
- w_key: bfloat16 [2, 768, 768], replicated, may hold values from -0.21875 to 0.21875
- w_value: bfloat16 [2, 768, 768], replicated, may hold values from -0.21875 to 0.21875
- w_output: bfloat16 [2, 768, 768], replicated, may hold values from -3.5 to 3.5
- rel_bias: float32 [32, 12], replicated, may hold values from -6 to 6
- gain_attn: float32 [2, 768], replicated, may hold values from 0.1 to 1.9
- gain_moe: float32 [2, 768], replicated, may hold values from 0.1 to 1.9
- w_router: float32 [2, 768, 4], replicated, may hold values from -0.21875 to 0.21875
- w_in: bfloat16 [2, 4, 768, 3072], P(None, 'expert'), may hold values from -0.21875 to 0.21875
- w_out: bfloat16 [2, 4, 3072, 768], P(None, 'expert'), may hold values from -0.3125 to 0.3125
- routes: int32 [2, 4, 1024, 1], P(None, 'dp', ('context', 'expert')), may hold values from 0 to 3; in each aligned block of 128 rows (0 to 127, 128 to 255, ..., all dimensions but the last counted through in order) at most 40 rows name the same one
- kept: int32 [2, 4, 1024], P(None, 'dp', ('context', 'expert')), may hold values 0 or 1
- cotangent: bfloat16 [4, 1024, 768], P('dp', ('context', 'expert')), may hold values from -6 to 6
Outputs:
- out: bfloat16 [4, 1024, 768], P('dp', ('context', 'expert'))
- d_tokens: float32 [4, 1024, 768], P('dp', ('context', 'expert'))
- grad_query: float32 [2, 768, 768], P(None, ('dp', 'context', 'expert'))
- grad_key: float32 [2, 768, 768], P(None, ('dp', 'context', 'expert'))
- grad_value: float32 [2, 768, 768], P(None, ('dp', 'context', 'expert'))
- grad_output: float32 [2, 768, 768], P(None, ('dp', 'context', 'expert'))
- grad_rel_bias: float32 [32, 12], replicated
- grad_gain_attn: float32 [2, 768], P(None, ('dp', 'context', 'expert'))
- grad_gain_moe: float32 [2, 768], P(None, ('dp', 'context', 'expert'))
- grad_router: float32 [2, 768, 4], P(None, ('dp', 'context', 'expert'))
- grad_in: float32 [2, 4, 768, 3072], P(None, 'expert', ('dp', 'context'))
- grad_out: float32 [2, 4, 3072, 768], P(None, 'expert', ('dp', 'context'))
The draws below stay inside these ranges and needn't reach their ends.
Inputs may be any that keep to these rules, and one draw needn't show every extreme that they name: `routes`: in each layer, among the 128 positions of one sequence on one device (aligned groups), no expert is named more than 40 times, a bound that some block reaches. `kept`: 1 where a token is processed by its expert, 0 where it overflowed and passes on without the expert branch.
All inputs are finite; a program needn't handle non-finite values. No bound on the sum of `kept` on one device may be relied on, other than what follows from the above.
Results may differ from the reference program's by a relative error of at most 0.025.
Values may be sent and summed in bfloat16 or wider, within the bound.
A program may use at most 256 MiB of HBM per device.

```python
import math
import jax
import jax.numpy as jnp
import numpy as np
from jax import lax

D = 768
H = 12
HD = 64
FF = 3072
NB = 32
LAYERS = 2
SEQ_DEV = 128
EXPERTS = 4
SEQ_LEN = 1024
BATCH = 4
SEQ_CAP = 40


def set_ends(entries, own_key, least, top_value):
    dims = entries.shape
    place = [jax.random.randint(jax.random.fold_in(own_key, axis), (), 0, dims[axis]) for axis in range(len(dims))]
    entries = entries.at[tuple(place)].set(least)
    longest = dims.index(max(dims))
    place[longest] = (place[longest] + 1) % dims[longest]
    return entries.at[tuple(place)].set(top_value)


def shard_levels(key, shape, cuts, least, top_value):
    def one(axis_at, shards_of):
        steps = jax.random.uniform(jax.random.fold_in(jax.random.fold_in(key, 6), axis_at), (shards_of,), jnp.float32, least / len(cuts), top_value / len(cuts))
        return jnp.repeat(jnp.exp(steps), shape[axis_at] // shards_of).reshape((-1,) + (1,) * (len(shape) - axis_at - 1))

    loudness = one(*cuts[0])
    for cut in cuts[1:]:
        loudness = loudness * one(*cut)
    return loudness


def shared_out(key, own, number, rows, number_of, top, most, skew):
    order = jax.random.permutation(key, number_of)
    packed, usual = shares(number_of, rows * top, most, skew, True), shares(number_of, rows * top, most, skew, False)
    places = jnp.arange(number_of)

    def named(sizes, rotation):
        used = int((sizes > 0).sum())
        fixed = max(1, used // 4)
        moved = fixed + (places - fixed + rotation * (used - fixed)) % max(1, number_of - fixed)
        return jnp.zeros((number_of,), jnp.int32).at[order[jnp.where(places < fixed, places, moved)]].set(jnp.asarray(sizes, jnp.int32))

    sizes = jnp.where(number % 4 == 0, named(packed, number // 4), named(usual, number - number // 4 - 1))
    mixed = jax.random.permutation(jax.random.fold_in(own, 3), number_of)
    giver, sink = mixed[0:number_of // 2 * 2:2], mixed[1:number_of // 2 * 2:2]
    slack = jnp.minimum(sizes[giver] - 1, most - sizes[sink]) // 2
    slack = jnp.where((giver == order[0]) | (sink == order[0]) | (sizes[sink] == 0), 0, jnp.maximum(slack, 0))
    moved = jax.random.randint(jax.random.fold_in(own, 4), (number_of // 2,), 0, 1 << 20) % (slack + 1)
    sizes = sizes.at[giver].add(-moved).at[sink].add(moved)
    members = jnp.searchsorted(jnp.cumsum(sizes), jnp.arange(rows * top), side="right").astype(jnp.int32)
    listing = members.reshape(top, rows).T
    listing = listing[jax.random.permutation(jax.random.fold_in(own, 1), rows)]
    rotation = jax.random.randint(jax.random.fold_in(own, 2), (rows, 1), 0, top)
    return jnp.take_along_axis(listing, (jnp.arange(top)[None, :] + rotation) % top, axis=1)


def shares(count, total, most, lean, full):
    loads = [(1 << 20) // math.isqrt(rank ** lean) + 1 for rank in range(1, count + 1)]
    largest = most if full else min(most, max(-(-total // count), total * loads[0] // sum(loads)))
    least = 1 if total - largest >= count - 1 else 0
    given, surplus = [largest] + [least] * (count - 1), total - largest - least * (count - 1)
    while surplus > 0:
        free = [i for i in range(1, count) if given[i] < largest] or [i for i in range(1, count) if given[i] < most]
        pool, budget = sum([loads[i] for i in free]), surplus
        for i in free:
            more = min(most - given[i], max(1, budget * loads[i] // pool), surplus)
            given[i] = given[i] + more
            surplus = surplus - more
    return np.array(given)


def scatter_about(stream_key, extent, spread, most, shards=(), kind=jnp.bfloat16):
    entries = jax.random.normal(stream_key, extent, jnp.float32) * spread
    if len(shards) > 0:
        entries = shard_levels(stream_key, extent, shards, -0.22, 0.18) * entries
    return jnp.clip(entries, min=-most, max=most).astype(kind)


def setup_inputs(seed: int = 0) -> dict:
    streams_of = jax.random.split(jax.random.key(seed), 15)
    tokens = scatter_about(streams_of[0], (BATCH, SEQ_LEN, D), 1.0, 6.0, ((0, 4), (1, 8)))
    w_query = scatter_about(streams_of[1], (LAYERS, D, D), (D * HD) ** -0.5, 0.02734375)
    w_key = scatter_about(streams_of[2], (LAYERS, D, D), D ** -0.5, 0.21875)
    w_value = scatter_about(streams_of[3], (LAYERS, D, D), D ** -0.5, 0.21875)
    w_output = scatter_about(streams_of[4], (LAYERS, D, D), 3 ** -0.5, 3.5)
    rel_bias = scatter_about(streams_of[5], (NB, H), 1.0, 6.0, (), jnp.float32)
    gain_attn = jnp.clip(1.0 + 0.18 * jax.random.normal(streams_of[6], (LAYERS, D), jnp.float32), 0.1, 1.9)
    gain_moe = jnp.clip(1.0 + 0.18 * jax.random.normal(streams_of[7], (LAYERS, D), jnp.float32), 0.1, 1.9)
    w_router = scatter_about(streams_of[8], (LAYERS, D, EXPERTS), D ** -0.5, 0.21875, (), jnp.float32)
    w_in = scatter_about(streams_of[9], (LAYERS, EXPERTS, D, FF), D ** -0.5, 0.21875, ((1, 4),))
    w_out = scatter_about(streams_of[10], (LAYERS, EXPERTS, FF, D), (FF // 8) ** -0.5, 0.3125, ((1, 4),))
    routes_keys = jax.random.split(jax.random.fold_in(streams_of[11], 1), LAYERS * BATCH * SEQ_LEN // SEQ_DEV)
    routes_turns = jax.random.permutation(jax.random.fold_in(streams_of[11], 3), LAYERS * BATCH * SEQ_LEN // SEQ_DEV)
    routes = jax.vmap(lambda own, number: shared_out(jax.random.fold_in(streams_of[11], 2), own, number, SEQ_DEV, EXPERTS, 1, SEQ_CAP, 2))(routes_keys, routes_turns).reshape((LAYERS, BATCH, SEQ_LEN, 1))
    kept = set_ends((jax.random.randint(streams_of[12], (LAYERS, BATCH, SEQ_LEN), 0, 8) < 7).astype(jnp.int32), jax.random.fold_in(streams_of[12], 1), 0, 1)
    cotangent = scatter_about(streams_of[13], (BATCH, SEQ_LEN, D), 1.0, 6.0, ((0, 4), (1, 8)))
    return {"tokens": tokens, "w_query": w_query, "w_key": w_key, "w_value": w_value, "w_output": w_output, "rel_bias": rel_bias, "gain_attn": gain_attn, "gain_moe": gain_moe, "w_router": w_router, "w_in": w_in, "w_out": w_out, "routes": routes, "kept": kept, "cotangent": cotangent}


highest = lax.Precision.HIGHEST
epsilon = 1e-06
thresholds = (12, 16, 23, 32, 46, 64, 91)

@jax.custom_vjp
def low(v):
    return lax.optimization_barrier(v.astype(jnp.bfloat16)).astype(jnp.float32)

@jax.custom_vjp
def low_back(v):
    return v

def low_keep(v):
    return (low(v), None)

def low_pass(kept, grad):
    return (grad,)

def back_keep(v):
    return (v, None)

def back_low(kept, grad):
    return (low(grad),)
low.defvjp(low_keep, low_pass)
low_back.defvjp(back_keep, back_low)

def rounded(value):
    return low_back(low(value))

def root_norm(value, gain):
    return value * lax.rsqrt(lax.optimization_barrier(jnp.mean(value * value, axis=-1, keepdims=True)) + epsilon) * gain

def bucket_of(offset):
    distance = jnp.abs(offset)
    beyond = 8 + sum(((distance >= limit).astype(jnp.int32) for limit in thresholds))
    inside = jnp.where(distance < 8, distance, beyond)
    return inside + jnp.where(offset > 0, 16, 0)

def attend_sequence(query, keys, values, table):
    length = query.shape[0]
    block = 512 if length % 512 == 0 else length

    def one_block(index):
        first = index.astype(jnp.int32) * block
        part = lax.dynamic_slice_in_dim(query, first, block, 0)
        offsets = lax.iota(jnp.int32, length)[None, :] - (first + lax.iota(jnp.int32, block))[:, None]
        bias = jnp.transpose(table[bucket_of(offsets)], (2, 0, 1))
        scores = jnp.einsum('ihd,jhd->hij', part, keys, precision=highest) + bias
        chances = jax.nn.softmax(low_back(scores), axis=-1)
        return jnp.einsum('hij,jhd->ihd', chances, values, precision=highest)
    blocks = lax.map(jax.checkpoint(one_block), jnp.arange(length // block))
    return blocks.reshape(length, -1)

def expert_apply(sent, inner_w, outer_w):
    before = low_back(jnp.einsum('bld,df->blf', sent, inner_w, precision=highest))
    hidden = low(jax.nn.gelu(before))
    return rounded(jnp.einsum('blf,fd->bld', hidden, outer_w, precision=highest))

def forward(residual, w_query, w_key, w_value, w_output, rel_bias, gain_attn, gain_moe, w_router, w_in, w_out, routes, kept):
    batch, length, width = residual.shape
    heads = rel_bias.shape[1]
    expert_step = jax.checkpoint(expert_apply)
    for layer in range(LAYERS):
        normed = low(root_norm(residual, gain_attn[layer]))
        query = rounded(jnp.einsum('bld,de->ble', normed, w_query[layer], precision=highest))
        keys = rounded(jnp.einsum('bld,de->ble', normed, w_key[layer], precision=highest))
        values = rounded(jnp.einsum('bld,de->ble', normed, w_value[layer], precision=highest))

        def per_sequence(triple):
            one_q, one_k, one_v = triple
            return attend_sequence(one_q.reshape(length, heads, -1), one_k.reshape(length, heads, -1), one_v.reshape(length, heads, -1), rel_bias)
        merged = lax.map(per_sequence, (query, keys, values))
        branch = low_back(jnp.einsum('bld,de->ble', rounded(merged), w_output[layer], precision=highest))
        middle = residual + branch
        moe_in = root_norm(middle, gain_moe[layer])
        router = jax.nn.softmax(jnp.einsum('bld,de->ble', moe_in, w_router[layer], precision=highest), axis=-1)
        chosen = (routes[layer][..., 0][..., None] == lax.iota(jnp.int32, EXPERTS)).astype(jnp.float32)
        gate = lax.optimization_barrier(jnp.sum(router * chosen, axis=-1)) * kept[layer].astype(jnp.float32)
        sent = rounded(moe_in)
        mixture = jnp.zeros_like(middle)
        for expert in range(EXPERTS):
            mixture = mixture + chosen[..., expert:expert + 1] * expert_step(sent, w_in[layer, expert], w_out[layer, expert])
        residual = middle + gate[..., None] * mixture
    return residual

def reference(tokens, w_query, w_key, w_value, w_output, rel_bias, gain_attn, gain_moe, w_router, w_in, w_out, routes, kept, cotangent):
    floats = tuple((item.astype(jnp.float32) for item in (tokens, w_query, w_key, w_value, w_output, rel_bias, gain_attn, gain_moe, w_router, w_in, w_out)))

    def run(*params):
        return forward(*params, routes, kept)
    result, pull = jax.vjp(run, *floats)
    grads = pull(cotangent.astype(jnp.float32))
    return (result.astype(jnp.bfloat16), grads[0], grads[1], grads[2], grads[3], grads[4], grads[5], grads[6], grads[7], grads[8], grads[9], grads[10])
```

```python
import functools

import jax
import jax.numpy as jnp
import numpy as np
from jax import lax
from jax.experimental import pallas as pl
from jax.experimental.pallas import tpu as pltpu
from jax.sharding import PartitionSpec as P

highest = lax.Precision.HIGHEST
epsilon = 1e-06
thresholds = (12, 16, 23, 32, 46, 64, 91)
MESH = pl.DeviceIdType.MESH
GROUP = 4
HEAD = 64
BLOCK = 128
FCHUNK = 512
f32, bf16 = jnp.float32, jnp.bfloat16


def div(a, b):
    return lax.div(a, jnp.int32(b))


def rem(a, b):
    return lax.rem(a, jnp.int32(b))


class Place:
    def __init__(self, parts, experts):
        self.parts, self.experts = parts, experts
        self.dp = lax.axis_index("dp")
        self.context = lax.axis_index("context")
        self.expert = lax.axis_index("expert")
        self.core = rem(self.dp, 2)
        self.far = div(self.context, 2)
        self.block = 2 * rem(self.context, 2) + div(self.dp, 2)
        self.part = 2 * self.far + self.core

    def flipped(self, flip):
        low = rem(rem(self.block, 2) + flip % 2, 2)
        high = rem(div(self.block, 2) + flip // 2, 2)
        return 2 * high + low

    def group_device(self, block):
        return {"dp": 2 * rem(block, 2) + self.core, "context": 2 * self.far + div(block, 2)}

    def part_other(self, step):
        return rem(self.part + step, self.parts)

    def part_device(self, part):
        return {
            "dp": self.dp - self.core + rem(part, 2),
            "context": 2 * div(part, 2) + rem(self.context, 2),
        }

    def expert_other(self, step):
        return rem(self.expert + step, self.experts)

    def offset(self, part, block, query_block):
        return 8 * (part // 2 - self.far) + 2 * (block - query_block) + (part % 2 - self.core)

    def bias_index(self, part, block, query_block):
        offset = self.offset(part, block, query_block)
        return jnp.minimum(jnp.maximum(offset, -2), 2) + 2

    def greet(self, expert=True):
        partners = [self.group_device(self.flipped(flip)) for flip in (1, 2, 3)]
        partners += [self.part_device(self.part_other(step)) for step in range(1, self.parts)]
        if expert:
            partners += [{"expert": self.expert_other(step)} for step in range(1, self.experts)]
        barrier = pltpu.get_barrier_semaphore()
        for partner in partners:
            pl.semaphore_signal(barrier, inc=1, device_id=partner, device_id_type=MESH)
        pl.semaphore_wait(barrier, len(partners))


def remote(source, target, send, receive, device):
    return pltpu.make_async_remote_copy(
        src_ref=source,
        dst_ref=target,
        send_sem=send,
        recv_sem=receive,
        device_id=device,
        device_id_type=MESH,
    )


def dot(a, b):
    return jnp.dot(a, b, preferred_element_type=f32)


def dot_nt(a, b):
    return lax.dot_general(a, b, (((1,), (1,)), ((), ())), preferred_element_type=f32)


def dot_tn(a, b):
    return lax.dot_general(a, b, (((0,), (0,)), ((), ())), preferred_element_type=f32)


def root_scale(value):
    return lax.rsqrt(jnp.mean(value * value, axis=-1, keepdims=True) + epsilon)


def lanes(rows, width):
    return lax.broadcasted_iota(jnp.int32, (rows, width), 1)


def gelu_parts(value):
    scale = 0.7978845608028654
    square = value * value
    inner = jnp.tanh(scale * (value + 0.044715 * (square * value)))
    half = 0.5 * (1.0 + inner)
    slope = half + 0.5 * value * (1.0 - inner * inner) * (scale * (1.0 + 3 * 0.044715 * square))
    return value * half, slope


def gelu(value):
    scale = 0.7978845608028654
    return value * (0.5 * (1.0 + jnp.tanh(scale * (value + 0.044715 * (value * value * value)))))


def forward_kernel(
    layer,
    parts,
    experts,
    x,
    gains,
    w_router,
    select,
    chosen,
    bias,
    w_qkv_hbm,
    w_output_hbm,
    w_in_hbm,
    w_out_hbm,
    normed,
    query,
    pair,
    merged,
    log_total,
    merged_low,
    middle,
    router,
    picked,
    arrived,
    before,
    x_next,
    w_qkv,
    w_output,
    w_in,
    w_out,
    scores,
    merged_mine,
    slots,
    total,
    answer,
    returned,
    load_sem,
    group_send,
    group_recv,
    part_send,
    part_recv,
    merge_send,
    merge_recv,
    slot_send,
    slot_recv,
    back_send,
    back_recv,
):
    here = Place(parts, experts)
    heads = 3
    wide = heads * HEAD
    loads = [
        pltpu.make_async_copy(w_qkv_hbm.at[layer], w_qkv, load_sem.at[0]),
        pltpu.make_async_copy(w_output_hbm.at[layer], w_output, load_sem.at[1]),
        pltpu.make_async_copy(w_in_hbm.at[layer, 0], w_in, load_sem.at[2]),
        pltpu.make_async_copy(w_out_hbm.at[layer, 0], w_out, load_sem.at[3]),
    ]
    for load in loads:
        load.start()
    value = x[...]
    block = here.block
    normed[block] = (value * root_scale(value) * gains[0:1, :]).astype(bf16)
    here.greet()

    def gather(flip, source):
        return remote(
            normed.at[source],
            normed.at[source],
            group_send.at[flip - 1],
            group_recv.at[flip - 1],
            here.group_device(here.flipped(flip)),
        )

    for flip in (1, 2, 3):
        gather(flip, block).start()

    def hand_pair(step, part, of_block):
        return remote(
            pair.at[part, of_block],
            pair.at[part, of_block],
            part_send.at[step - 1, of_block],
            part_recv.at[step - 1, of_block],
            here.part_device(here.part_other(step)),
        )

    def project(of_block):
        made = dot(normed[of_block], w_qkv[...]).astype(bf16)
        pair[here.part, of_block] = made[:, : 2 * wide]
        query[of_block] = made[:, 2 * wide :]
        for step in range(1, parts):
            hand_pair(step, here.part, of_block).start()

    loads[0].wait()
    project(block)
    for flip in (1, 2, 3):
        source = here.flipped(flip)
        gather(flip, source).wait_recv()
        project(source)
    for step in range(1, parts):
        source = rem(here.part + parts - step, parts)
        for of_block in range(GROUP):
            hand_pair(step, source, of_block).wait_recv()

    lane = lanes(BLOCK, wide)
    lane_out = lanes(BLOCK, 2 * BLOCK)
    lane_log = lanes(BLOCK, BLOCK)

    def hand_merged(flip, source):
        return remote(
            merged_mine.at[here.flipped(flip)],
            merged_low.at[source],
            merge_send.at[flip - 1],
            merge_recv.at[flip - 1],
            here.group_device(here.flipped(flip)),
        )

    for flip in (3, 1, 2, 0):
        mine = here.flipped(flip)
        rows = query[mine]
        gathered = jnp.zeros((BLOCK, 2 * BLOCK), f32)
        logs = jnp.zeros((BLOCK, BLOCK), f32)
        for head in range(heads):
            masked = jnp.where(lane // HEAD == head, rows, jnp.zeros_like(rows))
            top = jnp.full((BLOCK, 1), -1e30, f32)
            for part in range(parts):
                keys = pair[part].reshape(GROUP * BLOCK, 2 * wide)[:, :wide]
                raw = dot_nt(masked, keys)
                for of_block in range(GROUP):
                    piece = (
                        raw[:, of_block * BLOCK : (of_block + 1) * BLOCK]
                        + bias[head, here.bias_index(part, of_block, mine)]
                    )
                    scores[part * GROUP + of_block] = piece
                    top = jnp.maximum(top, jnp.max(piece, axis=-1, keepdims=True))
            summed = jnp.zeros((BLOCK, 1), f32)
            out = jnp.zeros((BLOCK, 2 * BLOCK), f32)
            for part in range(parts):
                pieces = []
                for of_block in range(GROUP):
                    weight = jnp.exp(scores[part * GROUP + of_block] - top)
                    summed = summed + jnp.sum(weight, axis=-1, keepdims=True)
                    pieces.append(weight.astype(bf16))
                values = pair[part].reshape(GROUP * BLOCK, 2 * wide)[:, BLOCK:]
                out = out + dot(jnp.concatenate(pieces, axis=1), values)
            gathered = jnp.where((lane_out + HEAD) // HEAD == head + 2, out / summed, gathered)
            logs = jnp.where(lane_log == head, top + jnp.log(summed), logs)
        final = gathered[:, HEAD:]
        merged[mine] = final
        log_total[mine] = logs
        if flip:
            merged_mine[mine] = final.astype(bf16)
            hand_merged(flip, block).start()
        else:
            merged_low[block] = final.astype(bf16)

    for flip in (1, 2, 3):
        hand_merged(flip, here.flipped(flip)).wait_recv()
    loads[1].wait()
    mid = value
    for of_block in range(GROUP):
        mid = mid + dot(merged_low[of_block], w_output[of_block * wide : (of_block + 1) * wide, :])
    middle[...] = mid
    moe_in = mid * root_scale(mid) * gains[1:2, :]
    moe_low = moe_in.astype(bf16)

    def hand_slots(step, source):
        return remote(
            slots.at[here.expert_other(step)],
            arrived.at[source],
            slot_send.at[step - 1],
            slot_recv.at[step - 1],
            {"expert": here.expert_other(step)},
        )

    for expert in range(experts):
        slots[expert] = dot(select[expert], moe_low).astype(bf16)
    for step in range(1, experts):
        hand_slots(step, here.expert).start()
    arrived[here.expert] = slots[here.expert]
    logits = jnp.dot(moe_in, w_router[...], precision=highest, preferred_element_type=f32)
    logits = jnp.where(lane_log < experts, logits, -1e30)
    raised = jnp.exp(logits - jnp.max(logits, axis=-1, keepdims=True))
    chances = raised / jnp.sum(raised, axis=-1, keepdims=True)
    router[...] = chances
    gate = jnp.sum(chances * chosen[...], axis=-1, keepdims=True)
    loads[2].wait()
    loads[3].wait()
    for step in range(1, experts):
        hand_slots(step, rem(here.expert + experts - step, experts)).wait_recv()
    given = jnp.concatenate([arrived[expert].astype(f32) for expert in range(experts)], axis=0)
    given = given.astype(bf16)
    room = arrived.shape[1]
    total[...] = jnp.zeros_like(total)

    @pl.loop(0, w_in.shape[1] // FCHUNK)
    def _(index):
        columns = pl.ds(pl.multiple_of(index * FCHUNK, FCHUNK), FCHUNK)
        first = dot(given, w_in[:, columns])
        before[:, columns] = first
        total[...] += dot(gelu(first).astype(bf16), w_out[columns, :])

    def hand_answer(step, source):
        return remote(
            answer.at[here.expert_other(step)],
            returned.at[source],
            back_send.at[step - 1],
            back_recv.at[step - 1],
            {"expert": here.expert_other(step)},
        )

    for expert in range(experts):
        answer[expert] = total[expert * room : (expert + 1) * room, :].astype(bf16)
    for step in range(1, experts):
        hand_answer(step, here.expert).start()
    returned[here.expert] = answer[here.expert]
    for step in range(1, experts):
        hand_answer(step, rem(here.expert + experts - step, experts)).wait_recv()
    back = jnp.zeros_like(value)
    for expert in range(experts):
        back = back + dot_tn(select[expert], returned[expert])
    picked[...] = back.astype(bf16)
    x_next[...] = mid + gate * back
    for flip in (1, 2, 3):
        gather(flip, block).wait_send()
        hand_merged(flip, block).wait_send()
    for step in range(1, parts):
        for of_block in range(GROUP):
            hand_pair(step, here.part, of_block).wait_send()
    for step in range(1, experts):
        hand_slots(step, here.expert).wait_send()
        hand_answer(step, here.expert).wait_send()


VMEM = pl.BlockSpec(memory_space=pltpu.VMEM)
ANY = pl.BlockSpec(memory_space=pl.ANY)
DMA = pltpu.SemaphoreType.DMA


def forward_layer(layer, x, gains, w_router, select, chosen, bias, w_qkv, w_output, w_in, w_out):
    count, width = x.shape
    parts, experts = lax.axis_size("context"), lax.axis_size("expert")
    wide = w_qkv.shape[2] // 3
    room = select.shape[1]
    hidden = w_in.shape[3]
    shape = jax.ShapeDtypeStruct
    return pl.pallas_call(
        functools.partial(forward_kernel, layer, parts, experts),
        out_shape=[
            shape((GROUP, count, width), bf16),
            shape((GROUP, count, wide), bf16),
            shape((parts, GROUP, count, 2 * wide), bf16),
            shape((GROUP, count, wide), f32),
            shape((GROUP, count, 128), f32),
            shape((GROUP, count, wide), bf16),
            shape((count, width), f32),
            shape((count, 128), f32),
            shape((count, width), bf16),
            shape((experts, room, width), bf16),
            shape((experts * room, hidden), f32),
            shape((count, width), f32),
        ],
        in_specs=[VMEM] * 6 + [ANY] * 4,
        out_specs=[VMEM] * 12,
        scratch_shapes=[
            pltpu.VMEM((width, 3 * wide), bf16),
            pltpu.VMEM((width, width), bf16),
            pltpu.VMEM((width, hidden), bf16),
            pltpu.VMEM((hidden, width), bf16),
            pltpu.VMEM((parts * GROUP, count, BLOCK), f32),
            pltpu.VMEM((GROUP, count, wide), bf16),
            pltpu.VMEM((experts, room, width), bf16),
            pltpu.VMEM((experts * room, width), f32),
            pltpu.VMEM((experts, room, width), bf16),
            pltpu.VMEM((experts, room, width), bf16),
            DMA((4,)),
            DMA((3,)),
            DMA((3,)),
            DMA((parts - 1, GROUP)),
            DMA((parts - 1, GROUP)),
            DMA((3,)),
            DMA((3,)),
            DMA((experts - 1,)),
            DMA((experts - 1,)),
            DMA((experts - 1,)),
            DMA((experts - 1,)),
        ],
        compiler_params=pltpu.CompilerParams(
            collective_id=layer, has_side_effects=True, vmem_limit_bytes=56 * 2**20
        ),
        name="layer_forward",
    )(x, gains, w_router, select, chosen, bias, w_qkv, w_output, w_in, w_out)


def bucket_blocks():
    row = np.arange(BLOCK)[:, None]
    column = np.arange(BLOCK)[None, :]
    made = []
    for offset in (-2, -1, 0, 1, 2):
        r = offset * BLOCK + column - row
        n = np.abs(r)
        beyond = 8 + sum((n >= limit).astype(np.int32) for limit in thresholds)
        made.append(np.where(n < 8, n, beyond) + np.where(r > 0, 16, 0))
    return np.stack(made).astype(np.int32)


def bias_blocks(rel_bias, first_head):
    mine = lax.dynamic_slice_in_dim(rel_bias, first_head, 3, 1)
    buckets = jnp.asarray(bucket_blocks())
    made = jnp.zeros((3,) + buckets.shape, f32)
    for bucket in range(rel_bias.shape[0]):
        made = jnp.where(buckets[None] == bucket, mine[bucket][:, None, None, None], made)
    return made


def swap_route():
    d, c, e = (lax.axis_size(name) for name in ("dp", "context", "expert"))
    return [((i * c + j) * e + k, (k * c + j) * e + i) for i in range(d) for j in range(c) for k in range(e)]


def swapped(block):
    return lax.ppermute(block, ("dp", "context", "expert"), swap_route())


def routing(routes, kept, experts, room):
    layers, count = routes.shape
    chosen = (routes[..., None] == lax.iota(jnp.int32, experts)).astype(jnp.int32)
    rank = jnp.sum(chosen * (jnp.cumsum(chosen, axis=1) - 1), axis=-1)
    target = routes * room + rank
    slot = lax.iota(jnp.int32, experts * room)[None, :, None]
    select = ((slot == target[:, None, :]) & (kept[:, None, :] > 0)).astype(bf16)
    live = ((routes[..., None] == lax.iota(jnp.int32, 128)) & (kept[..., None] > 0)).astype(f32)
    return select.reshape(layers, experts, room, count), live


def forward_path(tokens, w_query, w_key, w_value, w_output, rel_bias, gain_attn, gain_moe, w_router, w_in, w_out, routes, kept):
    batch, count, width = tokens.shape
    experts = w_router.shape[2]
    room = count * 5 // (4 * experts)
    layers = w_query.shape[0]
    block = 2 * (lax.axis_index("context") % 2) + lax.axis_index("dp") // 2
    x = swapped(tokens[0]).astype(f32)
    marks = swapped(jnp.stack([routes[:, 0, :, 0], kept[:, 0, :]]))
    select, chosen = routing(marks[0], marks[1], experts, room)
    bias = bias_blocks(rel_bias, 3 * block)
    wide = 3 * HEAD
    w_qkv = jnp.concatenate(
        [lax.dynamic_slice_in_dim(w, wide * block, wide, 2) for w in (w_key, w_value, w_query)], axis=2
    )
    router_wide = jnp.pad(w_router, ((0, 0), (0, 0), (0, 128 - experts)))
    for layer in range(layers):
        gains = jnp.stack([gain_attn[layer], gain_moe[layer]])
        saved = forward_layer(layer, x, gains, router_wide[layer], select[layer], chosen[layer], bias, w_qkv, w_output, w_in, w_out)
        x = saved[-1]
    return swapped(x.astype(bf16))[None]


def passed_along(block, axis, distance):
    devices = range(lax.axis_size(axis))
    route = [((i - distance) % len(devices), i) for i in devices]
    return lax.ppermute(block, axis, route)


def root_norm(value, gain):
    return value * lax.rsqrt(jnp.mean(value * value, axis=-1, keepdims=True) + epsilon) * gain


def bucket_of(offset):
    distance = jnp.abs(offset)
    beyond = 8 + sum(((distance >= limit).astype(jnp.int32) for limit in thresholds))
    inside = jnp.where(distance < 8, distance, beyond)
    return inside + jnp.where(offset > 0, 16, 0)


def bucket_hot(first, width, buckets):
    offsets = first + lax.iota(jnp.int32, width)
    return (bucket_of(offsets)[:, None] == lax.iota(jnp.int32, buckets)[None, :]).astype(
        jnp.float32
    )


def spread_line(line, count):
    heads, width = line.shape
    tiled = jnp.tile(line, (1, count))[:, : count * (width - 1)]
    return tiled.reshape(heads, count, width - 1)[:, :, count - 1 :]


def fold_line(block, count, columns):
    heads = block.shape[0]
    width = count + columns
    padded = jnp.pad(block, ((0, 0), (0, 0), (count - 1, 0)))
    flat = jnp.pad(padded.reshape(heads, count * (width - 1)), ((0, 0), (0, count)))
    return jnp.sum(flat.reshape(heads, count, width), axis=1)


def split_product(form, weights, other):
    upper = weights.astype(jnp.bfloat16)
    lower = (weights - upper.astype(jnp.float32)).astype(jnp.bfloat16)
    return jnp.einsum(form, upper, other, preferred_element_type=jnp.float32) + jnp.einsum(
        form, lower, other, preferred_element_type=jnp.float32
    )


def block_scores(query, keys, table, first):
    batch, count, width = query.shape
    columns = keys.shape[1]
    heads = table.shape[1]
    onehot = bucket_hot(first, count + columns, table.shape[0])
    line = jnp.dot(onehot, table, precision=highest).T
    shaped_query = query.reshape(batch, count, heads, width // heads)
    shaped_keys = keys.reshape(batch, columns, heads, width // heads)
    scores = jnp.einsum(
        "sihd,sjhd->shij", shaped_query, shaped_keys, preferred_element_type=jnp.float32
    )
    return (scores + spread_line(line, count)[None], onehot)


def forward_block(state, pair, query, table, first):
    top, total, summed = state
    scores, unused = block_scores(query, pair[0], table, first)
    new_top = jnp.maximum(top, jnp.max(scores, axis=-1))
    factor = jnp.exp(top - new_top)
    weights = jnp.exp(scores - new_top[..., None])
    total = total * factor + jnp.sum(weights, axis=-1)
    batch, columns, width = pair.shape[1:]
    heads = top.shape[1]
    values = pair[1].reshape(batch, columns, heads, width // heads)
    summed = summed * factor[..., None] + split_product("shij,sjhd->shid", weights, values)
    return (new_top, total, summed)


def attend(query, pair, table, first_for, context_size):
    batch, count, width = query.shape
    heads = table.shape[1]
    start_state = (
        jnp.full((batch, heads, count), -1e30, jnp.float32),
        jnp.zeros((batch, heads, count), jnp.float32),
        jnp.zeros((batch, heads, count, width // heads), jnp.float32),
    )
    state = forward_block(start_state, pair, query, table, first_for(0))

    def step_fn(carry, step):
        moving, inner = carry
        moving = passed_along(moving, "context", 1)
        return ((moving, forward_block(inner, moving, query, table, first_for(step))), None)

    (unused, state), unused_out = lax.scan(
        step_fn, (pair, state), jnp.arange(1, context_size, dtype=jnp.int32)
    )
    top, total, summed = state
    merged = jnp.transpose(summed / total[..., None], (0, 2, 1, 3)).reshape(batch, count, width)
    return (merged, top + jnp.log(total))


def backward_block(query, grad_merged, delta, log_total, pair, table, first):
    scores, onehot = block_scores(query, pair[0], table, first)
    chances = jnp.exp(scores - log_total[..., None])
    batch, columns, width = pair.shape[1:]
    count = query.shape[1]
    heads = table.shape[1]
    keys = pair[0].reshape(batch, columns, heads, width // heads)
    values = pair[1].reshape(batch, columns, heads, width // heads)
    shaped_query = query.reshape(batch, count, heads, width // heads)
    shaped_grad = grad_merged.reshape(batch, count, heads, width // heads)
    dot_grad = jnp.einsum(
        "sihd,sjhd->shij", shaped_grad, values, preferred_element_type=jnp.float32
    )
    score_grad = (chances * (dot_grad - delta[..., None])).astype(jnp.bfloat16)
    query_grad = jnp.einsum("shij,sjhd->sihd", score_grad, keys, preferred_element_type=jnp.float32)
    key_grad = jnp.einsum(
        "shij,sihd->sjhd", score_grad, shaped_query, preferred_element_type=jnp.float32
    )
    value_grad = split_product("shij,sihd->sjhd", chances, shaped_grad)
    diagonal = fold_line(jnp.sum(score_grad.astype(jnp.float32), axis=0), count, columns)
    table_grad = jnp.einsum("wb,hw->bh", onehot, diagonal, precision=highest)
    pair_grad = jnp.stack(
        [key_grad.reshape(batch, columns, width), value_grad.reshape(batch, columns, width)]
    )
    return (query_grad.reshape(batch, count, width), pair_grad, table_grad)


def attend_back(
    query, grad_merged, delta, log_total, pair, table, first_for, source_for, context_size
):
    query_grad, pair_grad, table_grad = backward_block(
        query, grad_merged, delta, log_total, pair, table, first_for(0)
    )
    batch, columns, width = pair.shape[1:]
    steps = jnp.arange(1, context_size, dtype=jnp.int32)

    def move_keys(moving):
        return passed_along(moving, "context", 1)

    store = jnp.zeros((2, batch, context_size * columns, width), jnp.float32)
    store = lax.dynamic_update_slice_in_dim(store, pair_grad, source_for(0) * columns, 2)

    def step_fn(carry, step):
        moving, store_now, query_sum, table_sum = carry
        moving = move_keys(moving)
        more_query, more_pair, more_table = backward_block(
            query, grad_merged, delta, log_total, moving, table, first_for(step)
        )
        store_now = lax.dynamic_update_slice_in_dim(
            store_now, more_pair, source_for(step) * columns, 2
        )
        return ((moving, store_now, query_sum + more_query, table_sum + more_table), None)

    (unused, store, query_grad, table_grad), unused_out = lax.scan(
        step_fn, (pair, store, query_grad, table_grad), steps
    )
    own = lax.psum_scatter(
        store.astype(jnp.bfloat16), ("context", "expert"), scatter_dimension=2, tiled=True
    ).astype(jnp.float32)
    return (query_grad, own, table_grad)


def expert_apply(inner_w, outer_w, arrived):
    slots = arrived.shape[1]
    local = inner_w.shape[0]
    grouped = arrived.reshape(-1, local, slots, arrived.shape[2])
    before = jnp.einsum("gend,edf->genf", grouped, inner_w, preferred_element_type=jnp.float32)
    hidden = jax.nn.gelu(before).astype(jnp.bfloat16)
    answer = jnp.einsum(
        "genf,efd->gend", hidden, outer_w, preferred_element_type=jnp.float32
    ).astype(jnp.bfloat16)
    return (answer.reshape(arrived.shape), before.reshape(arrived.shape[0], slots, -1), arrived)


def on_device(
    tokens,
    w_query,
    w_key,
    w_value,
    w_output,
    rel_bias,
    gain_attn,
    gain_moe,
    w_router,
    w_in,
    w_out,
    routes,
    kept,
    cotangent,
):
    batch, count, width = tokens.shape
    layers = w_query.shape[0]
    heads = rel_bias.shape[1]
    experts = w_router.shape[2]
    local_experts = w_in.shape[1]
    hidden_width = w_in.shape[3]
    context_size = lax.axis_size("context")
    group = lax.axis_size("expert")
    here = lax.axis_index("context")
    place = lax.axis_index("expert")
    columns = group * count
    anchor = (here * group + place) * count
    token_count = batch * count
    room = count * 5 // (4 * experts)
    capacity = batch * room

    def source_for(step):
        return (here - step) % context_size

    def first_for(step):
        return source_for(step) * columns - anchor - (count - 1)

    residual = tokens.astype(jnp.float32).reshape(token_count, width)
    saved = []
    for layer in range(layers):
        normed_low = root_norm(residual, gain_attn[layer]).astype(jnp.bfloat16)
        query = (
            jnp.dot(normed_low, w_query[layer], preferred_element_type=jnp.float32)
            .astype(jnp.bfloat16)
            .reshape(batch, count, width)
        )
        keys = (
            jnp.dot(normed_low, w_key[layer], preferred_element_type=jnp.float32)
            .astype(jnp.bfloat16)
            .reshape(batch, count, width)
        )
        values = (
            jnp.dot(normed_low, w_value[layer], preferred_element_type=jnp.float32)
            .astype(jnp.bfloat16)
            .reshape(batch, count, width)
        )
        pair = lax.all_gather(jnp.stack([keys, values]), "expert", axis=2, tiled=True)
        merged, log_total = attend(query, pair, rel_bias, first_for, context_size)
        merged_low = merged.astype(jnp.bfloat16).reshape(token_count, width)
        middle = residual + jnp.dot(merged_low, w_output[layer], preferred_element_type=jnp.float32)
        moe_in = root_norm(middle, gain_moe[layer])
        router = jax.nn.softmax(jnp.dot(moe_in, w_router[layer], precision=highest), axis=-1)
        route = routes[layer][..., 0]
        chosen = (route[..., None] == lax.iota(jnp.int32, experts)).astype(jnp.int32)
        rank = jnp.sum(chosen * (jnp.cumsum(chosen, axis=1) - 1), axis=-1)
        target = route * capacity + lax.iota(jnp.int32, batch)[:, None] * room + rank
        live = kept[layer].reshape(token_count)
        select = (
            (lax.iota(jnp.int32, experts * capacity)[:, None] == target) & (live[None, :] > 0)
        ).astype(jnp.bfloat16)
        chosen_float = chosen.reshape(token_count, experts).astype(jnp.float32)
        live_float = live.astype(jnp.float32)
        gate = jnp.sum(router * chosen_float, axis=-1) * live_float
        sent = jnp.dot(
            select, moe_in.astype(jnp.bfloat16), preferred_element_type=jnp.float32
        ).astype(jnp.bfloat16)
        answer, before, arrived = expert_apply(
            w_in[layer],
            w_out[layer],
            lax.all_to_all(
                sent.reshape(experts, capacity, width),
                "expert",
                split_axis=0,
                concat_axis=0,
                tiled=True,
            ),
        )
        returned = lax.all_to_all(answer, "expert", split_axis=0, concat_axis=0, tiled=True)
        picked = jnp.einsum(
            "ct,cd->td",
            select,
            returned.reshape(experts * capacity, width),
            preferred_element_type=jnp.float32,
        )
        saved.append(
            (
                residual,
                normed_low,
                query,
                pair,
                merged,
                log_total,
                merged_low,
                middle,
                moe_in,
                router,
                chosen_float,
                live_float,
                gate,
                select,
                picked,
                before,
                arrived,
            )
        )
        residual = middle + gate[:, None] * picked
    output = residual.astype(jnp.bfloat16).reshape(batch, count, width)
    grad = cotangent.astype(jnp.float32).reshape(token_count, width)
    table_grad = jnp.zeros_like(rel_bias)
    query_list, key_list, value_list, output_list = ([], [], [], [])
    gain_attn_list, gain_moe_list, router_list, in_list, out_list = ([], [], [], [], [])
    for layer in reversed(range(layers)):
        (
            residual_in,
            normed_low,
            query,
            pair,
            merged,
            log_total,
            merged_low,
            middle,
            moe_in,
            router,
            chosen_float,
            live_float,
            gate,
            select,
            picked,
            before,
            arrived,
        ) = saved[layer]
        gate_grad = jnp.sum(grad * picked, axis=-1)
        answer_grad = (gate[:, None] * grad).astype(jnp.bfloat16)
        back_sent = jnp.dot(select, answer_grad, preferred_element_type=jnp.float32).astype(
            jnp.bfloat16
        )
        arrived_grad = lax.all_to_all(
            back_sent.reshape(experts, capacity, width),
            "expert",
            split_axis=0,
            concat_axis=0,
            tiled=True,
        )
        shaped_grad = arrived_grad.reshape(group, local_experts, capacity, width)
        shaped_in = arrived.reshape(group, local_experts, capacity, width)
        shaped_before = before.reshape(group, local_experts, capacity, hidden_width)
        hidden, slope = jax.vjp(jax.nn.gelu, shaped_before)
        hidden_low = hidden.astype(jnp.bfloat16)
        out_list.insert(
            0,
            jnp.einsum(
                "genf,gend->efd", hidden_low, shaped_grad, preferred_element_type=jnp.float32
            ),
        )
        hidden_grad = jnp.einsum(
            "gend,efd->genf", shaped_grad, w_out[layer], preferred_element_type=jnp.float32
        )
        before_grad = slope(hidden_grad)[0].astype(jnp.bfloat16)
        in_list.insert(
            0,
            jnp.einsum(
                "gend,genf->edf", shaped_in, before_grad, preferred_element_type=jnp.float32
            ),
        )
        arrived_back = jnp.einsum(
            "genf,edf->gend", before_grad, w_in[layer], preferred_element_type=jnp.float32
        ).astype(jnp.bfloat16)
        home_grad = lax.all_to_all(
            arrived_back.reshape(experts, capacity, width),
            "expert",
            split_axis=0,
            concat_axis=0,
            tiled=True,
        )
        moe_grad = jnp.einsum(
            "ct,cd->td",
            select,
            home_grad.reshape(experts * capacity, width),
            preferred_element_type=jnp.float32,
        )
        chance_grad = chosen_float * (gate_grad * live_float)[:, None]
        logit_grad = router * (chance_grad - jnp.sum(router * chance_grad, axis=-1, keepdims=True))
        router_list.insert(0, jnp.einsum("td,te->de", moe_in, logit_grad, precision=highest))
        moe_grad = moe_grad + jnp.einsum(
            "te,de->td", logit_grad, w_router[layer], precision=highest
        )
        unused, norm_back = jax.vjp(root_norm, middle, gain_moe[layer])
        middle_grad, moe_gain_grad = norm_back(moe_grad)
        gain_moe_list.insert(0, moe_gain_grad)
        grad = grad + middle_grad
        grad_low = grad.astype(jnp.bfloat16)
        output_list.insert(
            0, jnp.einsum("td,te->de", merged_low, grad_low, preferred_element_type=jnp.float32)
        )
        merged_grad = jnp.einsum(
            "te,de->td", grad_low, w_output[layer], preferred_element_type=jnp.float32
        ).astype(jnp.bfloat16)
        merged_grad = merged_grad.reshape(batch, count, width)
        delta = jnp.einsum(
            "sihd,sihd->shi",
            merged_grad.astype(jnp.float32).reshape(batch, count, heads, -1),
            merged.reshape(batch, count, heads, -1),
            precision=highest,
        )
        query_grad, pair_grad, more_table = attend_back(
            query,
            merged_grad,
            delta,
            log_total,
            pair,
            rel_bias,
            first_for,
            source_for,
            context_size,
        )
        table_grad = table_grad + more_table
        query_low = query_grad.astype(jnp.bfloat16).reshape(token_count, width)
        key_low = pair_grad[0].astype(jnp.bfloat16).reshape(token_count, width)
        value_low = pair_grad[1].astype(jnp.bfloat16).reshape(token_count, width)
        query_list.insert(
            0, jnp.einsum("td,te->de", normed_low, query_low, preferred_element_type=jnp.float32)
        )
        key_list.insert(
            0, jnp.einsum("td,te->de", normed_low, key_low, preferred_element_type=jnp.float32)
        )
        value_list.insert(
            0, jnp.einsum("td,te->de", normed_low, value_low, preferred_element_type=jnp.float32)
        )
        normed_grad = (
            jnp.einsum("te,de->td", query_low, w_query[layer], preferred_element_type=jnp.float32)
            + jnp.einsum("te,de->td", key_low, w_key[layer], preferred_element_type=jnp.float32)
            + jnp.einsum("te,de->td", value_low, w_value[layer], preferred_element_type=jnp.float32)
        )
        unused, norm_back = jax.vjp(root_norm, residual_in, gain_attn[layer])
        residual_grad, attn_gain_grad = norm_back(normed_grad)
        gain_attn_list.insert(0, attn_gain_grad)
        grad = grad + residual_grad
    query_out, key_out, value_out, output_out, gain_attn_out, gain_moe_out, router_out = (
        lax.psum_scatter(
            jnp.stack(query_list), ("dp", "context", "expert"), scatter_dimension=1, tiled=True
        ),
        lax.psum_scatter(
            jnp.stack(key_list), ("dp", "context", "expert"), scatter_dimension=1, tiled=True
        ),
        lax.psum_scatter(
            jnp.stack(value_list), ("dp", "context", "expert"), scatter_dimension=1, tiled=True
        ),
        lax.psum_scatter(
            jnp.stack(output_list), ("dp", "context", "expert"), scatter_dimension=1, tiled=True
        ),
        lax.psum_scatter(
            jnp.stack(gain_attn_list), ("dp", "context", "expert"), scatter_dimension=1, tiled=True
        ),
        lax.psum_scatter(
            jnp.stack(gain_moe_list), ("dp", "context", "expert"), scatter_dimension=1, tiled=True
        ),
        lax.psum_scatter(
            jnp.stack(router_list), ("dp", "context", "expert"), scatter_dimension=1, tiled=True
        ),
    )
    in_out, out_out = (
        lax.psum_scatter(
            jnp.stack(in_list).astype(jnp.bfloat16),
            ("dp", "context"),
            scatter_dimension=2,
            tiled=True,
        ).astype(jnp.float32),
        lax.psum_scatter(
            jnp.stack(out_list).astype(jnp.bfloat16),
            ("dp", "context"),
            scatter_dimension=2,
            tiled=True,
        ).astype(jnp.float32),
    )
    bias_out = lax.psum(table_grad, ("dp", "context", "expert"))
    output = forward_path(
        tokens, w_query, w_key, w_value, w_output, rel_bias, gain_attn, gain_moe, w_router, w_in, w_out, routes, kept
    )
    return (
        output,
        grad.reshape(batch, count, width),
        query_out,
        key_out,
        value_out,
        output_out,
        bias_out,
        gain_attn_out,
        gain_moe_out,
        router_out,
        in_out,
        out_out,
    )


def solution(mesh):
    in_specs = (
        P("dp", ("context", "expert"), None),
        P(),
        P(),
        P(),
        P(),
        P(),
        P(),
        P(),
        P(),
        P(None, "expert", None, None),
        P(None, "expert", None, None),
        P(None, "dp", ("context", "expert"), None),
        P(None, "dp", ("context", "expert")),
        P("dp", ("context", "expert"), None),
    )
    out_specs = (
        P("dp", ("context", "expert"), None),
        P("dp", ("context", "expert"), None),
        P(None, ("dp", "context", "expert"), None),
        P(None, ("dp", "context", "expert"), None),
        P(None, ("dp", "context", "expert"), None),
        P(None, ("dp", "context", "expert"), None),
        P(),
        P(None, ("dp", "context", "expert")),
        P(None, ("dp", "context", "expert")),
        P(None, ("dp", "context", "expert"), None),
        P(None, "expert", ("dp", "context"), None),
        P(None, "expert", ("dp", "context"), None),
    )
    return jax.shard_map(
        on_device, mesh=mesh, in_specs=in_specs, out_specs=out_specs, check_vma=False
    )
```

```python
import functools

import jax
import jax.numpy as jnp
import numpy as np
from jax import lax
from jax.experimental import pallas as pl
from jax.experimental.pallas import tpu as pltpu
from jax.sharding import PartitionSpec as P

highest = lax.Precision.HIGHEST
epsilon = 1e-06
thresholds = (12, 16, 23, 32, 46, 64, 91)
MESH = pl.DeviceIdType.MESH
GROUP = 4
HEAD = 64
BLOCK = 128
FCHUNK = 512
f32, bf16 = jnp.float32, jnp.bfloat16


def div(a, b):
    return lax.div(a, jnp.int32(b))


def rem(a, b):
    return lax.rem(a, jnp.int32(b))


class Place:
    def __init__(self, parts, experts):
        self.parts, self.experts = parts, experts
        self.dp = lax.axis_index("dp")
        self.context = lax.axis_index("context")
        self.expert = lax.axis_index("expert")
        self.core = rem(self.dp, 2)
        self.far = div(self.context, 2)
        self.block = 2 * rem(self.context, 2) + div(self.dp, 2)
        self.part = 2 * self.far + self.core

    def flipped(self, flip):
        low = rem(rem(self.block, 2) + flip % 2, 2)
        high = rem(div(self.block, 2) + flip // 2, 2)
        return 2 * high + low

    def group_device(self, block):
        return {"dp": 2 * rem(block, 2) + self.core, "context": 2 * self.far + div(block, 2)}

    def part_other(self, step):
        return rem(self.part + step, self.parts)

    def part_device(self, part):
        return {
            "dp": self.dp - self.core + rem(part, 2),
            "context": 2 * div(part, 2) + rem(self.context, 2),
        }

    def expert_other(self, step):
        return rem(self.expert + step, self.experts)

    def offset(self, part, block, query_block):
        return 8 * (part // 2 - self.far) + 2 * (block - query_block) + (part % 2 - self.core)

    def bias_index(self, part, block, query_block):
        offset = self.offset(part, block, query_block)
        return jnp.minimum(jnp.maximum(offset, -2), 2) + 2

    def core_device(self):
        return {"dp": self.dp + 1 - 2 * self.core}

    def plane_others(self):
        made = []
        for step in range(self.parts // 2):
            far = rem(self.far + step, self.parts // 2)
            for flip in range(GROUP):
                if step or flip:
                    other = self.flipped(flip)
                    device = {"dp": 2 * rem(other, 2) + self.core, "context": 2 * far + div(other, 2)}
                    made.append((step, flip, far, other, device))
        return made

    def greet(self, plane=False):
        if plane:
            partners = [item[-1] for item in self.plane_others()]
            partners += [{**device, "dp": device.get("dp") + 1 - 2 * self.core} for device in partners]
            partners += [self.core_device()]
        else:
            partners = [self.group_device(self.flipped(flip)) for flip in (1, 2, 3)]
            partners += [self.part_device(self.part_other(step)) for step in range(1, self.parts)]
        partners += [{"expert": self.expert_other(step)} for step in range(1, self.experts)]
        barrier = pltpu.get_barrier_semaphore()
        for partner in partners:
            pl.semaphore_signal(barrier, inc=1, device_id=partner, device_id_type=MESH)
        pl.semaphore_wait(barrier, len(partners))


def remote(source, target, send, receive, device):
    return pltpu.make_async_remote_copy(
        src_ref=source,
        dst_ref=target,
        send_sem=send,
        recv_sem=receive,
        device_id=device,
        device_id_type=MESH,
    )


def dot(a, b):
    return jnp.dot(a, b, preferred_element_type=f32)


def dot_nt(a, b):
    return lax.dot_general(a, b, (((1,), (1,)), ((), ())), preferred_element_type=f32)


def dot_tn(a, b):
    return lax.dot_general(a, b, (((0,), (0,)), ((), ())), preferred_element_type=f32)


def root_scale(value):
    return lax.rsqrt(jnp.mean(value * value, axis=-1, keepdims=True) + epsilon)


def lanes(rows, width):
    return lax.broadcasted_iota(jnp.int32, (rows, width), 1)


def gelu_parts(value):
    scale = 0.7978845608028654
    square = value * value
    inner = jnp.tanh(scale * (value + 0.044715 * (square * value)))
    half = 0.5 * (1.0 + inner)
    slope = half + 0.5 * value * (1.0 - inner * inner) * (scale * (1.0 + 3 * 0.044715 * square))
    return value * half, slope


def gelu(value):
    scale = 0.7978845608028654
    return value * (0.5 * (1.0 + jnp.tanh(scale * (value + 0.044715 * (value * value * value)))))


def forward_kernel(
    layer,
    parts,
    experts,
    x,
    gains,
    w_router,
    select,
    chosen,
    bias,
    w_qkv_hbm,
    w_output_hbm,
    w_in_hbm,
    w_out_hbm,
    turned,
    query,
    pair,
    merged,
    log_total,
    merged_low,
    middle,
    router,
    picked,
    arrived,
    before,
    x_next,
    normed,
    w_qkv,
    w_output,
    w_in,
    w_out,
    scores,
    merged_mine,
    slots,
    total,
    answer,
    returned,
    load_sem,
    group_send,
    group_recv,
    part_send,
    part_recv,
    merge_send,
    merge_recv,
    slot_send,
    slot_recv,
    back_send,
    back_recv,
):
    here = Place(parts, experts)
    heads = 3
    wide = heads * HEAD
    loads = [
        pltpu.make_async_copy(w_qkv_hbm.at[layer], w_qkv, load_sem.at[0]),
        pltpu.make_async_copy(w_output_hbm.at[layer], w_output, load_sem.at[1]),
        pltpu.make_async_copy(w_in_hbm.at[layer, 0], w_in, load_sem.at[2]),
        pltpu.make_async_copy(w_out_hbm.at[layer, 0], w_out, load_sem.at[3]),
    ]
    for load in loads:
        load.start()
    value = x[...]
    block = here.block
    normed[block] = (value * root_scale(value) * gains[0:1, :]).astype(bf16)
    here.greet()

    def gather(flip, source):
        return remote(
            normed.at[source],
            normed.at[source],
            group_send.at[flip - 1],
            group_recv.at[flip - 1],
            here.group_device(here.flipped(flip)),
        )

    for flip in (1, 2, 3):
        gather(flip, block).start()

    def hand_pair(step, part, of_block):
        return remote(
            pair.at[part, of_block],
            pair.at[part, of_block],
            part_send.at[step - 1, of_block],
            part_recv.at[step - 1, of_block],
            here.part_device(here.part_other(step)),
        )

    def project(of_block):
        made = dot(normed[of_block], w_qkv[...]).astype(bf16)
        pair[here.part, of_block] = made[:, : 2 * wide]
        query[of_block] = made[:, 2 * wide :]
        for step in range(1, parts):
            hand_pair(step, here.part, of_block).start()
        columns = pl.ds(pl.multiple_of(of_block * BLOCK, BLOCK), BLOCK)
        turned[:, columns] = normed[of_block].astype(f32).T.astype(bf16)

    loads[0].wait()
    project(block)
    for flip in (1, 2, 3):
        source = here.flipped(flip)
        gather(flip, source).wait_recv()
        project(source)
    for step in range(1, parts):
        source = rem(here.part + parts - step, parts)
        for of_block in range(GROUP):
            hand_pair(step, source, of_block).wait_recv()

    lane = lanes(BLOCK, 2 * BLOCK)
    lane_out = lanes(BLOCK, 2 * BLOCK)
    lane_log = lanes(BLOCK, BLOCK)

    def hand_merged(flip, source):
        return remote(
            merged_mine.at[here.flipped(flip)],
            merged_low.at[source],
            merge_send.at[flip - 1],
            merge_recv.at[flip - 1],
            here.group_device(here.flipped(flip)),
        )

    for flip in (3, 1, 2, 0):
        mine = here.flipped(flip)
        rows = query[mine]
        gathered = jnp.zeros((BLOCK, 2 * BLOCK), f32)
        logs = jnp.zeros((BLOCK, BLOCK), f32)
        for head in range(heads):
            masked = jnp.where(lane // HEAD == head, rows, jnp.zeros_like(rows))
            top = jnp.full((BLOCK, 1), -1e30, f32)
            for part in range(parts):
                keys = pair[part].reshape(GROUP * BLOCK, 2 * wide)[:, : 2 * BLOCK]
                raw = dot_nt(masked, keys)
                for of_block in range(GROUP):
                    piece = (
                        raw[:, of_block * BLOCK : (of_block + 1) * BLOCK]
                        + bias[head, here.bias_index(part, of_block, mine)]
                    )
                    scores[part * GROUP + of_block] = piece
                    top = jnp.maximum(top, jnp.max(piece, axis=-1, keepdims=True))
            summed = jnp.zeros((BLOCK, 1), f32)
            out = jnp.zeros((BLOCK, 2 * BLOCK), f32)
            for part in range(parts):
                pieces = []
                for of_block in range(GROUP):
                    weight = jnp.exp(scores[part * GROUP + of_block] - top)
                    summed = summed + jnp.sum(weight, axis=-1, keepdims=True)
                    pieces.append(weight.astype(bf16))
                values = pair[part].reshape(GROUP * BLOCK, 2 * wide)[:, BLOCK:]
                out = out + dot(jnp.concatenate(pieces, axis=1), values)
            gathered = jnp.where((lane_out + HEAD) // HEAD == head + 2, out / summed, gathered)
            logs = jnp.where(lane_log == head, top + jnp.log(summed), logs)
        final = gathered[:, HEAD:]
        merged[mine] = gathered
        log_total[mine] = logs
        if flip:
            merged_mine[mine] = final.astype(bf16)
            hand_merged(flip, block).start()
        else:
            merged_low[block] = final.astype(bf16)

    for flip in (1, 2, 3):
        hand_merged(flip, here.flipped(flip)).wait_recv()
    loads[1].wait()
    mid = value
    for of_block in range(GROUP):
        mid = mid + dot(merged_low[of_block], w_output[of_block * wide : (of_block + 1) * wide, :])
    middle[...] = mid
    moe_in = mid * root_scale(mid) * gains[1:2, :]
    moe_low = moe_in.astype(bf16)

    def hand_slots(step, source):
        return remote(
            slots.at[here.expert_other(step)],
            arrived.at[source],
            slot_send.at[step - 1],
            slot_recv.at[step - 1],
            {"expert": here.expert_other(step)},
        )

    for expert in range(experts):
        slots[expert] = dot(select[expert], moe_low).astype(bf16)
    for step in range(1, experts):
        hand_slots(step, here.expert).start()
    arrived[here.expert] = slots[here.expert]
    logits = jnp.dot(moe_in, w_router[...], precision=highest, preferred_element_type=f32)
    logits = jnp.where(lane_log < experts, logits, -1e30)
    raised = jnp.exp(logits - jnp.max(logits, axis=-1, keepdims=True))
    chances = raised / jnp.sum(raised, axis=-1, keepdims=True)
    router[...] = chances
    gate = jnp.sum(chances * chosen[...], axis=-1, keepdims=True)
    loads[2].wait()
    loads[3].wait()
    for step in range(1, experts):
        hand_slots(step, rem(here.expert + experts - step, experts)).wait_recv()
    given = jnp.concatenate([arrived[expert].astype(f32) for expert in range(experts)], axis=0)
    given = given.astype(bf16)
    room = arrived.shape[1]
    total[...] = jnp.zeros_like(total)

    @pl.loop(0, w_in.shape[1] // FCHUNK)
    def _(index):
        columns = pl.ds(pl.multiple_of(index * FCHUNK, FCHUNK), FCHUNK)
        first = dot(given, w_in[:, columns])
        before[:, columns] = first
        total[...] += dot(gelu(first).astype(bf16), w_out[columns, :])

    def hand_answer(step, source):
        return remote(
            answer.at[here.expert_other(step)],
            returned.at[source],
            back_send.at[step - 1],
            back_recv.at[step - 1],
            {"expert": here.expert_other(step)},
        )

    for expert in range(experts):
        answer[expert] = total[expert * room : (expert + 1) * room, :].astype(bf16)
    for step in range(1, experts):
        hand_answer(step, here.expert).start()
    returned[here.expert] = answer[here.expert]
    for step in range(1, experts):
        hand_answer(step, rem(here.expert + experts - step, experts)).wait_recv()
    back = jnp.zeros_like(value)
    for expert in range(experts):
        back = back + dot_tn(select[expert], returned[expert])
    picked[...] = back.astype(bf16)
    x_next[...] = mid + gate * back
    for flip in (1, 2, 3):
        gather(flip, block).wait_send()
        hand_merged(flip, block).wait_send()
    for step in range(1, parts):
        for of_block in range(GROUP):
            hand_pair(step, here.part, of_block).wait_send()
    for step in range(1, experts):
        hand_slots(step, here.expert).wait_send()
        hand_answer(step, here.expert).wait_send()


def backward_kernel(
    layer,
    parts,
    experts,
    grad,
    x,
    gains,
    w_router,
    select,
    chosen,
    bias,
    turned,
    query,
    pair,
    merged,
    log_total,
    middle,
    router,
    picked,
    arrived,
    before,
    w_qkv_hbm,
    w_output_hbm,
    w_in_hbm,
    w_out_hbm,
    grad_next,
    final_in,
    final_out,
    grad_qkv,
    grad_output,
    grad_bias,
    grad_rows,
    grad_in,
    grad_out,
    core_in,
    core_out,
    second_in,
    second_out,
    third_in,
    third_out,
    far_in,
    far_out,
    output_sum,
    w_qkv,
    w_output,
    slots,
    arrived_grad,
    answer,
    returned,
    branches,
    merged_grad,
    query_grad,
    pair_sent,
    pair_recv,
    made_grad,
    normed_sent,
    normed_recv,
    load_sem,
    slot_send,
    slot_recv,
    back_send,
    back_recv,
    group_send,
    group_recv,
    part_send,
    part_recv,
    merge_send,
    merge_recv,
    core_send,
    core_recv,
    second_send,
    second_recv,
    third_send,
    third_recv,
    far_send,
    far_recv,
):
    here = Place(parts, experts)
    heads = 3
    wide = heads * HEAD
    block = here.block
    fars = parts // 2
    side, level = div(here.dp, 2), rem(here.context, 2)
    across, beside = here.group_device(here.flipped(1)), here.group_device(here.flipped(2))
    own_in, own_out = grad_in.at[2 * side + here.core], grad_out.at[2 * side + here.core]

    def to_core(turns=(0, 1)):
        made = []
        for at in turns:
            there = 2 * at + 1 - here.core
            for kind, (source, target) in enumerate(((grad_in, core_in), (grad_out, core_out))):
                sems = core_send.at[kind, at], core_recv.at[kind, at]
                made.append(remote(source.at[there], target.at[at], *sems, here.core_device()))
        return made

    def second():
        made = []
        for far in range(fars):
            for turn in range(2):
                at = 2 * far + rem(level + 1 + turn, 2)
                sems = second_send.at[0, far, turn], second_recv.at[0, far, turn]
                source = grad_in.at[2 * (1 - side) + here.core, at]
                made.append(remote(source, second_in.at[far, 1 - turn], *sems, across))
                sems = second_send.at[1, far, turn], second_recv.at[1, far, turn]
                there = 2 * rem(side + 1 + turn, 2) + here.core
                source = grad_out.at[there, 2 * far + 1 - level]
                made.append(remote(source, second_out.at[far, 1 - turn], *sems, beside))
        return made

    def third():
        made = []
        for far in range(fars):
            sems = third_send.at[0, far], third_recv.at[0, far]
            made.append(remote(own_in.at[2 * far + 1 - level], third_in.at[far], *sems, beside))
            sems = third_send.at[1, far], third_recv.at[1, far]
            source = grad_out.at[2 * (1 - side) + here.core, 2 * far + level]
            made.append(remote(source, third_out.at[far], *sems, across))
        return made

    def fourth():
        made = []
        for step in range(1, fars):
            far = rem(here.far + step, fars)
            device = {"context": 2 * far + level}
            sems = far_send.at[0, step - 1], far_recv.at[0, step - 1]
            made.append(remote(own_in.at[2 * far + level], far_in.at[step - 1], *sems, device))
            sems = far_send.at[1, step - 1], far_recv.at[1, step - 1]
            made.append(remote(own_out.at[2 * far + level], far_out.at[step - 1], *sems, device))
        return made

    def add(target, source):
        target[...] = (target[...].astype(f32) + source[...].astype(f32)).astype(bf16)
    later = [
        pltpu.make_async_copy(
            w_output_hbm.at[layer, pl.ds(pl.multiple_of(block * wide, wide), wide)],
            w_output.at[pl.ds(HEAD, wide)],
            load_sem.at[2],
        ),
        pltpu.make_async_copy(w_qkv_hbm.at[layer], w_qkv, load_sem.at[3]),
    ]

    def hand_slots(step, source):
        return remote(
            slots.at[here.expert_other(step)],
            arrived_grad.at[source],
            slot_send.at[step - 1],
            slot_recv.at[step - 1],
            {"expert": here.expert_other(step)},
        )

    def hand_answer(step, source):
        return remote(
            answer.at[here.expert_other(step)],
            returned.at[source],
            back_send.at[step - 1],
            back_recv.at[step - 1],
            {"expert": here.expert_other(step)},
        )

    def experts_phase(w_in, w_out, hidden, slope, before_grad, total, turned_given):
        loads = [
            pltpu.make_async_copy(w_out_hbm.at[layer, 0], w_out, load_sem.at[0]),
            pltpu.make_async_copy(w_in_hbm.at[layer, 0], w_in, load_sem.at[1]),
        ]
        for load in loads + later:
            load.start()
        w_output[:HEAD, :] = jnp.zeros((HEAD, w_output.shape[1]), bf16)
        came = grad[...]
        chances = router[...]
        gate = jnp.sum(chances * chosen[...], axis=-1, keepdims=True)
        gate_grad = jnp.sum(came * picked[...].astype(f32), axis=-1, keepdims=True)
        answer_grad = (gate * came).astype(bf16)
        for expert in range(experts):
            slots[expert] = dot(select[expert], answer_grad).astype(bf16)
        here.greet()


        for step in range(1, experts):
            hand_slots(step, here.expert).start()
        arrived_grad[here.expert] = slots[here.expert]
        room = arrived.shape[1]
        hidden_width = w_in.shape[1]

        @pl.loop(0, hidden_width // FCHUNK)
        def _(index):
            columns = pl.ds(pl.multiple_of(index * FCHUNK, FCHUNK), FCHUNK)
            made, steep = gelu_parts(before[:, columns])
            hidden[:, columns] = made.astype(bf16)
            slope[:, columns] = steep

        mid = middle[...]
        scale = root_scale(mid)
        unit = mid * scale
        moe_in = unit * gains[1:2, :]
        chance_grad = chosen[...] * gate_grad
        logit_grad = chances * (chance_grad - jnp.sum(chances * chance_grad, axis=-1, keepdims=True))
        router_grad = lax.dot_general(
            logit_grad, moe_in, (((0,), (0,)), ((), ())), precision=highest, preferred_element_type=f32
        )
        grad_rows[...] = router_grad[:8, :]
        moe_part = lax.dot_general(
            logit_grad, w_router[...], (((1,), (1,)), ((), ())), precision=highest, preferred_element_type=f32
        )
        given = jnp.concatenate([arrived[expert].astype(f32) for expert in range(experts)], axis=0)
        turned_given[...] = given.T.astype(bf16)
        total[...] = jnp.zeros_like(total)
        loads[0].wait()
        loads[1].wait()
        for step in range(1, experts):
            hand_slots(step, rem(here.expert + experts - step, experts)).wait_recv()
        given_grad = jnp.concatenate(
            [arrived_grad[expert].astype(f32) for expert in range(experts)], axis=0
        ).astype(bf16)

        @pl.loop(0, hidden_width // FCHUNK)
        def _(index):
            columns = pl.ds(pl.multiple_of(index * FCHUNK, FCHUNK), FCHUNK)
            hidden_grad = dot_nt(given_grad, w_out[columns, :])
            low = (hidden_grad * slope[:, columns]).astype(bf16)
            before_grad[:, columns] = low
            total[...] += dot_nt(low, w_in[:, columns])


        for expert in range(experts):
            answer[expert] = total[expert * room : (expert + 1) * room, :].astype(bf16)
        for step in range(1, experts):
            hand_answer(step, here.expert).start()
        returned[here.expert] = answer[here.expert]

        rows_in, rows_out = grad_in.shape[2], grad_out.shape[2]
        columns_in = grad_in.shape[3] // GROUP
        for turn in range(4):
            there = 2 * (turn % 2) + (1 - here.core if turn < 2 else here.core)
            rows = pl.ds(pl.multiple_of(there * (parts * rows_in), parts * rows_in), parts * rows_in)
            for piece in range(GROUP):
                columns = slice(piece * columns_in, (piece + 1) * columns_in)
                made = dot(turned_given[rows, :], before_grad[:, columns])
                for at in range(parts):
                    grad_in[there, at, :, columns] = made[at * rows_in : (at + 1) * rows_in, :].astype(bf16)
            columns = pl.ds(pl.multiple_of(there * (parts * rows_out), parts * rows_out), parts * rows_out)
            made = dot_tn(hidden[:, columns], given_grad)
            for at in range(parts):
                grad_out[there, at] = made[at * rows_out : (at + 1) * rows_out, :].astype(bf16)
            if turn < 2:
                for copy in to_core((turn,)):
                    copy.start()

        for step in range(1, experts):
            hand_answer(step, rem(here.expert + experts - step, experts)).wait_recv()
        moe_grad = moe_part
        for expert in range(experts):
            moe_grad = moe_grad + dot_tn(select[expert], returned[expert])
        grad_rows[4:5, :] = jnp.sum(moe_grad * unit, axis=0, keepdims=True)
        scaled = moe_grad * gains[1:2, :]
        mid_grad = came + scale * (scaled - unit * jnp.mean(unit * scaled, axis=-1, keepdims=True))
        branches[block] = mid_grad.astype(bf16)
        return mid_grad

    slot_rows = experts * arrived.shape[1]
    mid_grad = pl.run_scoped(
        experts_phase,
        pltpu.VMEM(w_in_hbm.shape[2:], bf16),
        pltpu.VMEM(w_out_hbm.shape[2:], bf16),
        pltpu.VMEM(before.shape, bf16),
        pltpu.VMEM(before.shape, f32),
        pltpu.VMEM(before.shape, bf16),
        pltpu.VMEM((slot_rows, grad.shape[1]), f32),
        pltpu.VMEM((grad.shape[1], slot_rows), bf16),
    )

    def gather(flip, source):
        return remote(
            branches.at[source],
            branches.at[source],
            group_send.at[flip - 1],
            group_recv.at[flip - 1],
            here.group_device(here.flipped(flip)),
        )

    for flip in (1, 2, 3):
        gather(flip, block).start()
    for turn in range(2):
        for copy in to_core((turn,)):
            copy.wait_recv()
        for at in range(parts):
            add(grad_in.at[2 * turn + here.core, at], core_in.at[turn, at])
            add(grad_out.at[2 * turn + here.core, at], core_out.at[turn, at])
    later[0].wait()
    later[1].wait()
    def hand_pair(step, source):
        return remote(
            pair_sent.at[step - 1],
            pair_recv.at[step - 1],
            part_send.at[step - 1],
            part_recv.at[step - 1],
            here.part_device(here.part_other(step)),
        )

    def attention_phase(score_grads, weights, pair_grad):
        lane = lanes(BLOCK, 2 * BLOCK)
        grad_bias[...] = jnp.zeros_like(grad_bias)
        output_sum[...] = jnp.zeros_like(output_sum)
        for head in range(heads):
            for flip in range(GROUP):
                mine = here.flipped(flip)
                if head == 0:
                    if flip:
                        gather(flip, mine).wait_recv()
                    merged_grad[mine] = dot_nt(branches[mine], w_output[...]).astype(bf16)
                    output_sum[...] += dot_tn(merged[mine].astype(bf16), branches[mine])[HEAD:, :]
                    query_grad[mine] = jnp.zeros((BLOCK, 2 * BLOCK), f32)
                    if flip == GROUP - 1:
                        for copy in second():
                            copy.start()
                rows = query[mine]
                masked = jnp.where(lane // HEAD == head, rows, jnp.zeros_like(rows))
                rows_grad = merged_grad[mine]
                masked_grad = jnp.where(lane // HEAD == head + 1, rows_grad, jnp.zeros_like(rows_grad))
                delta = jnp.sum(masked_grad.astype(f32) * merged[mine], axis=-1, keepdims=True)
                log_sum = log_total[mine][:, head : head + 1]
                gathered = jnp.zeros((BLOCK, 2 * BLOCK), f32)
                for part in range(parts):
                    both = pair[part].reshape(GROUP * BLOCK, 2 * wide)
                    raw = dot_nt(masked, both[:, : 2 * BLOCK])
                    raw_grad = dot_nt(masked_grad, both[:, BLOCK:])
                    pieces = []
                    for of_block in range(GROUP):
                        columns = slice(of_block * BLOCK, (of_block + 1) * BLOCK)
                        place = here.bias_index(part, of_block, mine)
                        weight = jnp.exp(raw[:, columns] + bias[head, place] - log_sum)
                        score_grad = weight * (raw_grad[:, columns] - delta)
                        grad_bias[head, place] += score_grad
                        low = score_grad.astype(bf16)
                        pieces.append(low)
                        weights[part, mine, :, columns] = weight.astype(bf16)
                        score_grads[part, mine, :, columns] = low
                    gathered = gathered + dot(jnp.concatenate(pieces, axis=1), both[:, : 2 * BLOCK])
                query_grad[mine] += jnp.where(lane // HEAD == head, gathered, 0.0)
            query_turned = [query[of_block].astype(f32).T.astype(bf16) for of_block in range(GROUP)]
            grad_turned = [merged_grad[of_block].astype(f32).T.astype(bf16) for of_block in range(GROUP)]
            own = slice(head * HEAD, (head + 1) * HEAD)
            own_grad = slice((head + 1) * HEAD, (head + 2) * HEAD)
            query_turned = jnp.concatenate([item[own] for item in query_turned], axis=1)
            grad_turned = jnp.concatenate([item[own_grad] for item in grad_turned], axis=1)
            for part in range(parts):
                pair_grad[part, own, :] = dot(
                    query_turned, score_grads[part].reshape(GROUP * BLOCK, GROUP * BLOCK)
                )
                pair_grad[part, wide + head * HEAD : wide + (head + 1) * HEAD, :] = dot(
                    grad_turned, weights[part].reshape(GROUP * BLOCK, GROUP * BLOCK)
                )


        for step in range(1, parts):
            pair_sent[step - 1] = pair_grad[here.part_other(step)].astype(bf16)
            hand_pair(step, 0).start()
        summed = pair_grad[here.part]
        for step in range(1, parts):
            hand_pair(step, 0).wait_recv()
            summed = summed + pair_recv[step - 1].astype(f32)
        summed = summed.T.astype(bf16)
        for of_block in range(GROUP):
            made_grad[of_block, :, : 2 * wide] = summed[of_block * BLOCK : (of_block + 1) * BLOCK, :]
            made_grad[of_block, :, 2 * wide :] = query_grad[of_block].astype(bf16)

    spread = (parts, GROUP, BLOCK, GROUP * BLOCK)
    pl.run_scoped(
        attention_phase,
        pltpu.VMEM(spread, bf16),
        pltpu.VMEM(spread, bf16),
        pltpu.VMEM((parts, 2 * wide, GROUP * BLOCK), f32),
    )

    def hand_normed(flip):
        return remote(
            normed_sent.at[flip - 1],
            normed_recv.at[flip - 1],
            merge_send.at[flip - 1],
            merge_recv.at[flip - 1],
            here.group_device(here.flipped(flip)),
        )

    for flip in (3, 1, 2):
        normed_sent[flip - 1] = dot_nt(made_grad[here.flipped(flip)], w_qkv[...]).astype(bf16)
        hand_normed(flip).start()
    normed_grad = dot_nt(made_grad[block], w_qkv[...])
    both = made_grad[...].reshape(GROUP * BLOCK, made_grad.shape[2])
    rows = turned.shape[0] // GROUP
    tall = grad_qkv.shape[3]
    for there in range(GROUP):
        made = dot(turned[there * rows : (there + 1) * rows, :], both)
        for at in range(parts):
            for expert in range(experts):
                first = (at * experts + expert) * tall
                grad_qkv[there, at, expert] = made[first : first + tall, :].astype(bf16)
    half = grad_output.shape[4]
    for at in range(parts):
        for expert in range(experts):
            first = (at * experts + expert) * tall
            for turn in range(2):
                piece = output_sum[first : first + tall, turn * half : (turn + 1) * half]
                grad_output[turn, at, expert] = piece.astype(bf16)
    value = x[...]
    scale = root_scale(value)
    unit = value * scale
    for flip in (1, 2, 3):
        hand_normed(flip).wait_recv()
        normed_grad = normed_grad + normed_recv[flip - 1].astype(f32)
    grad_rows[5:6, :] = jnp.sum(normed_grad * unit, axis=0, keepdims=True)
    scaled = normed_grad * gains[0:1, :]
    grad_next[...] = mid_grad + scale * (scaled - unit * jnp.mean(unit * scaled, axis=-1, keepdims=True))
    for copy in second():
        copy.wait_recv()
    for far in range(fars):
        add(own_in.at[2 * far + 1 - level], second_in.at[far, 1])
        add(grad_out.at[2 * (1 - side) + here.core, 2 * far + level], second_out.at[far, 1])
    for copy in third():
        copy.start()
    for far in range(fars):
        add(own_in.at[2 * far + level], second_in.at[far, 0])
        add(own_out.at[2 * far + level], second_out.at[far, 0])
    for copy in third():
        copy.wait_recv()
    for far in range(fars):
        add(own_in.at[2 * far + level], third_in.at[far])
        add(own_out.at[2 * far + level], third_out.at[far])
    for copy in fourth():
        copy.start()
    for copy in fourth():
        copy.wait_recv()
    sum_in, sum_out = own_in[here.context].astype(f32), own_out[here.context].astype(f32)
    for step in range(1, fars):
        sum_in = sum_in + far_in[step - 1].astype(f32)
        sum_out = sum_out + far_out[step - 1].astype(f32)
    final_in[...] = sum_in
    final_out[...] = sum_out
    for copy in to_core() + second() + third() + fourth():
        copy.wait_send()
    for flip in (1, 2, 3):
        gather(flip, block).wait_send()
        hand_normed(flip).wait_send()
    for step in range(1, parts):
        hand_pair(step, 0).wait_send()
    for step in range(1, experts):
        hand_slots(step, here.expert).wait_send()
        hand_answer(step, here.expert).wait_send()


VMEM = pl.BlockSpec(memory_space=pltpu.VMEM)
ANY = pl.BlockSpec(memory_space=pl.ANY)
DMA = pltpu.SemaphoreType.DMA


def forward_layer(layer, x, gains, w_router, select, chosen, bias, w_qkv, w_output, w_in, w_out):
    count, width = x.shape
    parts, experts = lax.axis_size("context"), lax.axis_size("expert")
    wide = 3 * HEAD
    room = select.shape[1]
    hidden = w_in.shape[3]
    shape = jax.ShapeDtypeStruct
    return pl.pallas_call(
        functools.partial(forward_kernel, layer, parts, experts),
        out_shape=[
            shape((width, GROUP * count), bf16),
            shape((GROUP, count, 2 * BLOCK), bf16),
            shape((parts, GROUP, count, 2 * wide), bf16),
            shape((GROUP, count, 2 * BLOCK), f32),
            shape((GROUP, count, 128), f32),
            shape((GROUP, count, wide), bf16),
            shape((count, width), f32),
            shape((count, 128), f32),
            shape((count, width), bf16),
            shape((experts, room, width), bf16),
            shape((experts * room, hidden), f32),
            shape((count, width), f32),
        ],
        in_specs=[VMEM] * 6 + [ANY] * 4,
        out_specs=[VMEM] * 12,
        scratch_shapes=[
            pltpu.VMEM((GROUP, count, width), bf16),
            pltpu.VMEM((width, w_qkv.shape[2]), bf16),
            pltpu.VMEM((width, width), bf16),
            pltpu.VMEM((width, hidden), bf16),
            pltpu.VMEM((hidden, width), bf16),
            pltpu.VMEM((parts * GROUP, count, BLOCK), f32),
            pltpu.VMEM((GROUP, count, wide), bf16),
            pltpu.VMEM((experts, room, width), bf16),
            pltpu.VMEM((experts * room, width), f32),
            pltpu.VMEM((experts, room, width), bf16),
            pltpu.VMEM((experts, room, width), bf16),
            DMA((4,)),
            DMA((3,)),
            DMA((3,)),
            DMA((parts - 1, GROUP)),
            DMA((parts - 1, GROUP)),
            DMA((3,)),
            DMA((3,)),
            DMA((experts - 1,)),
            DMA((experts - 1,)),
            DMA((experts - 1,)),
            DMA((experts - 1,)),
        ],
        compiler_params=pltpu.CompilerParams(
            collective_id=layer, has_side_effects=True, vmem_limit_bytes=56 * 2**20
        ),
        name="layer_forward",
    )(x, gains, w_router, select, chosen, bias, w_qkv, w_output, w_in, w_out)


def bucket_blocks():
    row = np.arange(BLOCK)[:, None]
    column = np.arange(BLOCK)[None, :]
    made = []
    for offset in (-2, -1, 0, 1, 2):
        r = offset * BLOCK + column - row
        n = np.abs(r)
        beyond = 8 + sum((n >= limit).astype(np.int32) for limit in thresholds)
        made.append(np.where(n < 8, n, beyond) + np.where(r > 0, 16, 0))
    return np.stack(made).astype(np.int32)


def bias_blocks(rel_bias, first_head):
    mine = lax.dynamic_slice_in_dim(rel_bias, first_head, 3, 1)
    buckets = jnp.asarray(bucket_blocks())
    made = jnp.zeros((3,) + buckets.shape, f32)
    for bucket in range(rel_bias.shape[0]):
        made = jnp.where(buckets[None] == bucket, mine[bucket][:, None, None, None], made)
    return made


def swap_route():
    d, c, e = (lax.axis_size(name) for name in ("dp", "context", "expert"))
    return [((i * c + j) * e + k, (k * c + j) * e + i) for i in range(d) for j in range(c) for k in range(e)]


def swapped(block):
    return lax.ppermute(block, ("dp", "context", "expert"), swap_route())


def routing(routes, kept, experts, room):
    layers, count = routes.shape
    chosen = (routes[..., None] == lax.iota(jnp.int32, experts)).astype(jnp.int32)
    rank = jnp.sum(chosen * (jnp.cumsum(chosen, axis=1) - 1), axis=-1)
    target = routes * room + rank
    slot = lax.iota(jnp.int32, experts * room)[None, :, None]
    select = ((slot == target[:, None, :]) & (kept[:, None, :] > 0)).astype(bf16)
    live = ((routes[..., None] == lax.iota(jnp.int32, 128)) & (kept[..., None] > 0)).astype(f32)
    return select.reshape(layers, experts, room, count), live


def backward_layer(layer, grad, saved, gains, w_router, select, chosen, bias, w_qkv, w_output, w_in, w_out):
    x, turned, query, pair, merged, log_total, middle, router, picked, arrived, before = saved
    count, width = grad.shape
    parts, experts = lax.axis_size("context"), lax.axis_size("expert")
    wide = 3 * HEAD
    room = select.shape[1]
    hidden = w_in.shape[3]
    shape = jax.ShapeDtypeStruct
    scratch = pltpu.VMEM
    span = GROUP * count
    rows_in, rows_out = width // (GROUP * parts), hidden // (GROUP * parts)
    tall = rows_in // experts
    fars = parts // 2
    more = max(fars - 1, 1)
    return pl.pallas_call(
        functools.partial(backward_kernel, layer, parts, experts),
        out_shape=[
            shape((count, width), f32),
            shape((rows_in, hidden), f32),
            shape((rows_out, width), f32),
            shape((GROUP, parts, experts, tall, w_qkv.shape[2]), bf16),
            shape((2, parts, experts, tall, width // 2), bf16),
            shape(bias.shape, f32),
            shape((8, width), f32),
        ],
        in_specs=[VMEM] * 17 + [ANY] * 4,
        out_specs=[VMEM] * 7,
        scratch_shapes=[
            scratch((GROUP, parts, rows_in, hidden), bf16),
            scratch((GROUP, parts, rows_out, width), bf16),
            scratch((2, parts, rows_in, hidden), bf16),
            scratch((2, parts, rows_out, width), bf16),
            scratch((fars, 2, rows_in, hidden), bf16),
            scratch((fars, 2, rows_out, width), bf16),
            scratch((fars, rows_in, hidden), bf16),
            scratch((fars, rows_out, width), bf16),
            scratch((more, rows_in, hidden), bf16),
            scratch((more, rows_out, width), bf16),
            scratch((wide, width), f32),
            scratch((width, w_qkv.shape[2]), bf16),
            scratch((2 * BLOCK, width), bf16),
            scratch((experts, room, width), bf16),
            scratch((experts, room, width), bf16),
            scratch((experts, room, width), bf16),
            scratch((experts, room, width), bf16),
            scratch((GROUP, count, width), bf16),
            scratch((GROUP, count, 2 * BLOCK), bf16),
            scratch((GROUP, count, 2 * BLOCK), f32),
            scratch((parts - 1, 2 * wide, span), bf16),
            scratch((parts - 1, 2 * wide, span), bf16),
            scratch((GROUP, count, w_qkv.shape[2]), bf16),
            scratch((GROUP - 1, count, width), bf16),
            scratch((GROUP - 1, count, width), bf16),
            DMA((4,)),
            DMA((experts - 1,)),
            DMA((experts - 1,)),
            DMA((experts - 1,)),
            DMA((experts - 1,)),
            DMA((3,)),
            DMA((3,)),
            DMA((parts - 1,)),
            DMA((parts - 1,)),
            DMA((3,)),
            DMA((3,)),
            DMA((2, 2)),
            DMA((2, 2)),
            DMA((2, fars, 2)),
            DMA((2, fars, 2)),
            DMA((2, fars)),
            DMA((2, fars)),
            DMA((2, more)),
            DMA((2, more)),
        ],
        compiler_params=pltpu.CompilerParams(
            collective_id=2 + layer, has_side_effects=True, vmem_limit_bytes=(58 if parts <= 2 else 63) * 2**20
        ),
        name="layer_backward",
    )(
        grad, x, gains, w_router, select, chosen, bias, turned, query, pair, merged, log_total,
        middle, router, picked, arrived, before, w_qkv, w_output, w_in, w_out,
    )


def finish_kernel(
    layers,
    parts,
    experts,
    *refs,
):
    qkv, output, rows, bias = (refs[i * layers : (i + 1) * layers] for i in range(4))
    (
        buckets,
        out_key,
        out_value,
        out_query,
        out_output,
        out_rows,
        out_table,
        table_sum,
        qkv_core,
        output_core,
        small_mine,
        small_core,
        qkv_line,
        output_line,
        small_line,
        qkv_came,
        output_came,
        small_came,
        qkv_plane,
        output_plane,
        small_plane,
        qkv_last,
        output_last,
        small_last,
        core_send,
        core_recv,
        line_send,
        line_recv,
        plane_send,
        plane_recv,
        output_send,
        output_recv,
    ) = refs[4 * layers :]
    here = Place(parts, experts)
    side, level, fars = div(here.dp, 2), rem(here.context, 2), parts // 2
    wide = 3 * HEAD
    here.greet(plane=True)

    def to_core():
        made = []
        for layer in range(layers):
            for at in range(2):
                sems = core_send.at[layer, at], core_recv.at[layer, at]
                source = qkv[layer].at[2 * at + 1 - here.core]
                made.append(remote(source, qkv_core.at[layer, at], *sems, here.core_device()))
            sems = core_send.at[layer, 2], core_recv.at[layer, 2]
            made.append(
                remote(output[layer].at[1 - here.core], output_core.at[layer], *sems, here.core_device())
            )
        return made

    def small_to_core():
        sems = core_send.at[0, 3], core_recv.at[0, 3]
        return remote(small_mine, small_core, *sems, here.core_device())

    for copy in to_core():
        copy.start()
    marks = lanes(buckets_count(out_table), 128)
    row = lax.broadcasted_iota(jnp.int32, marks.shape, 0)
    table_sum[...] = jnp.zeros_like(table_sum)
    for head in range(3):
        grads = bias[0][head]
        for layer in range(1, layers):
            grads = grads + bias[layer][head]

        def one(bucket, made, grads=grads):
            lines = jnp.sum(jnp.where(buckets[...] == bucket, grads, 0.0), axis=0)
            line = jnp.sum(lines, axis=0, keepdims=True)
            return jnp.where(row == bucket, line, made)

        made = lax.fori_loop(0, buckets_count(out_table), one, jnp.zeros(marks.shape, f32))
        column = jnp.sum(made, axis=-1, keepdims=True)
        table_sum[...] += jnp.where(marks == 3 * here.block + head, column, 0.0)
    table_rows = table_sum.shape[0]
    for layer in range(layers):
        for piece in range(rows[layer].shape[1] // 128):
            first = (layer * (rows[layer].shape[1] // 128) + piece) * 8
            small_mine[first : first + 8, :] = rows[layer][:, piece * 128 : (piece + 1) * 128]
    small_mine[small_mine.shape[0] - table_rows :, :] = table_sum[...]
    small_to_core().start()

    def line(step, source):
        target = here.expert_other(step)
        device = {"expert": target}
        return [
            remote(qkv_line.at[target], qkv_came.at[source], line_send.at[0, step - 1], line_recv.at[0, step - 1], device),
            remote(output_line.at[target], output_came.at[source], line_send.at[1, step - 1], line_recv.at[1, step - 1], device),
            remote(small_line, small_came.at[source], line_send.at[2, step - 1], line_recv.at[2, step - 1], device),
        ]

    copies = to_core()
    for layer in range(layers):
        for copy in copies[3 * layer : 3 * layer + 3]:
            copy.wait_recv()
        for expert in range(experts):
            for context in range(parts):
                for at in range(2):
                    qkv_line[expert, layer, at, context] = (
                        qkv[layer][2 * at + here.core, context, expert].astype(f32)
                        + qkv_core[layer, at, context, expert].astype(f32)
                    ).astype(bf16)
                output_line[expert, layer, context] = (
                    output[layer][here.core, context, expert].astype(f32)
                    + output_core[layer, context, expert].astype(f32)
                ).astype(bf16)
    small_to_core().wait_recv()
    small_line[...] = small_mine[...] + small_core[...]
    for step in range(1, experts):
        for copy in line(step, here.expert):
            copy.start()
    for step in range(1, experts):
        for copy in line(step, rem(here.expert + experts - step, experts)):
            copy.wait_recv()
    sources = [rem(here.expert + step, experts) for step in range(1, experts)]
    for layer in range(layers):
        for context in range(parts):
            for at in range(2):
                total = qkv_line[here.expert, layer, at, context].astype(f32)
                for source in sources:
                    total = total + qkv_came[source, layer, at, context].astype(f32)
                qkv_plane[at, context, layer] = total.astype(bf16)
            total = output_line[here.expert, layer, context].astype(f32)
            for source in sources:
                total = total + output_came[source, layer, context].astype(f32)
            output_plane[context, layer] = total.astype(bf16)
    total = small_line[...]
    for source in sources:
        total = total + small_came[source]
    small_plane[...] = total

    def plane(block_from, far_from):
        made = []
        for step, flip, far, other, device in here.plane_others():
            sems = [(plane_send.at[kind, step, flip], plane_recv.at[kind, step, flip]) for kind in range(2)]
            source = qkv_plane.at[rem(other, 2), 2 * far + div(other, 2)]
            made.append(remote(source, qkv_last.at[here.block, here.far], *sems[0], device))
            made.append(remote(small_plane, small_last.at[here.block, here.far], *sems[1], device))
        return made

    for copy in plane(0, 0):
        copy.start()

    def hand_output(context):
        device = {"dp": here.block, "context": jnp.int32(context)}
        return remote(
            output_plane.at[context],
            output_last.at[here.core, here.far],
            output_send.at[context],
            output_recv.at[here.core, here.far],
            device,
        )

    def is_here(context):
        return (here.block == here.dp) & (here.context == context)

    for context in range(parts):

        @pl.when(jnp.logical_not(is_here(context)))
        def _():
            hand_output(context).start()

        @pl.when(is_here(context))
        def _():
            output_last[here.core, here.far] = output_plane[context]

    qkv_last[here.block, here.far] = qkv_plane[side, here.context]
    small_last[here.block, here.far] = small_plane[...]
    for copy in plane(0, 0):
        copy.wait_recv()
    for core in range(2):
        for far in range(fars):
            source_dp = 2 * here.core + core
            source_context = 2 * far + side

            @pl.when(jnp.logical_not((source_dp == here.dp) & (source_context == here.context)))
            def _():
                remote(
                    output_plane.at[0],
                    output_last.at[core, far],
                    output_send.at[0],
                    output_recv.at[core, far],
                    here.core_device(),
                ).wait_recv()

    total = jnp.zeros(small_plane.shape, f32)
    for block in range(GROUP):
        for far in range(fars):
            total = total + small_last[block, far]
        for layer in range(layers):
            made = qkv_last[block, 0, layer].astype(f32)
            for far in range(1, fars):
                made = made + qkv_last[block, far, layer].astype(f32)
            columns = slice(block * wide, (block + 1) * wide)
            out_key[layer, :, columns] = made[:, :wide]
            out_value[layer, :, columns] = made[:, wide : 2 * wide]
            out_query[layer, :, columns] = made[:, 2 * wide : 3 * wide]
    half = output_last.shape[4]
    for core in range(2):
        for layer in range(layers):
            made = output_last[core, 0, layer].astype(f32)
            for far in range(1, fars):
                made = made + output_last[core, far, layer].astype(f32)
            out_output[layer, :, core * half : (core + 1) * half] = made
    pieces = rows[0].shape[1] // 128
    for layer in range(layers):
        for piece in range(pieces):
            first = (layer * pieces + piece) * 8
            out_rows[layer, :, piece * 128 : (piece + 1) * 128] = total[first : first + 8, :]
    out_table[...] = total[total.shape[0] - table_rows :, :]
    for copy in to_core() + [small_to_core()] + plane(0, 0):
        copy.wait_send()
    for step in range(1, experts):
        for copy in line(step, here.expert):
            copy.wait_send()
    for context in range(parts):

        @pl.when(jnp.logical_not(is_here(context)))
        def _():
            hand_output(context).wait_send()


def buckets_count(table):
    return table.shape[0]


def finish(qkv, output, rows, bias, count_buckets):
    layers = len(qkv)
    parts, experts = lax.axis_size("context"), lax.axis_size("expert")
    fars = parts // 2
    tall, packed = qkv[0].shape[3:]
    half = output[0].shape[4]
    width = 2 * half
    small = layers * 8 * (width // 128) + count_buckets
    shape = jax.ShapeDtypeStruct
    scratch = pltpu.VMEM
    return pl.pallas_call(
        functools.partial(finish_kernel, layers, parts, experts),
        out_shape=[shape((layers, tall, width), f32)] * 4
        + [shape((layers, 8, width), f32), shape((count_buckets, 128), f32)],
        in_specs=[VMEM] * (4 * layers + 1),
        out_specs=[VMEM] * 6,
        scratch_shapes=[
            scratch((count_buckets, 128), f32),
            scratch((layers, 2, parts, experts, tall, packed), bf16),
            scratch((layers, parts, experts, tall, half), bf16),
            scratch((small, 128), f32),
            scratch((small, 128), f32),
            scratch((experts, layers, 2, parts, tall, packed), bf16),
            scratch((experts, layers, parts, tall, half), bf16),
            scratch((small, 128), f32),
            scratch((experts, layers, 2, parts, tall, packed), bf16),
            scratch((experts, layers, parts, tall, half), bf16),
            scratch((experts, small, 128), f32),
            scratch((2, parts, layers, tall, packed), bf16),
            scratch((parts, layers, tall, half), bf16),
            scratch((small, 128), f32),
            scratch((GROUP, fars, layers, tall, packed), bf16),
            scratch((2, fars, layers, tall, half), bf16),
            scratch((GROUP, fars, small, 128), f32),
            DMA((layers, 4)),
            DMA((layers, 4)),
            DMA((3, experts - 1)),
            DMA((3, experts - 1)),
            DMA((2, fars, GROUP)),
            DMA((2, fars, GROUP)),
            DMA((parts,)),
            DMA((2, fars)),
        ],
        compiler_params=pltpu.CompilerParams(
            collective_id=2 + layers, has_side_effects=True, vmem_limit_bytes=40 * 2**20
        ),
        name="finish",
    )(*qkv, *output, *rows, *bias, jnp.asarray(bucket_blocks()))


def on_device(tokens, w_query, w_key, w_value, w_output, rel_bias, gain_attn, gain_moe, w_router, w_in, w_out, routes, kept, cotangent):
    batch, count, width = tokens.shape
    experts = w_router.shape[2]
    room = count * 5 // (4 * experts)
    layers = w_query.shape[0]
    everywhere = ("dp", "context", "expert")
    block = 2 * (lax.axis_index("context") % 2) + lax.axis_index("dp") // 2
    x = swapped(tokens[0]).astype(f32)
    marks = swapped(jnp.stack([routes[:, 0, :, 0], kept[:, 0, :]]))
    grad = swapped(cotangent[0])
    select, chosen = routing(marks[0], marks[1], experts, room)
    bias = bias_blocks(rel_bias, 3 * block)
    wide = 3 * HEAD
    w_qkv = jnp.concatenate(
        [lax.dynamic_slice_in_dim(w, wide * block, wide, 2) for w in (w_key, w_value, w_query)], axis=2
    )
    w_qkv = jnp.pad(w_qkv, ((0, 0), (0, 0), (0, HEAD)))
    router_wide = jnp.pad(w_router, ((0, 0), (0, 0), (0, 128 - experts)))
    gains = jnp.stack([gain_attn, gain_moe], axis=1)
    shared = [(gains[i], router_wide[i], select[i], chosen[i], bias, w_qkv, w_output, w_in, w_out) for i in range(layers)]
    saved = []
    for layer in range(layers):
        turned, query, pair, merged, logs, low, middle, router, picked, arrived, before, x_next = forward_layer(layer, x, *shared[layer])
        saved.append((x, turned, query, pair, merged, logs, middle, router, picked, arrived, before))
        x = x_next
    out = swapped(x.astype(bf16))[None]
    grad = grad.astype(f32)
    in_list, out_list, parts_list = [], [], []
    for layer in reversed(range(layers)):
        grad, g_in, g_out, *others = backward_layer(layer, grad, saved[layer], *shared[layer])
        in_list.insert(0, g_in)
        out_list.insert(0, g_out)
        parts_list.insert(0, others)
    d_tokens = swapped(grad)[None]
    qkv, output, bias_grad, rows = zip(*parts_list)
    key_out, value_out, query_out, output_out, rows, table = finish(qkv, output, rows, bias_grad, rel_bias.shape[0])
    rank = (lax.axis_index("dp") * lax.axis_size("context") + lax.axis_index("context")) * experts + lax.axis_index("expert")
    tall = key_out.shape[1]
    rows = lax.dynamic_slice_in_dim(rows, rank * tall, tall, 2)
    return (
        out,
        d_tokens,
        query_out,
        key_out,
        value_out,
        output_out,
        table[:, : rel_bias.shape[1]],
        rows[:, 5],
        rows[:, 4],
        jnp.swapaxes(rows[:, :experts], 1, 2),
        jnp.stack(in_list)[:, None],
        jnp.stack(out_list)[:, None],
    )


def solution(mesh):
    in_specs = (
        P("dp", ("context", "expert"), None),
        P(),
        P(),
        P(),
        P(),
        P(),
        P(),
        P(),
        P(),
        P(None, "expert", None, None),
        P(None, "expert", None, None),
        P(None, "dp", ("context", "expert"), None),
        P(None, "dp", ("context", "expert")),
        P("dp", ("context", "expert"), None),
    )
    out_specs = (
        P("dp", ("context", "expert"), None),
        P("dp", ("context", "expert"), None),
        P(None, ("dp", "context", "expert"), None),
        P(None, ("dp", "context", "expert"), None),
        P(None, ("dp", "context", "expert"), None),
        P(None, ("dp", "context", "expert"), None),
        P(),
        P(None, ("dp", "context", "expert")),
        P(None, ("dp", "context", "expert")),
        P(None, ("dp", "context", "expert"), None),
        P(None, "expert", ("dp", "context"), None),
        P(None, "expert", ("dp", "context"), None),
    )
    return jax.shard_map(
        on_device, mesh=mesh, in_specs=in_specs, out_specs=out_specs, check_vma=False
    )
```

```python
import functools
from typing import Any, NamedTuple

import jax
import jax.numpy as jnp
import numpy as np
from jax import lax
from jax.experimental import pallas as pl
from jax.experimental.pallas import tpu as pltpu
from jax.sharding import PartitionSpec as P

highest = lax.Precision.HIGHEST
epsilon = 1e-06
thresholds = (12, 16, 23, 32, 46, 64, 91)
MESH = pl.DeviceIdType.MESH
GROUP = 4
HEAD = 64
BLOCK = 128
FCHUNK = 512
f32, bf16 = jnp.float32, jnp.bfloat16


def div(a, b):
    return lax.div(a, jnp.int32(b))


def rem(a, b):
    return lax.rem(a, jnp.int32(b))


def turned_pair(index):
    return 2 * rem(index, 2) + div(index, 2)


class Place:
    def __init__(self, parts, experts):
        self.parts, self.experts = parts, experts
        self.dp = lax.axis_index("dp")
        self.context = lax.axis_index("context")
        self.expert = lax.axis_index("expert")
        self.core = rem(self.dp, 2)
        self.far = div(self.context, 2)
        self.block = 2 * rem(self.context, 2) + div(self.dp, 2)
        self.part = 2 * self.far + self.core

    def flipped(self, flip):
        low = rem(rem(self.block, 2) + flip % 2, 2)
        high = rem(div(self.block, 2) + flip // 2, 2)
        return 2 * high + low

    def group_device(self, block):
        return {"dp": 2 * rem(block, 2) + self.core, "context": 2 * self.far + div(block, 2)}

    def part_other(self, step):
        return rem(self.part + step, self.parts)

    def part_device(self, part):
        return {
            "dp": self.dp - self.core + rem(part, 2),
            "context": 2 * div(part, 2) + rem(self.context, 2),
        }

    def expert_other(self, step):
        return rem(self.expert + step, self.experts)

    def offset(self, part, block, query_block):
        across = 4 * (block // 2 - div(query_block, 2)) + (block % 2 - rem(query_block, 2))
        return 8 * (part // 2 - self.far) + across + 2 * (part % 2 - self.core)

    def bias_index(self, part, block, query_block):
        offset = self.offset(part, block, query_block)
        return jnp.minimum(jnp.maximum(offset, -2), 2) + 2

    def core_device(self):
        return {"dp": self.dp + 1 - 2 * self.core}

    def plane_others(self):
        made = []
        for step in range(self.parts // 2):
            far = rem(self.far + step, self.parts // 2)
            for flip in range(GROUP):
                if step or flip:
                    other = self.flipped(flip)
                    device = {"dp": 2 * rem(other, 2) + self.core, "context": 2 * far + div(other, 2)}
                    made.append((step, flip, far, other, device))
        return made

    def is_swapped(self):
        return self.dp != turned_pair(self.expert)

    def swap_device(self):
        return {"dp": turned_pair(self.expert), "expert": turned_pair(self.dp)}

    def greet(self, plane=False, swap=False):
        if plane:
            partners = [item[-1] for item in self.plane_others()]
            partners += [{**device, "dp": device.get("dp") + 1 - 2 * self.core} for device in partners]
            partners += [self.core_device()]
        else:
            partners = [self.group_device(self.flipped(flip)) for flip in (1, 2, 3)]
            partners += [self.part_device(self.part_other(step)) for step in range(1, self.parts)]
        partners += [{"expert": self.expert_other(step)} for step in range(1, self.experts)]
        barrier = pltpu.get_barrier_semaphore()
        for partner in partners:
            pl.semaphore_signal(barrier, inc=1, device_id=partner, device_id_type=MESH)
        if swap:

            @pl.when(self.is_swapped())
            def _():
                pl.semaphore_signal(barrier, inc=1, device_id=self.swap_device(), device_id_type=MESH)
                pl.semaphore_wait(barrier, len(partners) + 1)

            @pl.when(jnp.logical_not(self.is_swapped()))
            def _():
                pl.semaphore_wait(barrier, len(partners))

        else:
            pl.semaphore_wait(barrier, len(partners))


def remote(source, target, send, receive, device):
    return pltpu.make_async_remote_copy(
        src_ref=source,
        dst_ref=target,
        send_sem=send,
        recv_sem=receive,
        device_id=device,
        device_id_type=MESH,
    )


def dot(a, b):
    return jnp.dot(a, b, preferred_element_type=f32)


def dot_nt(a, b):
    return lax.dot_general(a, b, (((1,), (1,)), ((), ())), preferred_element_type=f32)


def dot_tn(a, b):
    return lax.dot_general(a, b, (((0,), (0,)), ((), ())), preferred_element_type=f32)


def root_scale(value):
    return lax.rsqrt(jnp.mean(value * value, axis=-1, keepdims=True) + epsilon)


def lanes(rows, width):
    return lax.broadcasted_iota(jnp.int32, (rows, width), 1)


def gelu_parts(value):
    scale = 0.7978845608028654
    square = value * value
    inner = jnp.tanh(scale * (value + 0.044715 * (square * value)))
    half = 0.5 * (1.0 + inner)
    slope = half + 0.5 * value * (1.0 - inner * inner) * (scale * (1.0 + 3 * 0.044715 * square))
    return value * half, slope


def gelu(value):
    scale = 0.7978845608028654
    return value * (0.5 * (1.0 + jnp.tanh(scale * (value + 0.044715 * (value * value * value)))))


class Swap:
    def __init__(self, here, pairs, send, recv):
        self.here, self.pairs, self.send, self.recv = here, pairs, send, recv

    def copies(self, which):
        made = []
        for index in which:
            source, target = self.pairs[index]
            made.append(remote(source, target, self.send.at[index], self.recv.at[index], self.here.swap_device()))
        return made

    def start(self, which):
        @pl.when(self.here.is_swapped())
        def _():
            for copy in self.copies(which):
                copy.start()

        @pl.when(jnp.logical_not(self.here.is_swapped()))
        def _():
            for index in which:
                source, target = self.pairs[index]
                target[...] = source[...]

    def wait(self, which):
        @pl.when(self.here.is_swapped())
        def _():
            for copy in self.copies(which):
                copy.wait_recv()

    def drain(self):
        @pl.when(self.here.is_swapped())
        def _():
            for copy in self.copies(range(len(self.pairs))):
                copy.wait_send()


def route_tokens(marks, layer, layers, select, chosen):
    experts, room, count = select.shape
    route = marks[layer : layer + 1, :]
    live = marks[layers + layer : layers + layer + 1, :] > 0
    named = lax.broadcasted_iota(jnp.int32, (8, count), 0) == route
    before = lax.broadcasted_iota(jnp.int32, (count, count), 0)
    after = lax.broadcasted_iota(jnp.int32, (count, count), 1)
    named = named.astype(f32)
    ahead = dot(named.astype(bf16), (before < after).astype(f32).astype(bf16))
    rank = jnp.sum(named * ahead, axis=0, keepdims=True)
    slot = lax.broadcasted_iota(jnp.int32, (room, count), 0).astype(f32)
    for expert in range(experts):
        select[expert] = ((slot == rank) & (route == expert) & live).astype(f32).astype(bf16)
    chosen[...] = ((before == route) & live).astype(f32).T


def bucket_block(place, half):
    row = lax.broadcasted_iota(jnp.int32, (BLOCK, BLOCK), 0)
    column = lax.broadcasted_iota(jnp.int32, (BLOCK, BLOCK), 1)
    offset = (place - 2) * BLOCK + column - row
    distance = jnp.abs(offset)
    beyond = 8 + sum((distance >= limit).astype(jnp.int32) for limit in thresholds)
    return jnp.where(distance < 8, distance, beyond) + jnp.where(offset > 0, half, 0)


def bucket_range(place, half):
    return (half, 2 * half) if place == 3 else (0, half if place == 1 else 2 * half)


def make_bias(bias, rel_bias, first):
    half = rel_bias.shape[0] // 2
    for head in range(3):
        bias[head, 0] = jnp.full((BLOCK, BLOCK), rel_bias[half - 1, first + head], f32)
        bias[head, 4] = jnp.full((BLOCK, BLOCK), rel_bias[2 * half - 1, first + head], f32)
    for place in (1, 2, 3):
        buckets = bucket_block(place, half)
        for head in range(3):

            def one(bucket, made, buckets=buckets, head=head):
                return jnp.where(buckets == bucket, rel_bias[bucket, first + head], made)

            bias[head, place] = lax.fori_loop(*bucket_range(place, half), one, jnp.zeros((BLOCK, BLOCK), f32))


def pack_weights(w_qkv, slabs, block):
    wide = 3 * HEAD
    shape = (slabs.shape[1], w_qkv.shape[1])
    row = lax.broadcasted_iota(jnp.int32, shape, 0)
    column = lax.broadcasted_iota(jnp.int32, shape, 1)
    head, inside = column // BLOCK, column % BLOCK
    kind = inside // HEAD
    source = jnp.where(
        column < 2 * wide, 2 * BLOCK * kind + HEAD * head + inside % HEAD, 4 * BLOCK + column - 2 * wide
    )
    source = source + HEAD * rem(block, 2)
    move = ((row == source) & (column < 3 * wide)).astype(f32).astype(bf16)
    w_qkv[...] = dot(slabs[...], move).astype(bf16)


def ones_where(condition):
    return condition.astype(f32).astype(bf16)


def query_spread(rows, columns):
    row = lax.broadcasted_iota(jnp.int32, (rows, columns), 0)
    column = lax.broadcasted_iota(jnp.int32, (rows, columns), 1)
    return ones_where((column % BLOCK < HEAD) & (row == HEAD * (column // BLOCK) + column % BLOCK))


def half_select(rows, columns, half):
    row = lax.broadcasted_iota(jnp.int32, (rows, columns), 0)
    column = lax.broadcasted_iota(jnp.int32, (rows, columns), 1)
    return ones_where((row == BLOCK * (column // HEAD) + HEAD * half + column % HEAD) & (column < 3 * HEAD))


def forward_kernel(layer, layers, parts, experts, first, *refs):
    if first:
        tokens, cotangent, marks_here, rel_bias, *refs = refs
    else:
        x, marks, bias, *refs = refs
    (
        gain_attn,
        gain_moe,
        w_router,
        w_key_hbm,
        w_value_hbm,
        w_query_hbm,
        w_output_hbm,
        w_in_hbm,
        w_out_hbm,
        *refs,
    ) = refs
    if first:
        x, grad, marks, bias, *refs = refs
    forward_body(
        layer,
        layers,
        parts,
        experts,
        (tokens, cotangent, marks_here, rel_bias, grad) if first else None,
        x,
        marks,
        bias,
        gain_attn,
        gain_moe,
        w_router,
        w_key_hbm,
        w_value_hbm,
        w_query_hbm,
        w_output_hbm,
        w_in_hbm,
        w_out_hbm,
        *refs,
    )


def halves(arrays):
    first = arrays[0].shape[1]
    return (0, first), (first, first + arrays[1].shape[1])


def joined(slots):
    return jnp.concatenate([slots[index].astype(f32) for index in range(slots.shape[0])], axis=0).astype(bf16)


def forward_body(
    layer,
    layers,
    parts,
    experts,
    begin,
    x,
    marks,
    bias,
    gain_attn,
    gain_moe,
    w_router,
    w_key_hbm,
    w_value_hbm,
    w_query_hbm,
    w_output_hbm,
    w_in_hbm,
    w_out_hbm,
    select,
    chosen,
    w_qkv_out,
    turned_out,
    query_out,
    pair_out,
    merged_out,
    log_total_out,
    middle,
    router,
    picked,
    arrived,
    arrived_more,
    before_out,
    x_next,
    w_qkv,
    turned,
    query,
    pair,
    merged,
    log_total,
    merged_low,
    before,
    normed,
    slabs,
    w_output,
    w_in,
    w_out,
    scores,
    merged_mine,
    slots,
    slots_more,
    total,
    answer,
    answer_more,
    returned,
    returned_more,
    load_sem,
    store_sem,
    group_send,
    group_recv,
    part_send,
    part_recv,
    merge_send,
    merge_recv,
    slot_send,
    slot_recv,
    back_send,
    back_recv,
    tokens_came=None,
    swap_send=None,
    swap_recv=None,
):
    here = Place(parts, experts)
    heads = 3
    wide = heads * HEAD
    block = here.block
    if begin:
        tokens, cotangent, marks_here, rel_bias, grad = begin
        here.greet(swap=True)
        pairs = [(marks_here, marks), (tokens, tokens_came), (cotangent, grad)]
        swap = Swap(here, pairs, swap_send, swap_recv)
        swap.start((0, 1))
    stores = [
        pltpu.make_async_copy(source, target, store_sem.at[index])
        for index, (source, target) in enumerate(
            (
                (w_qkv, w_qkv_out),
                (turned, turned_out),
                (query, query_out),
                (pair, pair_out),
                (merged, merged_out),
                (log_total, log_total_out),
                (before, before_out),
            )
        )
    ]
    slab = pl.ds(pl.multiple_of(BLOCK * div(3 * block, 2), BLOCK), 2 * BLOCK)
    loads = []
    for kind, source in enumerate((w_key_hbm, w_value_hbm, w_query_hbm)):
        target = slabs.at[:, kind * 2 * BLOCK : (kind + 1) * 2 * BLOCK]
        loads.append(pltpu.make_async_copy(source.at[layer, :, slab], target, load_sem.at[kind]))
    loads += [
        pltpu.make_async_copy(w_output_hbm.at[layer], w_output, load_sem.at[3]),
        pltpu.make_async_copy(w_in_hbm.at[layer, 0], w_in, load_sem.at[4]),
        pltpu.make_async_copy(w_out_hbm.at[layer, 0], w_out, load_sem.at[5]),
    ]
    for load in loads:
        load.start()
    if begin:
        for load in loads[:3]:
            load.wait()
        pack_weights(w_qkv, slabs, block)
        swap.wait((0, 1))
        value = tokens_came[...].astype(f32)
        x[...] = value
    else:
        value = x[...]
    normed[block] = (value * root_scale(value) * gain_attn[layer : layer + 1, :]).astype(bf16)
    if not begin:
        here.greet()

    def gather(flip, source):
        return remote(
            normed.at[source],
            normed.at[source],
            group_send.at[flip - 1],
            group_recv.at[flip - 1],
            here.group_device(here.flipped(flip)),
        )

    for flip in (1, 2, 3):
        gather(flip, block).start()

    def hand_pair(step, part, of_block):
        return remote(
            pair.at[part, of_block],
            pair.at[part, of_block],
            part_send.at[step - 1, of_block],
            part_recv.at[step - 1, of_block],
            here.part_device(here.part_other(step)),
        )

    def project(of_block):
        made = dot(normed[of_block], w_qkv[...]).astype(bf16)
        pair[here.part, of_block] = made[:, : 2 * wide]
        query[of_block] = dot(made[:, 2 * wide :], query_spread(2 * BLOCK, 3 * BLOCK)).astype(bf16)
        for step in range(1, parts):
            hand_pair(step, here.part, of_block).start()
        columns = pl.ds(pl.multiple_of(of_block * BLOCK, BLOCK), BLOCK)
        turned[:, columns] = normed[of_block].astype(f32).T.astype(bf16)

    if begin:
        swap.start((2,))
    else:
        for load in loads[:3]:
            load.wait()
        pack_weights(w_qkv, slabs, block)
    project(block)
    route_tokens(marks, layer, layers, select, chosen)
    if begin:
        make_bias(bias, rel_bias, heads * block)
    for flip in (1, 2, 3):
        source = here.flipped(flip)
        gather(flip, source).wait_recv()
        project(source)
    for step in range(1, parts):
        source = rem(here.part + parts - step, parts)
        for of_block in range(GROUP):
            hand_pair(step, source, of_block).wait_recv()

    for store in stores[:4]:
        store.start()
    lane_log = lanes(BLOCK, BLOCK)

    def hand_merged(flip, source):
        return remote(
            merged_mine.at[here.flipped(flip)],
            merged_low.at[source],
            merge_send.at[flip - 1],
            merge_recv.at[flip - 1],
            here.group_device(here.flipped(flip)),
        )

    for flip in (3, 1, 2, 0):
        mine = here.flipped(flip)
        logs = jnp.zeros((BLOCK, BLOCK), f32)
        for head in range(heads):
            columns = slice(head * BLOCK, (head + 1) * BLOCK)
            top = jnp.full((BLOCK, 1), -1e30, f32)
            for part in range(parts):
                both = pair[part, :, :, columns].reshape(GROUP * BLOCK, BLOCK)
                raw = dot_nt(query[mine, :, columns], both)
                for of_block in range(GROUP):
                    piece = (
                        raw[:, of_block * BLOCK : (of_block + 1) * BLOCK]
                        + bias[head, here.bias_index(part, of_block, mine)]
                    )
                    scores[part * GROUP + of_block] = piece
                    top = jnp.maximum(top, jnp.max(piece, axis=-1, keepdims=True))
            summed = jnp.zeros((BLOCK, 1), f32)
            out = jnp.zeros((BLOCK, BLOCK), f32)
            for part in range(parts):
                pieces = []
                for of_block in range(GROUP):
                    weight = jnp.exp(scores[part * GROUP + of_block] - top)
                    summed = summed + jnp.sum(weight, axis=-1, keepdims=True)
                    pieces.append(weight.astype(bf16))
                both = pair[part, :, :, columns].reshape(GROUP * BLOCK, BLOCK)
                out = out + dot(jnp.concatenate(pieces, axis=1), both)
            merged[mine, :, columns] = jnp.where(lane_log >= HEAD, out / summed, 0.0)
            logs = jnp.where(lane_log == head, top + jnp.log(summed), logs)
        final = dot(merged[mine].astype(bf16), half_select(3 * BLOCK, wide, 1))
        log_total[mine] = logs
        if flip:
            merged_mine[mine] = final.astype(bf16)
            hand_merged(flip, block).start()
        else:
            merged_low[block] = final.astype(bf16)

    for store in stores[4:6]:
        store.start()
    for flip in (1, 2, 3):
        hand_merged(flip, here.flipped(flip)).wait_recv()
    loads[3].wait()
    mid = value
    for of_block in range(GROUP):
        mid = mid + dot(merged_low[of_block], w_output[of_block * wide : (of_block + 1) * wide, :])
    middle[...] = mid
    moe_in = mid * root_scale(mid) * gain_moe[layer : layer + 1, :]
    moe_low = moe_in.astype(bf16)

    slots, arrived = (slots, slots_more), (arrived, arrived_more)
    answer, returned = (answer, answer_more), (returned, returned_more)
    spans = halves(arrived)

    def hand_slots(half, step, source):
        return remote(
            slots[half].at[here.expert_other(step)],
            arrived[half].at[source],
            slot_send.at[half, step - 1],
            slot_recv.at[half, step - 1],
            {"expert": here.expert_other(step)},
        )

    for half, (low, high) in enumerate(spans):
        for expert in range(experts):
            slots[half][expert] = dot(select[expert, low:high], moe_low).astype(bf16)
        for step in range(1, experts):
            hand_slots(half, step, here.expert).start()
        arrived[half][here.expert] = slots[half][here.expert]
    logits = jnp.dot(moe_in, w_router[layer], precision=highest, preferred_element_type=f32)
    logits = jnp.where(lane_log < experts, logits, -1e30)
    raised = jnp.exp(logits - jnp.max(logits, axis=-1, keepdims=True))
    chances = raised / jnp.sum(raised, axis=-1, keepdims=True)
    router[...] = chances
    gate = jnp.sum(chances * chosen[...], axis=-1, keepdims=True)
    total[...] = jnp.zeros_like(total)
    loads[4].wait()
    loads[5].wait()

    def hand_answer(half, step, source):
        return remote(
            answer[half].at[here.expert_other(step)],
            returned[half].at[source],
            back_send.at[half, step - 1],
            back_recv.at[half, step - 1],
            {"expert": here.expert_other(step)},
        )

    for half, (low, high) in enumerate(spans):
        for step in range(1, experts):
            hand_slots(half, step, rem(here.expert + experts - step, experts)).wait_recv()
        given = joined(arrived[half])
        rows = slice(experts * low, experts * high)

        @pl.loop(0, w_in.shape[1] // FCHUNK)
        def _(index, given=given, rows=rows):
            columns = pl.ds(pl.multiple_of(index * FCHUNK, FCHUNK), FCHUNK)
            first = dot(given, w_in[:, columns])
            before[rows, columns] = first
            total[rows, :] += dot(gelu(first).astype(bf16), w_out[columns, :])

        for expert in range(experts):
            first = experts * low + expert * (high - low)
            answer[half][expert] = total[first : first + high - low, :].astype(bf16)
        for step in range(1, experts):
            hand_answer(half, step, here.expert).start()
        returned[half][here.expert] = answer[half][here.expert]
    stores[6].start()
    back = jnp.zeros_like(value)
    for half, (low, high) in enumerate(spans):
        for step in range(1, experts):
            hand_answer(half, step, rem(here.expert + experts - step, experts)).wait_recv()
        for expert in range(experts):
            back = back + dot_tn(select[expert, low:high], returned[half][expert])
    picked[...] = back.astype(bf16)
    x_next[...] = mid + gate * back
    for store in stores:
        store.wait()
    if begin:
        swap.wait((2,))
        swap.drain()
    for flip in (1, 2, 3):
        gather(flip, block).wait_send()
        hand_merged(flip, block).wait_send()
    for step in range(1, parts):
        for of_block in range(GROUP):
            hand_pair(step, here.part, of_block).wait_send()
    for step in range(1, experts):
        for half in range(2):
            hand_slots(half, step, here.expert).wait_send()
            hand_answer(half, step, here.expert).wait_send()


def table_sum(table, grads, block):
    marks = lanes(table, 128)
    row = lax.broadcasted_iota(jnp.int32, marks.shape, 0)
    half = table // 2
    total = jnp.zeros(marks.shape, f32)
    for head in range(3):
        made = jnp.zeros(marks.shape, f32)
        for place, bucket in ((0, half - 1), (4, 2 * half - 1)):
            line = jnp.sum(grads[head, place], axis=0, keepdims=True)
            made = made + jnp.where(row == bucket, line, 0.0)
        for place in (1, 2, 3):
            buckets = bucket_block(place, half)

            def one(bucket, made, buckets=buckets, place=place, head=head):
                found = jnp.where(buckets == bucket, grads[head, place], 0.0)
                return made + jnp.where(row == bucket, jnp.sum(found, axis=0, keepdims=True), 0.0)

            made = lax.fori_loop(*bucket_range(place, half), one, made)
        column = jnp.sum(made, axis=-1, keepdims=True)
        total = total + jnp.where(marks == 3 * block + head, column, 0.0)
    return total


class Saved(NamedTuple):
    x: Any
    grad: Any
    marks: Any
    bias: Any
    select: Any
    chosen: Any
    w_qkv: Any
    turned: Any
    query: Any
    pair: Any
    merged: Any
    log_total: Any
    middle: Any
    router: Any
    picked: Any
    arrived: Any
    arrived_more: Any
    before: Any
    x_next: Any


class Own(NamedTuple):
    grad_next: Any
    in_across: Any
    in_beside: Any
    in_own: Any
    out_across: Any
    out_beside: Any
    out_own: Any
    qkv: Any
    output: Any
    bias: Any
    rows: Any


class Taken(NamedTuple):
    in_across: Any
    in_beside: Any
    out_across: Any
    out_beside: Any
    qkv: Any
    output: Any
    rows: Any
    table_part: Any = None


class Given(NamedTuple):
    in_from_across: Any
    in_from_beside: Any
    out_from_across: Any
    out_from_beside: Any
    sums: Any
    rows_sum: Any
    table_out: Any = None


class Needed(NamedTuple):
    small: Any
    qkv_core: Any
    output_core: Any
    small_core: Any
    qkv_line: Any
    output_line: Any
    small_line: Any
    qkv_came: Any
    output_came: Any
    small_came: Any
    qkv_plane: Any
    output_plane: Any
    small_plane: Any
    qkv_last: Any
    output_last: Any
    small_last: Any
    expert_send: Any
    expert_recv: Any
    core_send: Any
    core_recv: Any
    line_send: Any
    line_recv: Any
    plane_send: Any
    plane_recv: Any
    output_send: Any
    output_recv: Any


def present(items):
    return [item for item in items if item is not None]


def taken_from(own, table):
    return Taken(
        own.in_across,
        own.in_beside,
        own.out_across,
        own.out_beside,
        own.qkv,
        own.output,
        own.rows,
        own.bias if table else None,
    )


class Earlier:
    def __init__(self, parts, experts, table, taken, given, needed):
        self.parts, self.experts, self.table, self.fars = parts, experts, table, parts // 2
        for refs in (Taken(*taken), Given(*given), Needed(*needed)):
            self.__dict__.update(refs._asdict())

    def expert_copies(self, which=(0, 1, 2, 3)):
        here, made = self.here, []
        across, beside = here.group_device(here.flipped(1)), here.group_device(here.flipped(2))
        for kind, (source, target, device) in enumerate(
            (
                (self.in_across, self.in_from_across, across),
                (self.out_beside, self.out_from_beside, beside),
                (self.in_beside, self.in_from_beside, beside),
                (self.out_across, self.out_from_across, across),
            )
        ):
            half = source.shape[2] // 2
            for turn in range(2):
                if kind // 2 * 2 + turn in which:
                    columns = slice(turn * half, (turn + 1) * half)
                    sems = self.expert_send.at[kind, turn], self.expert_recv.at[kind, turn]
                    made.append(remote(source.at[:, :, columns], target.at[:, :, columns], *sems, device))
        return made

    def core_copies(self):
        here, made = self.here, []
        device = here.core_device()
        for at in range(2):
            sems = self.core_send.at[at], self.core_recv.at[at]
            made.append(remote(self.qkv.at[2 * at + 1 - here.core], self.qkv_core.at[at], *sems, device))
        sems = self.core_send.at[2], self.core_recv.at[2]
        made.append(remote(self.output.at[1 - here.core], self.output_core, *sems, device))
        sems = self.core_send.at[3], self.core_recv.at[3]
        made.append(remote(self.small, self.small_core, *sems, device))
        return made

    def line_copies(self, step, source):
        here = self.here
        target = here.expert_other(step)
        device = {"expert": target}
        sems = [(self.line_send.at[kind, step - 1], self.line_recv.at[kind, step - 1]) for kind in range(3)]
        return [
            remote(self.qkv_line.at[target], self.qkv_came.at[source], *sems[0], device),
            remote(self.output_line.at[target], self.output_came.at[source], *sems[1], device),
            remote(self.small_line, self.small_came.at[source], *sems[2], device),
        ]

    def plane_copies(self):
        here, made = self.here, []
        for step, flip, far, other, device in here.plane_others():
            sems = [(self.plane_send.at[kind, step, flip], self.plane_recv.at[kind, step, flip]) for kind in range(2)]
            source = self.qkv_plane.at[rem(other, 2), 2 * far + div(other, 2)]
            made.append(remote(source, self.qkv_last.at[here.block, here.far], *sems[0], device))
            made.append(remote(self.small_plane, self.small_last.at[here.block, here.far], *sems[1], device))
        return made

    def output_copy(self, context):
        here = self.here
        return remote(
            self.output_plane.at[context],
            self.output_last.at[here.core, here.far],
            self.output_send.at[context],
            self.output_recv.at[here.core, here.far],
            {"dp": here.block, "context": jnp.int32(context)},
        )

    def is_here(self, context):
        return (self.here.block == self.here.dp) & (self.here.context == context)

    def begin(self, here, which=(0, 1, 2, 3)):
        self.here = here
        for copy in self.expert_copies(which):
            copy.start()
        pieces = self.rows.shape[1] // 128
        for piece in range(pieces):
            self.small[8 * piece : 8 * piece + 8, :] = self.rows[:, piece * 128 : (piece + 1) * 128]
        for copy in self.core_copies()[:3]:
            copy.start()
        if self.table:
            self.small[8 * pieces :, :] = self.table_part[...]
        self.core_copies()[3].start()

    def pass_line(self):
        here = self.here
        for copy in self.core_copies():
            copy.wait_recv()
        for expert in range(self.experts):
            for context in range(self.parts):
                for at in range(2):
                    self.qkv_line[expert, at, context] = (
                        self.qkv[2 * at + here.core, context, expert].astype(f32)
                        + self.qkv_core[at, context, expert].astype(f32)
                    ).astype(bf16)
                self.output_line[expert, context] = (
                    self.output[here.core, context, expert].astype(f32)
                    + self.output_core[context, expert].astype(f32)
                ).astype(bf16)
        self.small_line[...] = self.small[...] + self.small_core[...]
        for step in range(1, self.experts):
            for copy in self.line_copies(step, here.expert):
                copy.start()

    def pass_plane(self, which=()):
        here = self.here
        for step in range(1, self.experts):
            for copy in self.line_copies(step, rem(here.expert + self.experts - step, self.experts)):
                copy.wait_recv()
        sources = [rem(here.expert + step, self.experts) for step in range(1, self.experts)]
        for context in range(self.parts):
            for at in range(2):
                total = self.qkv_line[here.expert, at, context].astype(f32)
                for source in sources:
                    total = total + self.qkv_came[source, at, context].astype(f32)
                self.qkv_plane[at, context] = total.astype(bf16)
            total = self.output_line[here.expert, context].astype(f32)
            for source in sources:
                total = total + self.output_came[source, context].astype(f32)
            self.output_plane[context] = total.astype(bf16)
        total = self.small_line[...]
        for source in sources:
            total = total + self.small_came[source]
        self.small_plane[...] = total
        for copy in self.plane_copies():
            copy.start()
        for context in range(self.parts):

            @pl.when(jnp.logical_not(self.is_here(context)))
            def _():
                self.output_copy(context).start()

            @pl.when(self.is_here(context))
            def _():
                self.output_last[here.core, here.far] = self.output_plane[context]

        for copy in self.expert_copies(which):
            copy.start()
        self.qkv_last[here.block, here.far] = self.qkv_plane[div(here.dp, 2), here.context]
        self.small_last[here.block, here.far] = self.small_plane[...]

    def finish(self):
        here = self.here
        for copy in self.plane_copies():
            copy.wait_recv()
        for core in range(2):
            for far in range(self.fars):
                source_dp = 2 * here.core + core
                source_context = 2 * far + div(here.dp, 2)

                @pl.when(jnp.logical_not((source_dp == here.dp) & (source_context == here.context)))
                def _():
                    remote(
                        self.output_plane.at[0],
                        self.output_last.at[core, far],
                        self.output_send.at[0],
                        self.output_recv.at[core, far],
                        here.core_device(),
                    ).wait_recv()

        wide = 3 * HEAD
        total = jnp.zeros(self.small_plane.shape, f32)
        for block in range(GROUP):
            made = jnp.zeros(self.qkv_last.shape[2:], f32)
            for far in range(self.fars):
                total = total + self.small_last[block, far]
                made = made + self.qkv_last[block, far].astype(f32)
            columns = slice(block * wide, (block + 1) * wide)
            for head in range(3):
                part = slice(block * wide + head * HEAD, block * wide + (head + 1) * HEAD)
                for kind in range(2):
                    first = head * BLOCK + kind * HEAD
                    self.sums[kind, :, part] = made[:, first : first + HEAD]
            self.sums[2, :, columns] = made[:, 2 * wide : 3 * wide]
        half = self.output_last.shape[3]
        for core in range(2):
            made = self.output_last[core, 0].astype(f32)
            for far in range(1, self.fars):
                made = made + self.output_last[core, far].astype(f32)
            self.sums[3, :, core * half : (core + 1) * half] = made
        pieces = self.rows.shape[1] // 128
        for piece in range(pieces):
            self.rows_sum[:, piece * 128 : (piece + 1) * 128] = total[8 * piece : 8 * piece + 8, :]
        if self.table:
            self.table_out[...] = total[8 * pieces :, :]
        for copy in self.expert_copies():
            copy.wait()
        for copy in self.core_copies() + self.plane_copies():
            copy.wait_send()
        for step in range(1, self.experts):
            for copy in self.line_copies(step, here.expert):
                copy.wait_send()
        for context in range(self.parts):

            @pl.when(jnp.logical_not(self.is_here(context)))
            def _():
                self.output_copy(context).wait_send()


def earlier_call(parts, experts, left, table):
    tall, packed = left.qkv.shape[3:]
    half = left.output.shape[4]
    fars = parts // 2
    small = 8 * (2 * half // 128) + (table or 0)
    shape, scratch = jax.ShapeDtypeStruct, pltpu.VMEM
    specs = [ANY] * 4 + [VMEM] * (4 if table else 3)
    gives = Given(
        shape(left.in_across.shape, bf16),
        shape(left.in_across.shape, bf16),
        shape(left.out_across.shape, bf16),
        shape(left.out_across.shape, bf16),
        shape((4, tall, 2 * half), f32),
        shape((8, 2 * half), f32),
        shape((table, 128), f32) if table else None,
    )
    needs = Needed(
        small=scratch((small, 128), f32),
        qkv_core=scratch((2, parts, experts, tall, packed), bf16),
        output_core=scratch((parts, experts, tall, half), bf16),
        small_core=scratch((small, 128), f32),
        qkv_line=scratch((experts, 2, parts, tall, packed), bf16),
        output_line=scratch((experts, parts, tall, half), bf16),
        small_line=scratch((small, 128), f32),
        qkv_came=scratch((experts, 2, parts, tall, packed), bf16),
        output_came=scratch((experts, parts, tall, half), bf16),
        small_came=scratch((experts, small, 128), f32),
        qkv_plane=scratch((2, parts, tall, packed), bf16),
        output_plane=scratch((parts, tall, half), bf16),
        small_plane=scratch((small, 128), f32),
        qkv_last=scratch((GROUP, fars, tall, packed), bf16),
        output_last=scratch((2, fars, tall, half), bf16),
        small_last=scratch((GROUP, fars, small, 128), f32),
        expert_send=DMA((4, 2)),
        expert_recv=DMA((4, 2)),
        core_send=DMA((4,)),
        core_recv=DMA((4,)),
        line_send=DMA((3, experts - 1)),
        line_recv=DMA((3, experts - 1)),
        plane_send=DMA((2, fars, GROUP)),
        plane_recv=DMA((2, fars, GROUP)),
        output_send=DMA((parts,)),
        output_recv=DMA((2, fars)),
    )
    given_specs = [ANY] * 4 + [VMEM] * (3 if table else 2)
    return specs, gives, given_specs, needs


def finish_kernel(parts, experts, table, last, *refs):
    here = Place(parts, experts)
    swap = None
    if last:
        grad, *refs = refs
        *refs, grad_low, grad_came, send, recv = refs
    takes = 8 if table else 7
    taken, refs = refs[:takes], refs[takes:]
    if last:
        d_tokens, *refs = refs
        swap = Swap(here, [(grad_low, grad_came)], send, recv)
    gives = takes - 1
    earlier = Earlier(parts, experts, table, taken, refs[:gives], refs[gives:])
    here.greet(plane=True, swap=last)
    earlier.begin(here, (0, 1, 2))
    if last:
        grad_low[...] = grad[...].astype(bf16)
        swap.start((0,))
    earlier.pass_line()
    earlier.pass_plane((3,))
    earlier.finish()
    if last:
        swap.wait((0,))
        d_tokens[...] = grad_came[...].astype(f32)
        swap.drain()


def finish(left, table, number, grad=None):
    parts, experts = lax.axis_size("context"), lax.axis_size("expert")
    specs, gives, given_specs, needs = earlier_call(parts, experts, left, table)
    last = grad is not None
    given = pl.pallas_call(
        functools.partial(finish_kernel, parts, experts, table, last),
        out_shape=([jax.ShapeDtypeStruct(grad.shape, f32)] if last else []) + present(gives),
        in_specs=[VMEM] * last + specs,
        out_specs=[VMEM] * last + given_specs,
        scratch_shapes=list(needs)
        + ([pltpu.VMEM(grad.shape, bf16)] * 2 + [DMA((1,)), DMA((1,))] if last else []),
        compiler_params=pltpu.CompilerParams(
            collective_id=number, has_side_effects=True, vmem_limit_bytes=60 * 2**20
        ),
        name="finish",
    )(*([grad] if last else []), *present(taken_from(left, table)))
    return Given(*given[last:]), given[0]


def backward_and_earlier(layer, parts, experts, counts, earlier_bias, table, *refs):
    own_in, takes, own_out, gives, needs, last = counts
    own_scratch = len(refs) - own_in - takes - own_out - gives - needs - 5 * last
    cuts = np.cumsum([0, own_in, takes, last, own_out, gives, last, own_scratch, needs, 3 * last])
    pieces = [refs[a:b] for a, b in zip(cuts[:-1], cuts[1:], strict=True)]
    earlier = Earlier(parts, experts, None, pieces[1], pieces[4], pieces[7]) if takes else None
    backward_kernel(
        layer,
        parts,
        experts,
        *pieces[0],
        *pieces[3],
        *pieces[6],
        earlier=earlier,
        earlier_bias=earlier_bias,
        table=table,
        last=pieces[2] + pieces[5] + pieces[8] if last else None,
    )


def backward_kernel(
    layer,
    parts,
    experts,
    grad,
    x,
    gain_attn,
    gain_moe,
    w_router,
    select,
    chosen,
    bias_hbm,
    bias_before,
    turned_hbm,
    query_hbm,
    pair_hbm,
    merged_hbm,
    log_total_hbm,
    middle,
    router,
    picked,
    arrived,
    arrived_more,
    before_hbm,
    w_qkv_hbm,
    w_output_hbm,
    w_in_hbm,
    w_out_hbm,
    grad_next,
    in_across,
    in_beside,
    in_own,
    out_across,
    out_beside,
    out_own,
    grad_qkv_out,
    grad_output,
    grad_bias_out,
    grad_rows,
    bias,
    turned,
    query,
    pair,
    merged,
    log_total,
    grad_qkv,
    grad_bias,
    grad_in,
    grad_out,
    core_in,
    core_out,
    second_in,
    second_out,
    output_sum,
    w_qkv,
    w_output,
    slots,
    slots_more,
    arrived_grad,
    arrived_grad_more,
    answer,
    answer_more,
    returned,
    returned_more,
    given_grad,
    branches,
    query_grad,
    pair_sent,
    pair_recv,
    made_grad,
    normed_sent,
    normed_recv,
    load_sem,
    slot_send,
    slot_recv,
    back_send,
    back_recv,
    group_send,
    group_recv,
    part_send,
    part_recv,
    merge_send,
    merge_recv,
    core_send,
    core_recv,
    second_send,
    second_recv,
    store_sem,
    earlier=None,
    earlier_bias=False,
    last=None,
    table=None,
):
    here = Place(parts, experts)
    heads = 3
    wide = heads * HEAD
    block = here.block
    fars = parts // 2
    side, level = div(here.dp, 2), rem(here.context, 2)
    across, beside = here.group_device(here.flipped(1)), here.group_device(here.flipped(2))
    own_in, own_out = grad_in.at[2 * side + here.core], grad_out.at[2 * side + here.core]

    def to_core(turns=(0, 1)):
        made = []
        for at in turns:
            there = 2 * at + 1 - here.core
            for kind, (source, target) in enumerate(((grad_in, core_in), (grad_out, core_out))):
                sems = core_send.at[kind, at], core_recv.at[kind, at]
                made.append(remote(source.at[there], target.at[at], *sems, here.core_device()))
        return made

    def second():
        made = []
        for far in range(fars):
            sems = second_send.at[0, far], second_recv.at[0, far]
            source = grad_in.at[2 * (1 - side) + here.core, 2 * far + 1 - level]
            made.append(remote(source, second_in.at[far], *sems, across))
            sems = second_send.at[1, far], second_recv.at[1, far]
            source = grad_out.at[2 * (1 - side) + here.core, 2 * far + 1 - level]
            made.append(remote(source, second_out.at[far], *sems, beside))
        return made

    def stores(kinds):
        made = []
        there = 2 * (1 - side) + here.core
        for far in range(fars):
            for kind, (source, target) in enumerate(
                (
                    (grad_in.at[there, 2 * far + level], in_across),
                    (own_in.at[2 * far + 1 - level], in_beside),
                    (own_in.at[2 * far + level], in_own),
                    (grad_out.at[there, 2 * far + level], out_across),
                    (own_out.at[2 * far + 1 - level], out_beside),
                    (own_out.at[2 * far + level], out_own),
                )
            ):
                if kind in kinds:
                    made.append(pltpu.make_async_copy(source, target.at[far], store_sem.at[kind, far]))
        return made

    def add(target, source):
        target[...] = (target[...].astype(f32) + source[...].astype(f32)).astype(bf16)
    later = [
        pltpu.make_async_copy(source, target, load_sem.at[6 + index])
        for index, (source, target) in enumerate(
            (
                (w_qkv_hbm, w_qkv),
                (turned_hbm, turned),
                (query_hbm, query),
                (pair_hbm, pair),
                (merged_hbm, merged),
                (log_total_hbm, log_total),
                (bias_hbm, bias),
                (bias_before, grad_bias),
            )[: 8 if earlier_bias else 7]
        )
    ]
    for head in range(heads):
        rows = pl.ds(pl.multiple_of(block * wide + head * HEAD, HEAD), HEAD)
        target = w_output.at[head * BLOCK + HEAD : (head + 1) * BLOCK]
        later.append(pltpu.make_async_copy(w_output_hbm.at[layer, rows], target, load_sem.at[3 + head]))

    slots, arrived_grad = (slots, slots_more), (arrived_grad, arrived_grad_more)
    answer, returned = (answer, answer_more), (returned, returned_more)
    spans = halves((arrived, arrived_more))

    def hand_slots(half, step, source):
        return remote(
            slots[half].at[here.expert_other(step)],
            arrived_grad[half].at[source],
            slot_send.at[half, step - 1],
            slot_recv.at[half, step - 1],
            {"expert": here.expert_other(step)},
        )

    def hand_answer(half, step, source):
        return remote(
            answer[half].at[here.expert_other(step)],
            returned[half].at[source],
            back_send.at[half, step - 1],
            back_recv.at[half, step - 1],
            {"expert": here.expert_other(step)},
        )

    def experts_phase(w_in, w_out, hidden, slope, before_grad, total, turned_given):
        loads = [
            pltpu.make_async_copy(before_hbm, slope, load_sem.at[2]),
            pltpu.make_async_copy(w_out_hbm.at[layer, 0], w_out, load_sem.at[0]),
            pltpu.make_async_copy(w_in_hbm.at[layer, 0], w_in, load_sem.at[1]),
        ]
        for load in loads + later:
            load.start()
        for head in range(heads):
            w_output[head * BLOCK : head * BLOCK + HEAD, :] = jnp.zeros((HEAD, w_output.shape[1]), bf16)
        came = grad[...].astype(f32)
        chances = router[...]
        gate = jnp.sum(chances * chosen[...], axis=-1, keepdims=True)
        gate_grad = jnp.sum(came * picked[...].astype(f32), axis=-1, keepdims=True)
        answer_grad = (gate * came).astype(bf16)
        for half, (low, high) in enumerate(spans):
            for expert in range(experts):
                slots[half][expert] = dot(select[expert, low:high], answer_grad).astype(bf16)
        here.greet(plane=earlier is not None, swap=last is not None)
        if earlier:
            earlier.begin(here)

        for half in range(2):
            for step in range(1, experts):
                hand_slots(half, step, here.expert).start()
            arrived_grad[half][here.expert] = slots[half][here.expert]
        hidden_width = w_in.shape[1]

        loads[0].wait()

        @pl.loop(0, hidden_width // FCHUNK)
        def _(index):
            columns = pl.ds(pl.multiple_of(index * FCHUNK, FCHUNK), FCHUNK)
            made, steep = gelu_parts(slope[:, columns])
            hidden[:, columns] = made.astype(bf16)
            slope[:, columns] = steep

        mid = middle[...]
        scale = root_scale(mid)
        unit = mid * scale
        moe_in = unit * gain_moe[layer : layer + 1, :]
        chance_grad = chosen[...] * gate_grad
        logit_grad = chances * (chance_grad - jnp.sum(chances * chance_grad, axis=-1, keepdims=True))
        router_grad = lax.dot_general(
            logit_grad, moe_in, (((0,), (0,)), ((), ())), precision=highest, preferred_element_type=f32
        )
        grad_rows[...] = router_grad[:8, :]
        moe_part = lax.dot_general(
            logit_grad, w_router[layer], (((1,), (1,)), ((), ())), precision=highest, preferred_element_type=f32
        )
        given = jnp.concatenate([joined(arrived), joined(arrived_more)], axis=0)
        turned_given[...] = given.astype(f32).T.astype(bf16)
        total[...] = jnp.zeros_like(total)
        loads[1].wait()
        loads[2].wait()
        for half, (low, high) in enumerate(spans):
            for step in range(1, experts):
                hand_slots(half, step, rem(here.expert + experts - step, experts)).wait_recv()
            rows = slice(experts * low, experts * high)
            given_grad[rows, :] = joined(arrived_grad[half])

            @pl.loop(0, hidden_width // FCHUNK)
            def _(index, rows=rows):
                columns = pl.ds(pl.multiple_of(index * FCHUNK, FCHUNK), FCHUNK)
                hidden_grad = dot_nt(given_grad[rows, :], w_out[columns, :])
                low_grad = (hidden_grad * slope[rows, columns]).astype(bf16)
                before_grad[rows, columns] = low_grad
                total[rows, :] += dot_nt(low_grad, w_in[:, columns])

            for expert in range(experts):
                first = experts * low + expert * (high - low)
                answer[half][expert] = total[first : first + high - low, :].astype(bf16)
            for step in range(1, experts):
                hand_answer(half, step, here.expert).start()
            returned[half][here.expert] = answer[half][here.expert]
        rows_in, rows_out = grad_in.shape[2], grad_out.shape[2]
        columns_in = grad_in.shape[3] // GROUP
        for turn in range(4):
            there = 2 * (turn % 2) + (1 - here.core if turn < 2 else here.core)
            rows = pl.ds(pl.multiple_of(there * (parts * rows_in), parts * rows_in), parts * rows_in)
            for piece in range(GROUP):
                columns = slice(piece * columns_in, (piece + 1) * columns_in)
                made = dot(turned_given[rows, :], before_grad[:, columns])
                for at in range(parts):
                    grad_in[there, at, :, columns] = made[at * rows_in : (at + 1) * rows_in, :].astype(bf16)
            columns = pl.ds(pl.multiple_of(there * (parts * rows_out), parts * rows_out), parts * rows_out)
            made = dot_tn(hidden[:, columns], given_grad[...])
            for at in range(parts):
                grad_out[there, at] = made[at * rows_out : (at + 1) * rows_out, :].astype(bf16)
            if turn < 2:
                for copy in to_core((turn,)):
                    copy.start()

        moe_grad = moe_part
        for half, (low, high) in enumerate(spans):
            for step in range(1, experts):
                hand_answer(half, step, rem(here.expert + experts - step, experts)).wait_recv()
            for expert in range(experts):
                moe_grad = moe_grad + dot_tn(select[expert, low:high], returned[half][expert])
        grad_rows[4:5, :] = jnp.sum(moe_grad * unit, axis=0, keepdims=True)
        scaled = moe_grad * gain_moe[layer : layer + 1, :]
        mid_grad = came + scale * (scaled - unit * jnp.mean(unit * scaled, axis=-1, keepdims=True))
        branches[block] = mid_grad.astype(bf16)
        return mid_grad

    slot_rows = given_grad.shape[0]
    mid_grad = pl.run_scoped(
        experts_phase,
        pltpu.VMEM(w_in_hbm.shape[2:], bf16),
        pltpu.VMEM(w_out_hbm.shape[2:], bf16),
        pltpu.VMEM(before_hbm.shape, bf16),
        pltpu.VMEM(before_hbm.shape, f32),
        pltpu.VMEM(before_hbm.shape, bf16),
        pltpu.VMEM((slot_rows, grad.shape[1]), f32),
        pltpu.VMEM((grad.shape[1], slot_rows), bf16),
    )

    def gather(flip, source):
        return remote(
            branches.at[source],
            branches.at[source],
            group_send.at[flip - 1],
            group_recv.at[flip - 1],
            here.group_device(here.flipped(flip)),
        )

    for flip in (1, 2, 3):
        gather(flip, block).start()
    for turn in range(2):
        for copy in to_core((turn,)):
            copy.wait_recv()
        for at in range(parts):
            add(grad_in.at[2 * turn + here.core, at], core_in.at[turn, at])
            add(grad_out.at[2 * turn + here.core, at], core_out.at[turn, at])
    for copy in second() + stores((0, 2, 4, 5)):
        copy.start()
    if earlier:
        earlier.pass_line()
    for load in later:
        load.wait()
    def hand_pair(step, source):
        return remote(
            pair_sent.at[step - 1],
            pair_recv.at[step - 1],
            part_send.at[step - 1],
            part_recv.at[step - 1],
            here.part_device(here.part_other(step)),
        )

    def attention_phase(pair_grad):
        lane = lanes(BLOCK, BLOCK)
        if not earlier_bias:
            grad_bias[...] = jnp.zeros_like(grad_bias)
        for flip in range(GROUP):
            mine = here.flipped(flip)
            if flip:
                gather(flip, mine).wait_recv()
            wanted = dot_nt(branches[mine], w_output[...])
            wanted_low = wanted.astype(bf16)
            wanted = wanted_low.astype(f32)
            turned_rows = jnp.concatenate([query[mine].astype(f32).T, wanted.T], axis=1).astype(bf16)
            products = wanted * merged[mine]
            for head in range(heads):
                columns = slice(head * BLOCK, (head + 1) * BLOCK)
                rows = jnp.concatenate([query[mine, :, columns], wanted_low[:, columns]], axis=0)
                delta = jnp.sum(products[:, columns], axis=-1, keepdims=True)
                log_sum = log_total[mine][:, head : head + 1]
                gathered = jnp.zeros((BLOCK, BLOCK), f32)
                for part in range(parts):
                    both = pair[part, :, :, columns].reshape(GROUP * BLOCK, BLOCK)
                    raw = dot_nt(rows, both)
                    upper, lower = [], []
                    for of_block in range(GROUP):
                        inside = slice(of_block * BLOCK, (of_block + 1) * BLOCK)
                        place = here.bias_index(part, of_block, mine)
                        weight = jnp.exp(raw[:BLOCK, inside] + (bias[head, place] - log_sum))
                        score_grad = weight * (raw[BLOCK:, inside] - delta)
                        grad_bias[head, place] += score_grad
                        upper.append(score_grad.astype(bf16))
                        lower.append(weight.astype(bf16))
                    upper = jnp.concatenate(upper, axis=1)
                    stacked = jnp.concatenate([upper, jnp.concatenate(lower, axis=1)], axis=0)
                    gathered = gathered + dot(upper, both)
                    more = dot(turned_rows[columns], stacked)
                    if flip:
                        pair_grad[part, columns, :] += more
                    else:
                        pair_grad[part, columns, :] = more
                query_grad[mine, :, columns] = jnp.where(lane < HEAD, gathered, 0.0).astype(bf16)
        for step in range(1, parts):
            pair_sent[step - 1] = pair_grad[here.part_other(step)].astype(bf16)
            hand_pair(step, 0).start()
        summed = pair_grad[here.part]
        for step in range(1, parts):
            hand_pair(step, 0).wait_recv()
            summed = summed + pair_recv[step - 1].astype(f32)
        summed = summed.T.astype(bf16)
        for of_block in range(GROUP):
            made_grad[of_block, :, : 2 * wide] = summed[of_block * BLOCK : (of_block + 1) * BLOCK, :]
            made_grad[of_block, :, 2 * wide :] = dot(
                query_grad[of_block], half_select(3 * BLOCK, 2 * BLOCK, 0)
            ).astype(bf16)

    pl.run_scoped(attention_phase, pltpu.VMEM((parts, 2 * wide, GROUP * BLOCK), f32))

    def hand_normed(flip):
        return remote(
            normed_sent.at[flip - 1],
            normed_recv.at[flip - 1],
            merge_send.at[flip - 1],
            merge_recv.at[flip - 1],
            here.group_device(here.flipped(flip)),
        )

    for flip in (3, 1, 2):
        normed_sent[flip - 1] = dot_nt(made_grad[here.flipped(flip)], w_qkv[...]).astype(bf16)
        hand_normed(flip).start()
    if last:
        x_last, out, out_low, send, recv = last
        out_low[...] = x_last[...].astype(bf16)
        swap = Swap(here, [(out_low, out)], send, recv)
        swap.start((0,))
    normed_grad = dot_nt(made_grad[block], w_qkv[...])
    if earlier:
        earlier.pass_plane()
    both = made_grad[...].reshape(GROUP * BLOCK, made_grad.shape[2])
    rows = turned.shape[0] // GROUP
    tall = grad_qkv.shape[3]
    for there in range(GROUP):
        made = dot(turned[there * rows : (there + 1) * rows, :], both)
        for at in range(parts):
            for expert in range(experts):
                first = (at * experts + expert) * tall
                grad_qkv[there, at, expert] = made[first : first + tall, :].astype(bf16)
    made = dot_tn(
        merged[...].reshape(GROUP * BLOCK, 3 * BLOCK).astype(bf16),
        branches[...].reshape(GROUP * BLOCK, branches.shape[2]),
    )
    for head in range(heads):
        output_sum[head * HEAD : (head + 1) * HEAD, :] = made[head * BLOCK + HEAD : (head + 1) * BLOCK, :]
    stores_late = [pltpu.make_async_copy(grad_qkv, grad_qkv_out, store_sem.at[6, 0])]
    if table:
        grad_bias_out[...] = table_sum(table, grad_bias, here.block)
    else:
        stores_late.append(pltpu.make_async_copy(grad_bias, grad_bias_out, store_sem.at[7, 0]))
    for store in stores_late:
        store.start()
    half = grad_output.shape[4]
    for at in range(parts):
        for expert in range(experts):
            first = (at * experts + expert) * tall
            for turn in range(2):
                piece = output_sum[first : first + tall, turn * half : (turn + 1) * half]
                grad_output[turn, at, expert] = piece.astype(bf16)
    for copy in second():
        copy.wait_recv()
    for far in range(fars):
        add(own_in.at[2 * far + 1 - level], second_in.at[far])
        add(grad_out.at[2 * (1 - side) + here.core, 2 * far + level], second_out.at[far])
    for copy in stores((1, 3)):
        copy.start()
    value = x[...]
    scale = root_scale(value)
    unit = value * scale
    for flip in (1, 2, 3):
        hand_normed(flip).wait_recv()
        normed_grad = normed_grad + normed_recv[flip - 1].astype(f32)
    grad_rows[5:6, :] = jnp.sum(normed_grad * unit, axis=0, keepdims=True)
    scaled = normed_grad * gain_attn[layer : layer + 1, :]
    grad_next[...] = mid_grad + scale * (scaled - unit * jnp.mean(unit * scaled, axis=-1, keepdims=True))
    if earlier:
        earlier.finish()
    if last:
        swap.wait((0,))
        swap.drain()
    for copy in stores(range(6)) + stores_late:
        copy.wait()
    for copy in to_core() + second():
        copy.wait_send()
    for flip in (1, 2, 3):
        gather(flip, block).wait_send()
        hand_normed(flip).wait_send()
    for step in range(1, parts):
        hand_pair(step, 0).wait_send()
    for step in range(1, experts):
        for half in range(2):
            hand_slots(half, step, here.expert).wait_send()
            hand_answer(half, step, here.expert).wait_send()


VMEM = pl.BlockSpec(memory_space=pltpu.VMEM)
ANY = pl.BlockSpec(memory_space=pl.ANY)
DMA = pltpu.SemaphoreType.DMA


def forward_layer(layer, layers, begin, going, weights):
    parts, experts = lax.axis_size("context"), lax.axis_size("expert")
    w_in = weights[7]
    width, hidden = w_in.shape[2:]
    count = BLOCK
    wide, packed = 3 * HEAD, 5 * BLOCK
    room = count * 5 // (4 * experts)
    cut = room // 32 * 16
    shape, scratch = jax.ShapeDtypeStruct, pltpu.VMEM
    first = begin is not None
    gives = Saved(
        x=shape((count, width), f32),
        grad=shape((count, width), bf16),
        marks=shape((8, count), jnp.int32),
        bias=shape((3, 5, BLOCK, BLOCK), f32),
        select=shape((experts, room, count), bf16),
        chosen=shape((count, BLOCK), f32),
        w_qkv=shape((width, packed), bf16),
        turned=shape((width, GROUP * count), bf16),
        query=shape((GROUP, count, 3 * BLOCK), bf16),
        pair=shape((parts, GROUP, count, 2 * wide), bf16),
        merged=shape((GROUP, count, 3 * BLOCK), f32),
        log_total=shape((GROUP, count, BLOCK), f32),
        middle=shape((count, width), f32),
        router=shape((count, BLOCK), f32),
        picked=shape((count, width), bf16),
        arrived=shape((experts, cut, width), bf16),
        arrived_more=shape((experts, room - cut, width), bf16),
        before=shape((experts * room, hidden), f32),
        x_next=shape((count, width), f32),
    )
    far = Saved(*[VMEM] * len(gives))._replace(
        w_qkv=ANY, turned=ANY, query=ANY, pair=ANY, merged=ANY, log_total=ANY, before=ANY
    )
    skipped = 0 if first else 4
    start = list(begin) if first else [going.x_next, going.marks, going.bias]
    start_specs = [VMEM] * 3 + [pl.BlockSpec(memory_space=pltpu.SMEM)] if first else [VMEM] * 3
    made = pl.pallas_call(
        functools.partial(forward_kernel, layer, layers, parts, experts, first),
        out_shape=list(gives[skipped:]),
        in_specs=start_specs + [VMEM] * 3 + [ANY] * 6,
        out_specs=list(far[skipped:]),
        scratch_shapes=[
            scratch((width, packed), bf16),
            scratch((width, GROUP * count), bf16),
            scratch((GROUP, count, 3 * BLOCK), bf16),
            scratch((parts, GROUP, count, 2 * wide), bf16),
            scratch((GROUP, count, 3 * BLOCK), f32),
            scratch((GROUP, count, BLOCK), f32),
            scratch((GROUP, count, wide), bf16),
            scratch((experts * room, hidden), f32),
            scratch((GROUP, count, width), bf16),
            scratch((width, 6 * BLOCK), bf16),
            scratch((width, width), bf16),
            scratch((width, hidden), bf16),
            scratch((hidden, width), bf16),
            scratch((parts * GROUP, count, BLOCK), f32),
            scratch((GROUP, count, wide), bf16),
            scratch((experts, cut, width), bf16),
            scratch((experts, room - cut, width), bf16),
            scratch((experts * room, width), f32),
            *[scratch((experts, cut, width), bf16), scratch((experts, room - cut, width), bf16)] * 2,
            DMA((6,)),
            DMA((7,)),
            DMA((3,)),
            DMA((3,)),
            DMA((parts - 1, GROUP)),
            DMA((parts - 1, GROUP)),
            DMA((3,)),
            DMA((3,)),
            DMA((2, experts - 1)),
            DMA((2, experts - 1)),
            DMA((2, experts - 1)),
            DMA((2, experts - 1)),
        ]
        + ([scratch((count, width), bf16), DMA((3,)), DMA((3,))] if first else []),
        compiler_params=pltpu.CompilerParams(
            collective_id=layer, has_side_effects=True, vmem_limit_bytes=60 * 2**20
        ),
        name="layer_forward",
    )(*start, *weights)
    return Saved(*([] if first else [going.x_next, going.grad, going.marks, going.bias]), *made)


def backward_layer(layer, layers, grad, saved, bias_before, left, weights, x_last, table):
    gain_attn, gain_moe, w_router, _, _, _, w_output, w_in, w_out = weights
    w_qkv, select, bias = saved.w_qkv, saved.select, saved.bias
    count, width = grad.shape
    parts, experts = lax.axis_size("context"), lax.axis_size("expert")
    wide = 3 * HEAD
    room = select.shape[1]
    hidden = w_in.shape[3]
    shape = jax.ShapeDtypeStruct
    scratch = pltpu.VMEM
    span = GROUP * count
    rows_in, rows_out = width // (GROUP * parts), hidden // (GROUP * parts)
    tall = rows_in // experts
    fars = parts // 2
    specs, gives, given_specs, needs = earlier_call(parts, experts, left, None) if left else ([], [], [], [])
    taken = present(taken_from(left, None)) if left else []
    gives = present(gives)
    cut = saved.arrived.shape[1]
    own_gives = Own(
        grad_next=shape((count, width), f32),
        in_across=shape((fars, rows_in, hidden), bf16),
        in_beside=shape((fars, rows_in, hidden), bf16),
        in_own=shape((fars, rows_in, hidden), bf16),
        out_across=shape((fars, rows_out, width), bf16),
        out_beside=shape((fars, rows_out, width), bf16),
        out_own=shape((fars, rows_out, width), bf16),
        qkv=shape((GROUP, parts, experts, tall, w_qkv.shape[1]), bf16),
        output=shape((2, parts, experts, tall, width // 2), bf16),
        bias=shape((table, 128) if table else bias.shape, f32),
        rows=shape((8, width), f32),
    )
    own_specs = [VMEM] + [ANY] * 7 + [VMEM, VMEM if table else ANY, VMEM]
    last = int(x_last is not None)
    counts = (24, len(taken), len(own_gives), len(gives), len(needs), last)
    given = pl.pallas_call(
        functools.partial(backward_and_earlier, layer, parts, experts, counts, bias_before is not None, table),
        out_shape=[*own_gives, *gives] + [shape(grad.shape, bf16)] * last,
        in_specs=[VMEM] * 7 + [ANY] * 7 + [VMEM] * 5 + [ANY] * 5 + specs + [VMEM] * last,
        out_specs=own_specs + given_specs + [VMEM] * last,
        scratch_shapes=[
            scratch(bias.shape, f32),
            scratch(saved.turned.shape, bf16),
            scratch(saved.query.shape, bf16),
            scratch(saved.pair.shape, bf16),
            scratch(saved.merged.shape, f32),
            scratch(saved.log_total.shape, f32),
            scratch((GROUP, parts, experts, tall, w_qkv.shape[1]), bf16),
            scratch(bias.shape, f32),
            scratch((GROUP, parts, rows_in, hidden), bf16),
            scratch((GROUP, parts, rows_out, width), bf16),
            scratch((2, parts, rows_in, hidden), bf16),
            scratch((2, parts, rows_out, width), bf16),
            scratch((fars, rows_in, hidden), bf16),
            scratch((fars, rows_out, width), bf16),
            scratch((wide, width), f32),
            scratch((width, w_qkv.shape[1]), bf16),
            scratch((3 * BLOCK, width), bf16),
            *[scratch((experts, cut, width), bf16), scratch((experts, room - cut, width), bf16)] * 4,
            scratch((experts * room, width), bf16),
            scratch((GROUP, count, width), bf16),
            scratch((GROUP, count, 3 * BLOCK), bf16),
            scratch((parts - 1, 2 * wide, span), bf16),
            scratch((parts - 1, 2 * wide, span), bf16),
            scratch((GROUP, count, w_qkv.shape[1]), bf16),
            scratch((GROUP - 1, count, width), bf16),
            scratch((GROUP - 1, count, width), bf16),
            DMA((14,)),
            DMA((2, experts - 1)),
            DMA((2, experts - 1)),
            DMA((2, experts - 1)),
            DMA((2, experts - 1)),
            DMA((3,)),
            DMA((3,)),
            DMA((parts - 1,)),
            DMA((parts - 1,)),
            DMA((3,)),
            DMA((3,)),
            DMA((2, 2)),
            DMA((2, 2)),
            DMA((2, fars)),
            DMA((2, fars)),
            DMA((8, fars)),
            *needs,
            *([scratch(grad.shape, bf16), DMA((1,)), DMA((1,))] if last else []),
        ],
        compiler_params=pltpu.CompilerParams(
            collective_id=layers + layer,
            has_side_effects=True,
            vmem_limit_bytes=(60 if parts <= 2 else 63) * 2**20,
        ),
        name="layer_backward",
    )(
        grad,
        saved.x,
        gain_attn,
        gain_moe,
        w_router,
        select,
        saved.chosen,
        bias,
        bias if bias_before is None else bias_before,
        saved.turned,
        saved.query,
        saved.pair,
        saved.merged,
        saved.log_total,
        saved.middle,
        saved.router,
        saved.picked,
        saved.arrived,
        saved.arrived_more,
        saved.before,
        w_qkv,
        w_output,
        w_in,
        w_out,
        *taken,
        *([x_last] if last else []),
    )
    own, sums = given[: len(own_gives)], given[len(own_gives) : len(own_gives) + len(gives)]
    return Own(*own), Given(*sums) if sums else None, given[-1]


def on_device(
    tokens,
    w_query,
    w_key,
    w_value,
    w_output,
    rel_bias,
    gain_attn,
    gain_moe,
    w_router,
    w_in,
    w_out,
    routes,
    kept,
    cotangent,
):
    experts = w_router.shape[2]
    layers = w_query.shape[0]
    parts = lax.axis_size("context")
    marks = jnp.concatenate([routes[:, 0, :, 0], kept[:, 0]])
    marks = jnp.pad(marks, ((0, -2 * layers % 8), (0, 0)))
    router_wide = jnp.pad(w_router, ((0, 0), (0, 0), (0, 128 - experts)))
    weights = (gain_attn, gain_moe, router_wide, w_key, w_value, w_query, w_output, w_in, w_out)
    saved, going = [], None
    for layer in range(layers):
        begin = (tokens[0], cotangent[0], marks, rel_bias) if layer == 0 else None
        going = forward_layer(layer, layers, begin, going, weights)
        saved.append(going)
    grad, bias_grad = saved[0].grad, None
    left, lefts, sums = None, [], []
    for layer in reversed(range(layers)):
        x_last = going.x_next if layer == layers - 1 else None
        carried = left if parts == 2 else None
        own, done, swapped = backward_layer(layer, layers, grad, saved[layer], bias_grad, carried, weights, x_last, None if layer else rel_bias.shape[0])
        if x_last is not None:
            out = swapped[None]
        if done:
            sums.insert(0, done)
        grad, bias_grad = own.grad_next, own.bias
        left = own
        lefts.insert(0, left)
        if layer == 0:
            done, d_tokens = finish(left, rel_bias.shape[0], 2 * layers, grad)
            sums.insert(0, done)
        elif parts > 2:
            sums.insert(0, finish(left, None, 2 * layers + layer)[0])

    def experts_sum(own, from_across, from_beside):
        total = own.astype(f32) + from_across.astype(f32) + from_beside.astype(f32)
        if parts == 2:
            return total[0]
        groups = [[2 * far + level for far in range(parts // 2)] for level in range(2)]
        total = lax.psum_scatter(total.astype(bf16), "context", scatter_dimension=0, axis_index_groups=groups)
        return total.astype(f32)

    grad_in = jnp.stack(
        [experts_sum(a.in_own, b.in_from_across, b.in_from_beside) for a, b in zip(lefts, sums)]
    )
    grad_out = jnp.stack(
        [experts_sum(a.out_own, b.out_from_across, b.out_from_beside) for a, b in zip(lefts, sums)]
    )
    rank = (lax.axis_index("dp") * parts + lax.axis_index("context")) * experts + lax.axis_index("expert")
    tall = sums[0].sums.shape[1]
    rows = jnp.stack([item.rows_sum for item in sums])
    rows = lax.dynamic_slice_in_dim(rows, rank * tall, tall, 2)
    key_out, value_out, query_out, output_out = (
        jnp.stack([item.sums[kind] for item in sums]) for kind in range(4)
    )
    return (
        out,
        d_tokens[None],
        query_out,
        key_out,
        value_out,
        output_out,
        sums[0].table_out[:, : rel_bias.shape[1]],
        rows[:, 5],
        rows[:, 4],
        jnp.swapaxes(rows[:, :experts], 1, 2),
        grad_in[:, None],
        grad_out[:, None],
    )


def solution(mesh):
    in_specs = (
        P("dp", ("context", "expert"), None),
        P(),
        P(),
        P(),
        P(),
        P(),
        P(),
        P(),
        P(),
        P(None, "expert", None, None),
        P(None, "expert", None, None),
        P(None, "dp", ("context", "expert"), None),
        P(None, "dp", ("context", "expert")),
        P("dp", ("context", "expert"), None),
    )
    out_specs = (
        P("dp", ("context", "expert"), None),
        P("dp", ("context", "expert"), None),
        P(None, ("dp", "context", "expert"), None),
        P(None, ("dp", "context", "expert"), None),
        P(None, ("dp", "context", "expert"), None),
        P(None, ("dp", "context", "expert"), None),
        P(),
        P(None, ("dp", "context", "expert")),
        P(None, ("dp", "context", "expert")),
        P(None, ("dp", "context", "expert"), None),
        P(None, "expert", ("dp", "context"), None),
        P(None, "expert", ("dp", "context"), None),
    )
    return jax.shard_map(
        on_device, mesh=mesh, in_specs=in_specs, out_specs=out_specs, check_vma=False
    )
```

```python
import functools
from typing import Any, NamedTuple

import jax
import jax.numpy as jnp
import numpy as np
from jax import lax
from jax.experimental import pallas as pl
from jax.experimental.pallas import tpu as pltpu
from jax.sharding import PartitionSpec as P

highest = lax.Precision.HIGHEST
epsilon = 1e-06
thresholds = (12, 16, 23, 32, 46, 64, 91)
MESH = pl.DeviceIdType.MESH
GROUP = 4
HEAD = 64
BLOCK = 128
FCHUNK = 512
f32, bf16 = jnp.float32, jnp.bfloat16


def div(a, b):
    return lax.div(a, jnp.int32(b))


def rem(a, b):
    return lax.rem(a, jnp.int32(b))


def turned_pair(index):
    return 2 * rem(index, 2) + div(index, 2)


class Place:
    def __init__(self, parts, experts):
        self.parts, self.experts = parts, experts
        self.dp = lax.axis_index("dp")
        self.context = lax.axis_index("context")
        self.expert = lax.axis_index("expert")
        self.core = rem(self.dp, 2)
        self.far = div(self.context, 2)
        self.block = 2 * rem(self.context, 2) + div(self.dp, 2)
        self.part = 2 * self.far + self.core

    def flipped(self, flip):
        low = rem(rem(self.block, 2) + flip % 2, 2)
        high = rem(div(self.block, 2) + flip // 2, 2)
        return 2 * high + low

    def group_device(self, block):
        return {"dp": 2 * rem(block, 2) + self.core, "context": 2 * self.far + div(block, 2)}

    def part_other(self, step):
        return rem(self.part + step, self.parts)

    def part_device(self, part):
        return {
            "dp": self.dp - self.core + rem(part, 2),
            "context": 2 * div(part, 2) + rem(self.context, 2),
        }

    def expert_other(self, step):
        return rem(self.expert + step, self.experts)

    def offset(self, part, block, query_block):
        across = 4 * (block // 2 - div(query_block, 2)) + (block % 2 - rem(query_block, 2))
        return 8 * (part // 2 - self.far) + across + 2 * (part % 2 - self.core)

    def bias_index(self, part, block, query_block):
        offset = self.offset(part, block, query_block)
        return jnp.minimum(jnp.maximum(offset, -2), 2) + 2

    def core_device(self):
        return {"dp": self.dp + 1 - 2 * self.core}

    def plane_others(self):
        made = []
        for step in range(self.parts // 2):
            far = rem(self.far + step, self.parts // 2)
            for flip in range(GROUP):
                if step or flip:
                    other = self.flipped(flip)
                    device = {"dp": 2 * rem(other, 2) + self.core, "context": 2 * far + div(other, 2)}
                    made.append((step, flip, far, other, device))
        return made

    def is_swapped(self):
        return self.dp != turned_pair(self.expert)

    def swap_device(self):
        return {"dp": turned_pair(self.expert), "expert": turned_pair(self.dp)}

    def greet(self, plane=False, swap=False):
        if plane:
            partners = [item[-1] for item in self.plane_others()]
            partners += [{**device, "dp": device.get("dp") + 1 - 2 * self.core} for device in partners]
            partners += [self.core_device()]
        else:
            partners = [self.group_device(self.flipped(flip)) for flip in (1, 2, 3)]
            partners += [self.part_device(self.part_other(step)) for step in range(1, self.parts)]
        partners += [{"expert": self.expert_other(step)} for step in range(1, self.experts)]
        barrier = pltpu.get_barrier_semaphore()
        for partner in partners:
            pl.semaphore_signal(barrier, inc=1, device_id=partner, device_id_type=MESH)
        if swap:

            @pl.when(self.is_swapped())
            def _():
                pl.semaphore_signal(barrier, inc=1, device_id=self.swap_device(), device_id_type=MESH)
                pl.semaphore_wait(barrier, len(partners) + 1)

            @pl.when(jnp.logical_not(self.is_swapped()))
            def _():
                pl.semaphore_wait(barrier, len(partners))

        else:
            pl.semaphore_wait(barrier, len(partners))


def remote(source, target, send, receive, device):
    return pltpu.make_async_remote_copy(
        src_ref=source,
        dst_ref=target,
        send_sem=send,
        recv_sem=receive,
        device_id=device,
        device_id_type=MESH,
    )


def dot(a, b):
    return jnp.dot(a, b, preferred_element_type=f32)


def dot_nt(a, b):
    return lax.dot_general(a, b, (((1,), (1,)), ((), ())), preferred_element_type=f32)


def dot_tn(a, b):
    return lax.dot_general(a, b, (((0,), (0,)), ((), ())), preferred_element_type=f32)


def root_scale(value):
    return lax.rsqrt(jnp.mean(value * value, axis=-1, keepdims=True) + epsilon)


def lanes(rows, width):
    return lax.broadcasted_iota(jnp.int32, (rows, width), 1)


def gelu_parts(value):
    scale = 0.7978845608028654
    square = value * value
    inner = jnp.tanh(scale * (value + 0.044715 * (square * value)))
    half = 0.5 * (1.0 + inner)
    slope = half + 0.5 * value * (1.0 - inner * inner) * (scale * (1.0 + 3 * 0.044715 * square))
    return value * half, slope


def gelu(value):
    scale = 0.7978845608028654
    return value * (0.5 * (1.0 + jnp.tanh(scale * (value + 0.044715 * (value * value * value)))))


class Swap:
    def __init__(self, here, pairs, send, recv):
        self.here, self.pairs, self.send, self.recv = here, pairs, send, recv

    def copies(self, which):
        made = []
        for index in which:
            source, target = self.pairs[index]
            made.append(remote(source, target, self.send.at[index], self.recv.at[index], self.here.swap_device()))
        return made

    def start(self, which):
        @pl.when(self.here.is_swapped())
        def _():
            for copy in self.copies(which):
                copy.start()

        @pl.when(jnp.logical_not(self.here.is_swapped()))
        def _():
            for index in which:
                source, target = self.pairs[index]
                target[...] = source[...]

    def wait(self, which):
        @pl.when(self.here.is_swapped())
        def _():
            for copy in self.copies(which):
                copy.wait_recv()

    def drain(self):
        @pl.when(self.here.is_swapped())
        def _():
            for copy in self.copies(range(len(self.pairs))):
                copy.wait_send()


def route_tokens(marks, layer, layers, select, chosen):
    experts, room, count = select.shape
    route = marks[layer : layer + 1, :]
    live = marks[layers + layer : layers + layer + 1, :] > 0
    named = lax.broadcasted_iota(jnp.int32, (8, count), 0) == route
    before = lax.broadcasted_iota(jnp.int32, (count, count), 0)
    after = lax.broadcasted_iota(jnp.int32, (count, count), 1)
    named = named.astype(f32)
    ahead = dot(named.astype(bf16), (before < after).astype(f32).astype(bf16))
    rank = jnp.sum(named * ahead, axis=0, keepdims=True)
    slot = lax.broadcasted_iota(jnp.int32, (room, count), 0).astype(f32)
    for expert in range(experts):
        select[expert] = ((slot == rank) & (route == expert) & live).astype(f32).astype(bf16)
    chosen[...] = ((before == route) & live).astype(f32).T


def bucket_block(place, half):
    row = lax.broadcasted_iota(jnp.int32, (BLOCK, BLOCK), 0)
    column = lax.broadcasted_iota(jnp.int32, (BLOCK, BLOCK), 1)
    offset = (place - 2) * BLOCK + column - row
    distance = jnp.abs(offset)
    beyond = 8 + sum((distance >= limit).astype(jnp.int32) for limit in thresholds)
    return jnp.where(distance < 8, distance, beyond) + jnp.where(offset > 0, half, 0)


def bucket_range(place, half):
    return (half, 2 * half) if place == 3 else (0, half if place == 1 else 2 * half)


def make_bias(bias, rel_bias, first):
    half = rel_bias.shape[0] // 2
    for head in range(3):
        bias[head, 0] = jnp.full((BLOCK, BLOCK), rel_bias[half - 1, first + head], f32)
        bias[head, 4] = jnp.full((BLOCK, BLOCK), rel_bias[2 * half - 1, first + head], f32)
    for place in (1, 2, 3):
        buckets = bucket_block(place, half)
        for head in range(3):

            def one(bucket, made, buckets=buckets, head=head):
                return jnp.where(buckets == bucket, rel_bias[bucket, first + head], made)

            bias[head, place] = lax.fori_loop(*bucket_range(place, half), one, jnp.zeros((BLOCK, BLOCK), f32))


def pack_weights(w_qkv, slabs, block):
    wide = 3 * HEAD
    shape = (slabs.shape[1], w_qkv.shape[1])
    row = lax.broadcasted_iota(jnp.int32, shape, 0)
    column = lax.broadcasted_iota(jnp.int32, shape, 1)
    head, inside = column // BLOCK, column % BLOCK
    kind = inside // HEAD
    source = jnp.where(
        column < 2 * wide, 2 * BLOCK * kind + HEAD * head + inside % HEAD, 4 * BLOCK + column - 2 * wide
    )
    source = source + HEAD * rem(block, 2)
    move = ((row == source) & (column < 3 * wide)).astype(f32).astype(bf16)
    w_qkv[...] = dot(slabs[...], move).astype(bf16)


def ones_where(condition):
    return condition.astype(f32).astype(bf16)


def query_spread(rows, columns):
    row = lax.broadcasted_iota(jnp.int32, (rows, columns), 0)
    column = lax.broadcasted_iota(jnp.int32, (rows, columns), 1)
    return ones_where((column % BLOCK < HEAD) & (row == HEAD * (column // BLOCK) + column % BLOCK))


def half_select(rows, columns, half):
    row = lax.broadcasted_iota(jnp.int32, (rows, columns), 0)
    column = lax.broadcasted_iota(jnp.int32, (rows, columns), 1)
    return ones_where((row == BLOCK * (column // HEAD) + HEAD * half + column % HEAD) & (column < 3 * HEAD))


def forward_kernel(layer, layers, parts, experts, first, *refs):
    if first:
        tokens, cotangent, routes, kept, rel_bias, *refs = refs
    else:
        x, marks, bias, *refs = refs
    (
        gain_attn,
        gain_moe,
        w_router,
        w_key_hbm,
        w_value_hbm,
        w_query_hbm,
        w_output_hbm,
        w_in_hbm,
        w_out_hbm,
        *refs,
    ) = refs
    if first:
        x, grad, marks, bias, *refs = refs
    forward_body(
        layer,
        layers,
        parts,
        experts,
        (tokens, cotangent, routes, kept, rel_bias, grad) if first else None,
        x,
        marks,
        bias,
        gain_attn,
        gain_moe,
        w_router,
        w_key_hbm,
        w_value_hbm,
        w_query_hbm,
        w_output_hbm,
        w_in_hbm,
        w_out_hbm,
        *refs,
    )


def widened(w_router, layer):
    rows = w_router[layer]
    return jnp.concatenate([rows, jnp.zeros((BLOCK - rows.shape[0], rows.shape[1]), f32)], axis=0)


def gathering(here, blocks, send, recv, straight):
    half = blocks.shape[1] // 2

    def gather(flip, source):
        device = here.group_device(here.flipped(flip))
        return remote(blocks.at[source], blocks.at[source], send.at[flip - 1], recv.at[flip - 1], device)

    def relay(flip, source):
        rows = blocks.at[source, (flip - 1) * half : flip * half]
        device = here.group_device(here.flipped(3 if straight else 3 - flip))
        return remote(rows, rows, send.at[flip + 1], recv.at[flip + 1], device)

    return gather, relay


def halves(arrays):
    first = arrays[0].shape[1]
    return (0, first), (first, first + arrays[1].shape[1])


def joined(slots):
    return jnp.concatenate([slots[index].astype(f32) for index in range(slots.shape[0])], axis=0).astype(bf16)


def forward_body(
    layer,
    layers,
    parts,
    experts,
    begin,
    x,
    marks,
    bias,
    gain_attn,
    gain_moe,
    w_router,
    w_key_hbm,
    w_value_hbm,
    w_query_hbm,
    w_output_hbm,
    w_in_hbm,
    w_out_hbm,
    select,
    chosen,
    w_qkv_out,
    turned_out,
    query_out,
    pair_out,
    merged_out,
    log_total_out,
    middle,
    router,
    picked,
    arrived,
    arrived_more,
    before_out,
    x_next,
    w_qkv,
    turned,
    query,
    pair,
    merged,
    log_total,
    merged_low,
    before,
    normed,
    slabs,
    w_output,
    w_in,
    w_out,
    scores,
    merged_mine,
    slots,
    slots_more,
    total,
    answer,
    answer_more,
    returned,
    returned_more,
    load_sem,
    store_sem,
    group_send,
    group_recv,
    part_send,
    part_recv,
    merge_send,
    merge_recv,
    slot_send,
    slot_recv,
    back_send,
    back_recv,
    tokens_came=None,
    marks_here=None,
    swap_send=None,
    swap_recv=None,
):
    here = Place(parts, experts)
    heads = 3
    wide = heads * HEAD
    block = here.block
    if begin:
        tokens, cotangent, routes, kept, rel_bias, grad = begin
        marks_here[...] = jnp.zeros_like(marks_here)
        marks_here[:layers, :] = routes[...]
        marks_here[layers : 2 * layers, :] = kept[...]
        here.greet(swap=True)
        pairs = [(marks_here, marks), (tokens, tokens_came), (cotangent, grad)]
        swap = Swap(here, pairs, swap_send, swap_recv)
        swap.start((0, 1))
    stores = [
        pltpu.make_async_copy(source, target, store_sem.at[index])
        for index, (source, target) in enumerate(
            (
                (w_qkv, w_qkv_out),
                (turned, turned_out),
                (query, query_out),
                (pair, pair_out),
                (merged, merged_out),
                (log_total, log_total_out),
                (before, before_out),
            )
        )
    ]
    slab = pl.ds(pl.multiple_of(BLOCK * div(3 * block, 2), BLOCK), 2 * BLOCK)
    loads = []
    for kind, source in enumerate((w_key_hbm, w_value_hbm, w_query_hbm)):
        target = slabs.at[:, kind * 2 * BLOCK : (kind + 1) * 2 * BLOCK]
        loads.append(pltpu.make_async_copy(source.at[layer, :, slab], target, load_sem.at[kind]))
    loads += [
        pltpu.make_async_copy(w_output_hbm.at[layer], w_output, load_sem.at[3]),
        pltpu.make_async_copy(w_in_hbm.at[layer, 0], w_in, load_sem.at[4]),
        pltpu.make_async_copy(w_out_hbm.at[layer, 0], w_out, load_sem.at[5]),
    ]
    for load in loads:
        load.start()
    if begin:
        for load in loads[:3]:
            load.wait()
        pack_weights(w_qkv, slabs, block)
        swap.wait((0, 1))
        value = tokens_came[...].astype(f32)
        x[...] = value
    else:
        value = x[...]
    normed[block] = (value * root_scale(value) * gain_attn[layer : layer + 1, :]).astype(bf16)
    if not begin:
        here.greet()

    gather, relay = gathering(here, normed, group_send, group_recv, True)
    for flip in (1, 2):
        gather(flip, block).start()
    for flip in (1, 2):
        relay(flip, block).start()

    def hand_pair(step, part, of_block):
        return remote(
            pair.at[part, of_block],
            pair.at[part, of_block],
            part_send.at[step - 1, of_block],
            part_recv.at[step - 1, of_block],
            here.part_device(here.part_other(step)),
        )

    def project(of_block):
        made = dot(normed[of_block], w_qkv[...]).astype(bf16)
        pair[here.part, of_block] = made[:, : 2 * wide]
        query[of_block] = dot(made[:, 2 * wide :], query_spread(2 * BLOCK, 3 * BLOCK)).astype(bf16)
        for step in range(1, parts):
            hand_pair(step, here.part, of_block).start()
        columns = pl.ds(pl.multiple_of(of_block * BLOCK, BLOCK), BLOCK)
        turned[:, columns] = normed[of_block].astype(f32).T.astype(bf16)

    if begin:
        swap.start((2,))
    else:
        for load in loads[:3]:
            load.wait()
        pack_weights(w_qkv, slabs, block)
    project(block)
    route_tokens(marks, layer, layers, select, chosen)
    if begin:
        make_bias(bias, rel_bias, heads * block)
    for flip in (1, 2):
        gather(flip, here.flipped(flip)).wait_recv()
        project(here.flipped(flip))
    for flip in (1, 2):
        relay(flip, here.flipped(3)).wait_recv()
    project(here.flipped(3))
    for step in range(1, parts):
        source = rem(here.part + parts - step, parts)
        for of_block in range(GROUP):
            hand_pair(step, source, of_block).wait_recv()

    for store in stores[:4]:
        store.start()
    lane_log = lanes(BLOCK, BLOCK)

    def hand_merged(flip, source):
        return remote(
            merged_mine.at[here.flipped(flip)],
            merged_low.at[source],
            merge_send.at[flip - 1],
            merge_recv.at[flip - 1],
            here.group_device(here.flipped(flip)),
        )

    for flip in (3, 1, 2, 0):
        mine = here.flipped(flip)
        logs = jnp.zeros((BLOCK, BLOCK), f32)
        for head in range(heads):
            columns = slice(head * BLOCK, (head + 1) * BLOCK)
            top = jnp.full((BLOCK, 1), -1e30, f32)
            for part in range(parts):
                both = pair[part, :, :, columns].reshape(GROUP * BLOCK, BLOCK)
                raw = dot_nt(query[mine, :, columns], both)
                for of_block in range(GROUP):
                    piece = (
                        raw[:, of_block * BLOCK : (of_block + 1) * BLOCK]
                        + bias[head, here.bias_index(part, of_block, mine)]
                    )
                    scores[part * GROUP + of_block] = piece
                    top = jnp.maximum(top, jnp.max(piece, axis=-1, keepdims=True))
            summed = jnp.zeros((BLOCK, 1), f32)
            out = jnp.zeros((BLOCK, BLOCK), f32)
            for part in range(parts):
                pieces = []
                for of_block in range(GROUP):
                    weight = jnp.exp(scores[part * GROUP + of_block] - top)
                    summed = summed + jnp.sum(weight, axis=-1, keepdims=True)
                    pieces.append(weight.astype(bf16))
                both = pair[part, :, :, columns].reshape(GROUP * BLOCK, BLOCK)
                out = out + dot(jnp.concatenate(pieces, axis=1), both)
            merged[mine, :, columns] = jnp.where(lane_log >= HEAD, out / summed, 0.0)
            logs = jnp.where(lane_log == head, top + jnp.log(summed), logs)
        final = dot(merged[mine].astype(bf16), half_select(3 * BLOCK, wide, 1))
        log_total[mine] = logs
        if flip:
            merged_mine[mine] = final.astype(bf16)
            hand_merged(flip, block).start()
        else:
            merged_low[block] = final.astype(bf16)

    for store in stores[4:6]:
        store.start()
    for flip in (1, 2, 3):
        hand_merged(flip, here.flipped(flip)).wait_recv()
    loads[3].wait()
    mid = value
    for of_block in range(GROUP):
        mid = mid + dot(merged_low[of_block], w_output[of_block * wide : (of_block + 1) * wide, :])
    middle[...] = mid
    moe_in = mid * root_scale(mid) * gain_moe[layer : layer + 1, :]
    moe_low = moe_in.astype(bf16)

    slots, arrived = (slots, slots_more), (arrived, arrived_more)
    answer, returned = (answer, answer_more), (returned, returned_more)
    spans = halves(arrived)

    def hand_slots(half, step, source):
        return remote(
            slots[half].at[here.expert_other(step)],
            arrived[half].at[source],
            slot_send.at[half, step - 1],
            slot_recv.at[half, step - 1],
            {"expert": here.expert_other(step)},
        )

    for half, (low, high) in enumerate(spans):
        for expert in range(experts):
            slots[half][expert] = dot(select[expert, low:high], moe_low).astype(bf16)
        for step in range(1, experts):
            hand_slots(half, step, here.expert).start()
        arrived[half][here.expert] = slots[half][here.expert]
    logits = lax.dot_general(
        moe_in, widened(w_router, layer), (((1,), (1,)), ((), ())), precision=highest, preferred_element_type=f32
    )
    logits = jnp.where(lane_log < experts, logits, -1e30)
    raised = jnp.exp(logits - jnp.max(logits, axis=-1, keepdims=True))
    chances = raised / jnp.sum(raised, axis=-1, keepdims=True)
    router[...] = chances
    gate = jnp.sum(chances * chosen[...], axis=-1, keepdims=True)
    total[...] = jnp.zeros_like(total)
    loads[4].wait()
    loads[5].wait()

    def hand_answer(half, step, source):
        return remote(
            answer[half].at[here.expert_other(step)],
            returned[half].at[source],
            back_send.at[half, step - 1],
            back_recv.at[half, step - 1],
            {"expert": here.expert_other(step)},
        )

    for half, (low, high) in enumerate(spans):
        for step in range(1, experts):
            hand_slots(half, step, rem(here.expert + experts - step, experts)).wait_recv()
        given = joined(arrived[half])
        rows = slice(experts * low, experts * high)

        @pl.loop(0, w_in.shape[1] // FCHUNK)
        def _(index, given=given, rows=rows):
            columns = pl.ds(pl.multiple_of(index * FCHUNK, FCHUNK), FCHUNK)
            first = dot(given, w_in[:, columns])
            before[rows, columns] = first
            total[rows, :] += dot(gelu(first).astype(bf16), w_out[columns, :])

        for expert in range(experts):
            first = experts * low + expert * (high - low)
            answer[half][expert] = total[first : first + high - low, :].astype(bf16)
        for step in range(1, experts):
            hand_answer(half, step, here.expert).start()
        returned[half][here.expert] = answer[half][here.expert]
    stores[6].start()
    back = jnp.zeros_like(value)
    for half, (low, high) in enumerate(spans):
        for step in range(1, experts):
            hand_answer(half, step, rem(here.expert + experts - step, experts)).wait_recv()
        for expert in range(experts):
            back = back + dot_tn(select[expert, low:high], returned[half][expert])
    picked[...] = back.astype(bf16)
    x_next[...] = mid + gate * back
    for store in stores:
        store.wait()
    if begin:
        swap.wait((2,))
        swap.drain()
    for flip in (1, 2):
        gather(flip, block).wait_send()
        relay(flip, here.flipped(flip)).wait_send()
    for flip in (1, 2, 3):
        hand_merged(flip, block).wait_send()
    for step in range(1, parts):
        for of_block in range(GROUP):
            hand_pair(step, here.part, of_block).wait_send()
    for step in range(1, experts):
        for half in range(2):
            hand_slots(half, step, here.expert).wait_send()
            hand_answer(half, step, here.expert).wait_send()


def table_sum(table, grads, block):
    marks = lanes(table, 128)
    row = lax.broadcasted_iota(jnp.int32, marks.shape, 0)
    half = table // 2
    total = jnp.zeros(marks.shape, f32)
    for head in range(3):
        made = jnp.zeros(marks.shape, f32)
        for place, bucket in ((0, half - 1), (4, 2 * half - 1)):
            line = jnp.sum(grads[head, place], axis=0, keepdims=True)
            made = made + jnp.where(row == bucket, line, 0.0)
        for place in (1, 2, 3):
            buckets = bucket_block(place, half)

            def one(bucket, made, buckets=buckets, place=place, head=head):
                found = jnp.where(buckets == bucket, grads[head, place], 0.0)
                return made + jnp.where(row == bucket, jnp.sum(found, axis=0, keepdims=True), 0.0)

            made = lax.fori_loop(*bucket_range(place, half), one, made)
        column = jnp.sum(made, axis=-1, keepdims=True)
        total = total + jnp.where(marks == 3 * block + head, column, 0.0)
    return total


class Saved(NamedTuple):
    x: Any
    grad: Any
    marks: Any
    bias: Any
    select: Any
    chosen: Any
    w_qkv: Any
    turned: Any
    query: Any
    pair: Any
    merged: Any
    log_total: Any
    middle: Any
    router: Any
    picked: Any
    arrived: Any
    arrived_more: Any
    before: Any
    x_next: Any


class Own(NamedTuple):
    grad_next: Any
    in_across: Any
    in_beside: Any
    in_own: Any
    out_across: Any
    out_beside: Any
    out_own: Any
    qkv: Any
    output: Any
    bias: Any
    rows: Any


class Taken(NamedTuple):
    in_across: Any
    in_beside: Any
    out_across: Any
    out_beside: Any
    qkv: Any
    output: Any
    rows: Any
    table_part: Any = None


class Given(NamedTuple):
    in_from_across: Any
    in_from_beside: Any
    out_from_across: Any
    out_from_beside: Any
    sums: Any
    rows_sum: Any
    table_out: Any = None


class Needed(NamedTuple):
    small: Any
    qkv_core: Any
    output_core: Any
    small_core: Any
    qkv_line: Any
    output_line: Any
    small_line: Any
    qkv_came: Any
    output_came: Any
    small_came: Any
    qkv_plane: Any
    output_plane: Any
    small_plane: Any
    qkv_last: Any
    output_last: Any
    small_last: Any
    expert_send: Any
    expert_recv: Any
    core_send: Any
    core_recv: Any
    line_send: Any
    line_recv: Any
    plane_send: Any
    plane_recv: Any
    output_send: Any
    output_recv: Any


def present(items):
    return [item for item in items if item is not None]


def taken_from(own, table):
    return Taken(
        own.in_across,
        own.in_beside,
        own.out_across,
        own.out_beside,
        own.qkv,
        own.output,
        own.rows,
        own.bias if table else None,
    )


class Earlier:
    def __init__(self, parts, experts, table, taken, given, needed):
        self.parts, self.experts, self.table, self.fars = parts, experts, table, parts // 2
        for refs in (Taken(*taken), Given(*given), Needed(*needed)):
            self.__dict__.update(refs._asdict())

    def expert_copies(self, which=(0, 1, 2, 3)):
        here, made = self.here, []
        across, beside = here.group_device(here.flipped(1)), here.group_device(here.flipped(2))
        for kind, (source, target, device) in enumerate(
            (
                (self.in_across, self.in_from_across, across),
                (self.out_beside, self.out_from_beside, beside),
                (self.in_beside, self.in_from_beside, beside),
                (self.out_across, self.out_from_across, across),
            )
        ):
            half = source.shape[2] // 2
            for turn in range(2):
                if kind // 2 * 2 + turn in which:
                    columns = slice(turn * half, (turn + 1) * half)
                    sems = self.expert_send.at[kind, turn], self.expert_recv.at[kind, turn]
                    made.append(remote(source.at[:, :, columns], target.at[:, :, columns], *sems, device))
        return made

    def core_copies(self):
        here, made = self.here, []
        device = here.core_device()
        for at in range(2):
            sems = self.core_send.at[at], self.core_recv.at[at]
            made.append(remote(self.qkv.at[2 * at + 1 - here.core], self.qkv_core.at[at], *sems, device))
        sems = self.core_send.at[2], self.core_recv.at[2]
        made.append(remote(self.output.at[1 - here.core], self.output_core, *sems, device))
        sems = self.core_send.at[3], self.core_recv.at[3]
        made.append(remote(self.small, self.small_core, *sems, device))
        return made

    def line_copies(self, step, source):
        here = self.here
        target = here.expert_other(step)
        device = {"expert": target}
        sems = [(self.line_send.at[kind, step - 1], self.line_recv.at[kind, step - 1]) for kind in range(3)]
        return [
            remote(self.qkv_line.at[target], self.qkv_came.at[source], *sems[0], device),
            remote(self.output_line.at[target], self.output_came.at[source], *sems[1], device),
            remote(self.small_line, self.small_came.at[source], *sems[2], device),
        ]

    def plane_copies(self):
        here, made = self.here, []
        for step, flip, far, other, device in here.plane_others():
            sems = [(self.plane_send.at[kind, step, flip], self.plane_recv.at[kind, step, flip]) for kind in range(2)]
            source = self.qkv_plane.at[rem(other, 2), 2 * far + div(other, 2)]
            made.append(remote(source, self.qkv_last.at[here.block, here.far], *sems[0], device))
            made.append(remote(self.small_plane, self.small_last.at[here.block, here.far], *sems[1], device))
        return made

    def output_copy(self, context):
        here = self.here
        return remote(
            self.output_plane.at[context],
            self.output_last.at[here.core, here.far],
            self.output_send.at[context],
            self.output_recv.at[here.core, here.far],
            {"dp": here.block, "context": jnp.int32(context)},
        )

    def is_here(self, context):
        return (self.here.block == self.here.dp) & (self.here.context == context)

    def begin(self, here, which=(0, 1, 2, 3)):
        self.here = here
        for copy in self.expert_copies(which):
            copy.start()
        pieces = self.rows.shape[1] // 128
        for piece in range(pieces):
            self.small[8 * piece : 8 * piece + 8, :] = self.rows[:, piece * 128 : (piece + 1) * 128]
        for copy in self.core_copies()[:3]:
            copy.start()
        if self.table:
            self.small[8 * pieces :, :] = self.table_part[...]
        self.core_copies()[3].start()

    def pass_line(self):
        here = self.here
        for copy in self.core_copies():
            copy.wait_recv()
        for expert in range(self.experts):
            for context in range(self.parts):
                for at in range(2):
                    self.qkv_line[expert, at, context] = (
                        self.qkv[2 * at + here.core, context, expert].astype(f32)
                        + self.qkv_core[at, context, expert].astype(f32)
                    ).astype(bf16)
                self.output_line[expert, context] = (
                    self.output[here.core, context, expert].astype(f32)
                    + self.output_core[context, expert].astype(f32)
                ).astype(bf16)
        self.small_line[...] = self.small[...] + self.small_core[...]
        for step in range(1, self.experts):
            for copy in self.line_copies(step, here.expert):
                copy.start()

    def pass_plane(self, which=()):
        here = self.here
        for step in range(1, self.experts):
            for copy in self.line_copies(step, rem(here.expert + self.experts - step, self.experts)):
                copy.wait_recv()
        sources = [rem(here.expert + step, self.experts) for step in range(1, self.experts)]
        for context in range(self.parts):
            for at in range(2):
                total = self.qkv_line[here.expert, at, context].astype(f32)
                for source in sources:
                    total = total + self.qkv_came[source, at, context].astype(f32)
                self.qkv_plane[at, context] = total.astype(bf16)
            total = self.output_line[here.expert, context].astype(f32)
            for source in sources:
                total = total + self.output_came[source, context].astype(f32)
            self.output_plane[context] = total.astype(bf16)
        total = self.small_line[...]
        for source in sources:
            total = total + self.small_came[source]
        self.small_plane[...] = total
        for copy in self.plane_copies():
            copy.start()
        for context in range(self.parts):

            @pl.when(jnp.logical_not(self.is_here(context)))
            def _():
                self.output_copy(context).start()

            @pl.when(self.is_here(context))
            def _():
                self.output_last[here.core, here.far] = self.output_plane[context]

        for copy in self.expert_copies(which):
            copy.start()
        self.qkv_last[here.block, here.far] = self.qkv_plane[div(here.dp, 2), here.context]
        self.small_last[here.block, here.far] = self.small_plane[...]

    def finish(self):
        here = self.here
        for copy in self.plane_copies():
            copy.wait_recv()
        for core in range(2):
            for far in range(self.fars):
                source_dp = 2 * here.core + core
                source_context = 2 * far + div(here.dp, 2)

                @pl.when(jnp.logical_not((source_dp == here.dp) & (source_context == here.context)))
                def _():
                    remote(
                        self.output_plane.at[0],
                        self.output_last.at[core, far],
                        self.output_send.at[0],
                        self.output_recv.at[core, far],
                        here.core_device(),
                    ).wait_recv()

        wide = 3 * HEAD
        total = jnp.zeros(self.small_plane.shape, f32)
        for block in range(GROUP):
            made = jnp.zeros(self.qkv_last.shape[2:], f32)
            for far in range(self.fars):
                total = total + self.small_last[block, far]
                made = made + self.qkv_last[block, far].astype(f32)
            columns = slice(block * wide, (block + 1) * wide)
            for head in range(3):
                part = slice(block * wide + head * HEAD, block * wide + (head + 1) * HEAD)
                for kind in range(2):
                    first = head * BLOCK + kind * HEAD
                    self.sums[kind, :, part] = made[:, first : first + HEAD]
            self.sums[2, :, columns] = made[:, 2 * wide : 3 * wide]
        half = self.output_last.shape[3]
        for core in range(2):
            made = self.output_last[core, 0].astype(f32)
            for far in range(1, self.fars):
                made = made + self.output_last[core, far].astype(f32)
            self.sums[3, :, core * half : (core + 1) * half] = made
        pieces = self.rows.shape[1] // 128
        for piece in range(pieces):
            self.rows_sum[:, piece * 128 : (piece + 1) * 128] = total[8 * piece : 8 * piece + 8, :]
        if self.table:
            self.table_out[...] = total[8 * pieces :, :]
        for copy in self.expert_copies():
            copy.wait()
        for copy in self.core_copies() + self.plane_copies():
            copy.wait_send()
        for step in range(1, self.experts):
            for copy in self.line_copies(step, here.expert):
                copy.wait_send()
        for context in range(self.parts):

            @pl.when(jnp.logical_not(self.is_here(context)))
            def _():
                self.output_copy(context).wait_send()


def earlier_call(parts, experts, left, table):
    tall, packed = left.qkv.shape[3:]
    half = left.output.shape[4]
    fars = parts // 2
    small = 8 * (2 * half // 128) + (table or 0)
    shape, scratch = jax.ShapeDtypeStruct, pltpu.VMEM
    specs = [ANY] * 4 + [VMEM] * (4 if table else 3)
    gives = Given(
        shape(left.in_across.shape, bf16),
        shape(left.in_across.shape, bf16),
        shape(left.out_across.shape, bf16),
        shape(left.out_across.shape, bf16),
        shape((4, tall, 2 * half), f32),
        shape((8, 2 * half), f32),
        shape((table, 128), f32) if table else None,
    )
    needs = Needed(
        small=scratch((small, 128), f32),
        qkv_core=scratch((2, parts, experts, tall, packed), bf16),
        output_core=scratch((parts, experts, tall, half), bf16),
        small_core=scratch((small, 128), f32),
        qkv_line=scratch((experts, 2, parts, tall, packed), bf16),
        output_line=scratch((experts, parts, tall, half), bf16),
        small_line=scratch((small, 128), f32),
        qkv_came=scratch((experts, 2, parts, tall, packed), bf16),
        output_came=scratch((experts, parts, tall, half), bf16),
        small_came=scratch((experts, small, 128), f32),
        qkv_plane=scratch((2, parts, tall, packed), bf16),
        output_plane=scratch((parts, tall, half), bf16),
        small_plane=scratch((small, 128), f32),
        qkv_last=scratch((GROUP, fars, tall, packed), bf16),
        output_last=scratch((2, fars, tall, half), bf16),
        small_last=scratch((GROUP, fars, small, 128), f32),
        expert_send=DMA((4, 2)),
        expert_recv=DMA((4, 2)),
        core_send=DMA((4,)),
        core_recv=DMA((4,)),
        line_send=DMA((3, experts - 1)),
        line_recv=DMA((3, experts - 1)),
        plane_send=DMA((2, fars, GROUP)),
        plane_recv=DMA((2, fars, GROUP)),
        output_send=DMA((parts,)),
        output_recv=DMA((2, fars)),
    )
    given_specs = [ANY] * 4 + [VMEM] * (3 if table else 2)
    return specs, gives, given_specs, needs


def finish_kernel(parts, experts, table, last, others, *refs):
    here = Place(parts, experts)
    swap = None
    if last:
        grad, *refs = refs
        *refs, grad_low, grad_came, send, recv = refs
    takes = 8 if table else 7
    taken, refs = refs[:takes], refs[takes:]
    if others:
        loads_from, refs = refs[: 2 + 6 * others], refs[2 + 6 * others :]
    if last:
        d_tokens, *refs = refs
        swap = Swap(here, [(grad_low, grad_came)], send, recv)
    if others:
        sums, rows_sum, table_out, final_in, final_out, *refs = refs
        *refs, in_part, in_whole, out_whole, out_part = refs
        *refs, load_sem = refs
        refs, loads_to = refs[: -2 - 6 * others], refs[-2 - 6 * others :]
        given = [in_part, in_whole, out_whole, out_part, sums, rows_sum, table_out]
        loads = [
            pltpu.make_async_copy(source, target, load_sem.at[index])
            for index, (source, target) in enumerate(zip(loads_from, loads_to, strict=True))
        ]
        for load in loads:
            load.start()
    else:
        given, refs = refs[: takes - 1], refs[takes - 1 :]
    earlier = Earlier(parts, experts, table, taken, given, refs)
    here.greet(plane=True, swap=last)
    earlier.begin(here, (0, 1, 2))
    if last:
        grad_low[...] = grad[...].astype(bf16)
        swap.start((0,))
    earlier.pass_line()

    def total(target, own, one, other):
        made = own[0].astype(f32) + one[0].astype(f32) + other[0].astype(f32)
        target[...] = made.astype(bf16)

    if others:
        for load in loads:
            load.wait()
        for layer in range(others):
            own_in, part_in, whole_in, own_out, part_out, whole_out = loads_to[2 + 6 * layer : 8 + 6 * layer]
            total(final_in.at[1 + layer], own_in, part_in, whole_in)
            total(final_out.at[1 + layer], own_out, part_out, whole_out)
    earlier.pass_plane((3,))
    earlier.finish()
    if others:
        total(final_in.at[0], loads_to[0], in_part, in_whole)
        total(final_out.at[0], loads_to[1], out_part, out_whole)
    if last:
        swap.wait((0,))
        d_tokens[...] = grad_came[...].astype(f32)
        swap.drain()


def finish(left, table, number, grad=None, others=()):
    parts, experts = lax.axis_size("context"), lax.axis_size("expert")
    specs, gives, given_specs, needs = earlier_call(parts, experts, left, table)
    last = grad is not None
    shape, scratch = jax.ShapeDtypeStruct, pltpu.VMEM
    loaded, more_scratch, finals = [], [], []
    if others:
        loaded = [left.in_own, left.out_own]
        for own, done in others:
            loaded += [own.in_own, done.in_from_across, done.in_from_beside]
            loaded += [own.out_own, done.out_from_beside, done.out_from_across]
        more_scratch = [scratch(item.shape, bf16) for item in loaded] + [DMA((len(loaded),))]
        more_scratch += [scratch(item.shape, bf16) for item in gives[:4]]
        finals = [shape((1 + len(others),) + item.shape[1:], bf16) for item in loaded[:2]]
        gives, given_specs = gives[4:], given_specs[4:]
    given = pl.pallas_call(
        functools.partial(finish_kernel, parts, experts, table, last, len(others)),
        out_shape=([shape(grad.shape, f32)] if last else []) + present(gives) + finals,
        in_specs=[VMEM] * last + specs + [ANY] * len(loaded),
        out_specs=[VMEM] * last + given_specs + [VMEM] * len(finals),
        scratch_shapes=list(needs)
        + more_scratch
        + ([scratch(grad.shape, bf16)] * 2 + [DMA((1,)), DMA((1,))] if last else []),
        compiler_params=pltpu.CompilerParams(
            collective_id=number, has_side_effects=True, vmem_limit_bytes=60 * 2**20
        ),
        name="finish",
    )(*([grad] if last else []), *present(taken_from(left, table)), *loaded)
    if others:
        return Given(None, None, None, None, *given[1:4]), given[0], given[4:]
    return Given(*given[last:]), given[0], None


def backward_and_earlier(layer, parts, experts, counts, earlier_bias, table, *refs):
    own_in, takes, own_out, gives, needs, last = counts
    own_scratch = len(refs) - own_in - takes - own_out - gives - needs - 5 * last
    cuts = np.cumsum([0, own_in, takes, last, own_out, gives, last, own_scratch, needs, 3 * last])
    pieces = [refs[a:b] for a, b in zip(cuts[:-1], cuts[1:], strict=True)]
    earlier = Earlier(parts, experts, None, pieces[1], pieces[4], pieces[7]) if takes else None
    backward_kernel(
        layer,
        parts,
        experts,
        *pieces[0],
        *pieces[3],
        *pieces[6],
        earlier=earlier,
        earlier_bias=earlier_bias,
        table=table,
        last=pieces[2] + pieces[5] + pieces[8] if last else None,
    )


def backward_kernel(
    layer,
    parts,
    experts,
    grad,
    x,
    gain_attn,
    gain_moe,
    w_router,
    select,
    chosen,
    bias_hbm,
    bias_before,
    turned_hbm,
    query_hbm,
    pair_hbm,
    merged_hbm,
    log_total_hbm,
    middle,
    router,
    picked,
    arrived,
    arrived_more,
    before_hbm,
    w_qkv_hbm,
    w_output_hbm,
    w_in_hbm,
    w_out_hbm,
    grad_next,
    in_across,
    in_beside,
    in_own,
    out_across,
    out_beside,
    out_own,
    grad_qkv_out,
    grad_output,
    grad_bias_out,
    grad_rows,
    bias,
    turned,
    query,
    pair,
    merged,
    log_total,
    grad_qkv,
    grad_bias,
    grad_in,
    grad_out,
    core_in,
    core_out,
    second_in,
    second_out,
    output_sum,
    w_qkv,
    w_output,
    slots,
    slots_more,
    arrived_grad,
    arrived_grad_more,
    answer,
    answer_more,
    returned,
    returned_more,
    given_grad,
    branches,
    query_grad,
    pair_sent,
    pair_recv,
    made_grad,
    normed_sent,
    normed_recv,
    load_sem,
    slot_send,
    slot_recv,
    back_send,
    back_recv,
    group_send,
    group_recv,
    part_send,
    part_recv,
    merge_send,
    merge_recv,
    core_send,
    core_recv,
    second_send,
    second_recv,
    store_sem,
    earlier=None,
    earlier_bias=False,
    last=None,
    table=None,
):
    here = Place(parts, experts)
    heads = 3
    wide = heads * HEAD
    block = here.block
    fars = parts // 2
    side, level = div(here.dp, 2), rem(here.context, 2)
    across, beside = here.group_device(here.flipped(1)), here.group_device(here.flipped(2))
    own_in, own_out = grad_in.at[2 * side + here.core], grad_out.at[2 * side + here.core]

    def to_core(turns=(0, 1)):
        made = []
        for at in turns:
            there = 2 * at + 1 - here.core
            for kind, (source, target) in enumerate(((grad_in, core_in), (grad_out, core_out))):
                sems = core_send.at[kind, at], core_recv.at[kind, at]
                made.append(remote(source.at[there], target.at[at], *sems, here.core_device()))
        return made

    def second():
        made = []
        for far in range(fars):
            sems = second_send.at[0, far], second_recv.at[0, far]
            source = grad_in.at[2 * (1 - side) + here.core, 2 * far + 1 - level]
            made.append(remote(source, second_in.at[far], *sems, across))
            sems = second_send.at[1, far], second_recv.at[1, far]
            source = grad_out.at[2 * (1 - side) + here.core, 2 * far + 1 - level]
            made.append(remote(source, second_out.at[far], *sems, beside))
        return made

    def stores(kinds):
        made = []
        there = 2 * (1 - side) + here.core
        for far in range(fars):
            for kind, (source, target) in enumerate(
                (
                    (grad_in.at[there, 2 * far + level], in_across),
                    (own_in.at[2 * far + 1 - level], in_beside),
                    (own_in.at[2 * far + level], in_own),
                    (grad_out.at[there, 2 * far + level], out_across),
                    (own_out.at[2 * far + 1 - level], out_beside),
                    (own_out.at[2 * far + level], out_own),
                )
            ):
                if kind in kinds:
                    made.append(pltpu.make_async_copy(source, target.at[far], store_sem.at[kind, far]))
        return made

    def add(target, source):
        target[...] = (target[...].astype(f32) + source[...].astype(f32)).astype(bf16)
    later = [
        pltpu.make_async_copy(source, target, load_sem.at[6 + index])
        for index, (source, target) in enumerate(
            (
                (w_qkv_hbm, w_qkv),
                (turned_hbm, turned),
                (query_hbm, query),
                (pair_hbm, pair),
                (merged_hbm, merged),
                (log_total_hbm, log_total),
                (bias_hbm, bias),
                (bias_before, grad_bias),
            )[: 8 if earlier_bias else 7]
        )
    ]
    for head in range(heads):
        rows = pl.ds(pl.multiple_of(block * wide + head * HEAD, HEAD), HEAD)
        target = w_output.at[head * BLOCK + HEAD : (head + 1) * BLOCK]
        later.append(pltpu.make_async_copy(w_output_hbm.at[layer, rows], target, load_sem.at[3 + head]))

    slots, arrived_grad = (slots, slots_more), (arrived_grad, arrived_grad_more)
    answer, returned = (answer, answer_more), (returned, returned_more)
    spans = halves((arrived, arrived_more))

    def hand_slots(half, step, source):
        return remote(
            slots[half].at[here.expert_other(step)],
            arrived_grad[half].at[source],
            slot_send.at[half, step - 1],
            slot_recv.at[half, step - 1],
            {"expert": here.expert_other(step)},
        )

    def hand_answer(half, step, source):
        return remote(
            answer[half].at[here.expert_other(step)],
            returned[half].at[source],
            back_send.at[half, step - 1],
            back_recv.at[half, step - 1],
            {"expert": here.expert_other(step)},
        )

    def experts_phase(w_in, w_out, hidden, slope, before_grad, total, turned_given):
        loads = [
            pltpu.make_async_copy(before_hbm, slope, load_sem.at[2]),
            pltpu.make_async_copy(w_out_hbm.at[layer, 0], w_out, load_sem.at[0]),
            pltpu.make_async_copy(w_in_hbm.at[layer, 0], w_in, load_sem.at[1]),
        ]
        for load in loads + later:
            load.start()
        for head in range(heads):
            w_output[head * BLOCK : head * BLOCK + HEAD, :] = jnp.zeros((HEAD, w_output.shape[1]), bf16)
        came = grad[...].astype(f32)
        chances = router[...]
        gate = jnp.sum(chances * chosen[...], axis=-1, keepdims=True)
        gate_grad = jnp.sum(came * picked[...].astype(f32), axis=-1, keepdims=True)
        answer_grad = (gate * came).astype(bf16)
        for half, (low, high) in enumerate(spans):
            for expert in range(experts):
                slots[half][expert] = dot(select[expert, low:high], answer_grad).astype(bf16)
        here.greet(plane=earlier is not None, swap=last is not None)
        if earlier:
            earlier.begin(here)

        for half in range(2):
            for step in range(1, experts):
                hand_slots(half, step, here.expert).start()
            arrived_grad[half][here.expert] = slots[half][here.expert]
        hidden_width = w_in.shape[1]

        loads[0].wait()

        @pl.loop(0, hidden_width // FCHUNK)
        def _(index):
            columns = pl.ds(pl.multiple_of(index * FCHUNK, FCHUNK), FCHUNK)
            made, steep = gelu_parts(slope[:, columns])
            hidden[:, columns] = made.astype(bf16)
            slope[:, columns] = steep

        mid = middle[...]
        scale = root_scale(mid)
        unit = mid * scale
        moe_in = unit * gain_moe[layer : layer + 1, :]
        chance_grad = chosen[...] * gate_grad
        logit_grad = chances * (chance_grad - jnp.sum(chances * chance_grad, axis=-1, keepdims=True))
        router_grad = lax.dot_general(
            logit_grad, moe_in, (((0,), (0,)), ((), ())), precision=highest, preferred_element_type=f32
        )
        grad_rows[...] = router_grad[:8, :]
        moe_part = jnp.dot(
            logit_grad, widened(w_router, layer), precision=highest, preferred_element_type=f32
        )
        given = jnp.concatenate([joined(arrived), joined(arrived_more)], axis=0)
        turned_given[...] = given.astype(f32).T.astype(bf16)
        total[...] = jnp.zeros_like(total)
        loads[1].wait()
        loads[2].wait()
        for half, (low, high) in enumerate(spans):
            for step in range(1, experts):
                hand_slots(half, step, rem(here.expert + experts - step, experts)).wait_recv()
            rows = slice(experts * low, experts * high)
            given_grad[rows, :] = joined(arrived_grad[half])

            @pl.loop(0, hidden_width // FCHUNK)
            def _(index, rows=rows):
                columns = pl.ds(pl.multiple_of(index * FCHUNK, FCHUNK), FCHUNK)
                hidden_grad = dot_nt(given_grad[rows, :], w_out[columns, :])
                low_grad = (hidden_grad * slope[rows, columns]).astype(bf16)
                before_grad[rows, columns] = low_grad
                total[rows, :] += dot_nt(low_grad, w_in[:, columns])

            for expert in range(experts):
                first = experts * low + expert * (high - low)
                answer[half][expert] = total[first : first + high - low, :].astype(bf16)
            for step in range(1, experts):
                hand_answer(half, step, here.expert).start()
            returned[half][here.expert] = answer[half][here.expert]
        rows_in, rows_out = grad_in.shape[2], grad_out.shape[2]
        columns_in = grad_in.shape[3] // GROUP
        for turn in range(4):
            there = 2 * (turn % 2) + (1 - here.core if turn < 2 else here.core)
            rows = pl.ds(pl.multiple_of(there * (parts * rows_in), parts * rows_in), parts * rows_in)
            for piece in range(GROUP):
                columns = slice(piece * columns_in, (piece + 1) * columns_in)
                made = dot(turned_given[rows, :], before_grad[:, columns])
                for at in range(parts):
                    grad_in[there, at, :, columns] = made[at * rows_in : (at + 1) * rows_in, :].astype(bf16)
            columns = pl.ds(pl.multiple_of(there * (parts * rows_out), parts * rows_out), parts * rows_out)
            made = dot_tn(hidden[:, columns], given_grad[...])
            for at in range(parts):
                grad_out[there, at] = made[at * rows_out : (at + 1) * rows_out, :].astype(bf16)
            if turn < 2:
                for copy in to_core((turn,)):
                    copy.start()

        moe_grad = moe_part
        for half, (low, high) in enumerate(spans):
            for step in range(1, experts):
                hand_answer(half, step, rem(here.expert + experts - step, experts)).wait_recv()
            for expert in range(experts):
                moe_grad = moe_grad + dot_tn(select[expert, low:high], returned[half][expert])
        grad_rows[4:5, :] = jnp.sum(moe_grad * unit, axis=0, keepdims=True)
        scaled = moe_grad * gain_moe[layer : layer + 1, :]
        mid_grad = came + scale * (scaled - unit * jnp.mean(unit * scaled, axis=-1, keepdims=True))
        branches[block] = mid_grad.astype(bf16)
        return mid_grad

    slot_rows = given_grad.shape[0]
    mid_grad = pl.run_scoped(
        experts_phase,
        pltpu.VMEM(w_in_hbm.shape[2:], bf16),
        pltpu.VMEM(w_out_hbm.shape[2:], bf16),
        pltpu.VMEM(before_hbm.shape, bf16),
        pltpu.VMEM(before_hbm.shape, f32),
        pltpu.VMEM(before_hbm.shape, bf16),
        pltpu.VMEM((slot_rows, grad.shape[1]), f32),
        pltpu.VMEM((grad.shape[1], slot_rows), bf16),
    )

    gather, relay = gathering(here, branches, group_send, group_recv, earlier is None)
    for flip in (1, 2):
        gather(flip, block).start()
    if earlier is None:
        for flip in (1, 2):
            relay(flip, block).start()
    for turn in range(2):
        for copy in to_core((turn,)):
            copy.wait_recv()
        for at in range(parts):
            add(grad_in.at[2 * turn + here.core, at], core_in.at[turn, at])
            add(grad_out.at[2 * turn + here.core, at], core_out.at[turn, at])
    if earlier:
        for flip in (1, 2):
            gather(flip, here.flipped(flip)).wait_recv()
            relay(flip, here.flipped(flip)).start()
    for copy in second() + stores((0, 2, 4, 5)):
        copy.start()
    if earlier:
        earlier.pass_line()
    for load in later:
        load.wait()
    def hand_pair(step, source):
        return remote(
            pair_sent.at[step - 1],
            pair_recv.at[step - 1],
            part_send.at[step - 1],
            part_recv.at[step - 1],
            here.part_device(here.part_other(step)),
        )

    def attention_phase(pair_grad):
        lane = lanes(BLOCK, BLOCK)
        if not earlier_bias:
            grad_bias[...] = jnp.zeros_like(grad_bias)
        for flip in range(GROUP):
            mine = here.flipped(flip)
            if flip == 3:
                for other in (1, 2):
                    relay(other, mine).wait_recv()
            elif flip and earlier is None:
                gather(flip, mine).wait_recv()
            wanted = dot_nt(branches[mine], w_output[...])
            wanted_low = wanted.astype(bf16)
            wanted = wanted_low.astype(f32)
            turned_rows = jnp.concatenate([query[mine].astype(f32).T, wanted.T], axis=1).astype(bf16)
            products = wanted * merged[mine]
            for head in range(heads):
                columns = slice(head * BLOCK, (head + 1) * BLOCK)
                rows = jnp.concatenate([query[mine, :, columns], wanted_low[:, columns]], axis=0)
                delta = jnp.sum(products[:, columns], axis=-1, keepdims=True)
                log_sum = log_total[mine][:, head : head + 1]
                gathered = jnp.zeros((BLOCK, BLOCK), f32)
                for part in range(parts):
                    both = pair[part, :, :, columns].reshape(GROUP * BLOCK, BLOCK)
                    raw = dot_nt(rows, both)
                    upper, lower = [], []
                    for of_block in range(GROUP):
                        inside = slice(of_block * BLOCK, (of_block + 1) * BLOCK)
                        place = here.bias_index(part, of_block, mine)
                        weight = jnp.exp(raw[:BLOCK, inside] + (bias[head, place] - log_sum))
                        score_grad = weight * (raw[BLOCK:, inside] - delta)
                        grad_bias[head, place] += score_grad
                        upper.append(score_grad.astype(bf16))
                        lower.append(weight.astype(bf16))
                    upper = jnp.concatenate(upper, axis=1)
                    stacked = jnp.concatenate([upper, jnp.concatenate(lower, axis=1)], axis=0)
                    gathered = gathered + dot(upper, both)
                    more = dot(turned_rows[columns], stacked)
                    if flip:
                        pair_grad[part, columns, :] += more
                    else:
                        pair_grad[part, columns, :] = more
                query_grad[mine, :, columns] = jnp.where(lane < HEAD, gathered, 0.0).astype(bf16)
        for step in range(1, parts):
            pair_sent[step - 1] = pair_grad[here.part_other(step)].astype(bf16)
            hand_pair(step, 0).start()
        summed = pair_grad[here.part]
        for step in range(1, parts):
            hand_pair(step, 0).wait_recv()
            summed = summed + pair_recv[step - 1].astype(f32)
        summed = summed.T.astype(bf16)
        for of_block in range(GROUP):
            made_grad[of_block, :, : 2 * wide] = summed[of_block * BLOCK : (of_block + 1) * BLOCK, :]
            made_grad[of_block, :, 2 * wide :] = dot(
                query_grad[of_block], half_select(3 * BLOCK, 2 * BLOCK, 0)
            ).astype(bf16)

    pl.run_scoped(attention_phase, pltpu.VMEM((parts, 2 * wide, GROUP * BLOCK), f32))

    def hand_normed(flip):
        return remote(
            normed_sent.at[flip - 1],
            normed_recv.at[flip - 1],
            merge_send.at[flip - 1],
            merge_recv.at[flip - 1],
            here.group_device(here.flipped(flip)),
        )

    for flip in (3, 1, 2):
        normed_sent[flip - 1] = dot_nt(made_grad[here.flipped(flip)], w_qkv[...]).astype(bf16)
        hand_normed(flip).start()
    if last:
        x_last, out, out_low, send, recv = last
        out_low[...] = x_last[...].astype(bf16)
        swap = Swap(here, [(out_low, out)], send, recv)
        swap.start((0,))
    normed_grad = dot_nt(made_grad[block], w_qkv[...])
    if earlier:
        earlier.pass_plane()
    both = made_grad[...].reshape(GROUP * BLOCK, made_grad.shape[2])
    rows = turned.shape[0] // GROUP
    tall = grad_qkv.shape[3]
    for there in range(GROUP):
        made = dot(turned[there * rows : (there + 1) * rows, :], both)
        for at in range(parts):
            for expert in range(experts):
                first = (at * experts + expert) * tall
                grad_qkv[there, at, expert] = made[first : first + tall, :].astype(bf16)
    made = dot_tn(
        merged[...].reshape(GROUP * BLOCK, 3 * BLOCK).astype(bf16),
        branches[...].reshape(GROUP * BLOCK, branches.shape[2]),
    )
    for head in range(heads):
        output_sum[head * HEAD : (head + 1) * HEAD, :] = made[head * BLOCK + HEAD : (head + 1) * BLOCK, :]
    stores_late = [pltpu.make_async_copy(grad_qkv, grad_qkv_out, store_sem.at[6, 0])]
    if table:
        grad_bias_out[...] = table_sum(table, grad_bias, here.block)
    else:
        stores_late.append(pltpu.make_async_copy(grad_bias, grad_bias_out, store_sem.at[7, 0]))
    for store in stores_late:
        store.start()
    half = grad_output.shape[4]
    for at in range(parts):
        for expert in range(experts):
            first = (at * experts + expert) * tall
            for turn in range(2):
                piece = output_sum[first : first + tall, turn * half : (turn + 1) * half]
                grad_output[turn, at, expert] = piece.astype(bf16)
    for copy in second():
        copy.wait_recv()
    for far in range(fars):
        add(own_in.at[2 * far + 1 - level], second_in.at[far])
        add(grad_out.at[2 * (1 - side) + here.core, 2 * far + level], second_out.at[far])
    for copy in stores((1, 3)):
        copy.start()
    value = x[...]
    scale = root_scale(value)
    unit = value * scale
    for flip in (1, 2, 3):
        hand_normed(flip).wait_recv()
        normed_grad = normed_grad + normed_recv[flip - 1].astype(f32)
    grad_rows[5:6, :] = jnp.sum(normed_grad * unit, axis=0, keepdims=True)
    scaled = normed_grad * gain_attn[layer : layer + 1, :]
    grad_next[...] = mid_grad + scale * (scaled - unit * jnp.mean(unit * scaled, axis=-1, keepdims=True))
    if earlier:
        earlier.finish()
    if last:
        swap.wait((0,))
        swap.drain()
    for copy in stores(range(6)) + stores_late:
        copy.wait()
    for copy in to_core() + second():
        copy.wait_send()
    for flip in (1, 2):
        gather(flip, block).wait_send()
        relay(flip, here.flipped(flip)).wait_send()
    for flip in (1, 2, 3):
        hand_normed(flip).wait_send()
    for step in range(1, parts):
        hand_pair(step, 0).wait_send()
    for step in range(1, experts):
        for half in range(2):
            hand_slots(half, step, here.expert).wait_send()
            hand_answer(half, step, here.expert).wait_send()


VMEM = pl.BlockSpec(memory_space=pltpu.VMEM)
ANY = pl.BlockSpec(memory_space=pl.ANY)
DMA = pltpu.SemaphoreType.DMA


def forward_layer(layer, layers, begin, going, weights):
    parts, experts = lax.axis_size("context"), lax.axis_size("expert")
    w_in = weights[7]
    width, hidden = w_in.shape[2:]
    count = BLOCK
    wide, packed = 3 * HEAD, 5 * BLOCK
    room = count * 5 // (4 * experts)
    cut = room // 32 * 16
    shape, scratch = jax.ShapeDtypeStruct, pltpu.VMEM
    first = begin is not None
    gives = Saved(
        x=shape((count, width), f32),
        grad=shape((count, width), bf16),
        marks=shape((8, count), jnp.int32),
        bias=shape((3, 5, BLOCK, BLOCK), f32),
        select=shape((experts, room, count), bf16),
        chosen=shape((count, BLOCK), f32),
        w_qkv=shape((width, packed), bf16),
        turned=shape((width, GROUP * count), bf16),
        query=shape((GROUP, count, 3 * BLOCK), bf16),
        pair=shape((parts, GROUP, count, 2 * wide), bf16),
        merged=shape((GROUP, count, 3 * BLOCK), f32),
        log_total=shape((GROUP, count, BLOCK), f32),
        middle=shape((count, width), f32),
        router=shape((count, BLOCK), f32),
        picked=shape((count, width), bf16),
        arrived=shape((experts, cut, width), bf16),
        arrived_more=shape((experts, room - cut, width), bf16),
        before=shape((experts * room, hidden), f32),
        x_next=shape((count, width), f32),
    )
    far = Saved(*[VMEM] * len(gives))._replace(
        w_qkv=ANY, turned=ANY, query=ANY, pair=ANY, merged=ANY, log_total=ANY, before=ANY
    )
    skipped = 0 if first else 4
    start = list(begin) if first else [going.x_next, going.marks, going.bias]
    start_specs = [VMEM] * 4 + [pl.BlockSpec(memory_space=pltpu.SMEM)] if first else [VMEM] * 3
    made = pl.pallas_call(
        functools.partial(forward_kernel, layer, layers, parts, experts, first),
        out_shape=list(gives[skipped:]),
        in_specs=start_specs + [VMEM] * 3 + [ANY] * 6,
        out_specs=list(far[skipped:]),
        scratch_shapes=[
            scratch((width, packed), bf16),
            scratch((width, GROUP * count), bf16),
            scratch((GROUP, count, 3 * BLOCK), bf16),
            scratch((parts, GROUP, count, 2 * wide), bf16),
            scratch((GROUP, count, 3 * BLOCK), f32),
            scratch((GROUP, count, BLOCK), f32),
            scratch((GROUP, count, wide), bf16),
            scratch((experts * room, hidden), f32),
            scratch((GROUP, count, width), bf16),
            scratch((width, 6 * BLOCK), bf16),
            scratch((width, width), bf16),
            scratch((width, hidden), bf16),
            scratch((hidden, width), bf16),
            scratch((parts * GROUP, count, BLOCK), f32),
            scratch((GROUP, count, wide), bf16),
            scratch((experts, cut, width), bf16),
            scratch((experts, room - cut, width), bf16),
            scratch((experts * room, width), f32),
            *[scratch((experts, cut, width), bf16), scratch((experts, room - cut, width), bf16)] * 2,
            DMA((6,)),
            DMA((7,)),
            DMA((4,)),
            DMA((4,)),
            DMA((parts - 1, GROUP)),
            DMA((parts - 1, GROUP)),
            DMA((3,)),
            DMA((3,)),
            DMA((2, experts - 1)),
            DMA((2, experts - 1)),
            DMA((2, experts - 1)),
            DMA((2, experts - 1)),
        ]
        + ([scratch((count, width), bf16), scratch((8, count), jnp.int32), DMA((3,)), DMA((3,))] if first else []),
        compiler_params=pltpu.CompilerParams(
            collective_id=layer, has_side_effects=True, vmem_limit_bytes=60 * 2**20
        ),
        name="layer_forward",
    )(*start, *weights)
    return Saved(*([] if first else [going.x_next, going.grad, going.marks, going.bias]), *made)


def backward_layer(layer, layers, grad, saved, bias_before, left, weights, x_last, table):
    gain_attn, gain_moe, w_router, _, _, _, w_output, w_in, w_out = weights
    w_qkv, select, bias = saved.w_qkv, saved.select, saved.bias
    count, width = grad.shape
    parts, experts = lax.axis_size("context"), lax.axis_size("expert")
    wide = 3 * HEAD
    room = select.shape[1]
    hidden = w_in.shape[3]
    shape = jax.ShapeDtypeStruct
    scratch = pltpu.VMEM
    span = GROUP * count
    rows_in, rows_out = width // (GROUP * parts), hidden // (GROUP * parts)
    tall = rows_in // experts
    fars = parts // 2
    specs, gives, given_specs, needs = earlier_call(parts, experts, left, None) if left else ([], [], [], [])
    taken = present(taken_from(left, None)) if left else []
    gives = present(gives)
    cut = saved.arrived.shape[1]
    own_gives = Own(
        grad_next=shape((count, width), f32),
        in_across=shape((fars, rows_in, hidden), bf16),
        in_beside=shape((fars, rows_in, hidden), bf16),
        in_own=shape((fars, rows_in, hidden), bf16),
        out_across=shape((fars, rows_out, width), bf16),
        out_beside=shape((fars, rows_out, width), bf16),
        out_own=shape((fars, rows_out, width), bf16),
        qkv=shape((GROUP, parts, experts, tall, w_qkv.shape[1]), bf16),
        output=shape((2, parts, experts, tall, width // 2), bf16),
        bias=shape((table, 128) if table else bias.shape, f32),
        rows=shape((8, width), f32),
    )
    own_specs = [VMEM] + [ANY] * 7 + [VMEM, VMEM if table else ANY, VMEM]
    last = int(x_last is not None)
    counts = (24, len(taken), len(own_gives), len(gives), len(needs), last)
    given = pl.pallas_call(
        functools.partial(backward_and_earlier, layer, parts, experts, counts, bias_before is not None, table),
        out_shape=[*own_gives, *gives] + [shape(grad.shape, bf16)] * last,
        in_specs=[VMEM] * 7 + [ANY] * 7 + [VMEM] * 5 + [ANY] * 5 + specs + [VMEM] * last,
        out_specs=own_specs + given_specs + [VMEM] * last,
        scratch_shapes=[
            scratch(bias.shape, f32),
            scratch(saved.turned.shape, bf16),
            scratch(saved.query.shape, bf16),
            scratch(saved.pair.shape, bf16),
            scratch(saved.merged.shape, f32),
            scratch(saved.log_total.shape, f32),
            scratch((GROUP, parts, experts, tall, w_qkv.shape[1]), bf16),
            scratch(bias.shape, f32),
            scratch((GROUP, parts, rows_in, hidden), bf16),
            scratch((GROUP, parts, rows_out, width), bf16),
            scratch((2, parts, rows_in, hidden), bf16),
            scratch((2, parts, rows_out, width), bf16),
            scratch((fars, rows_in, hidden), bf16),
            scratch((fars, rows_out, width), bf16),
            scratch((wide, width), f32),
            scratch((width, w_qkv.shape[1]), bf16),
            scratch((3 * BLOCK, width), bf16),
            *[scratch((experts, cut, width), bf16), scratch((experts, room - cut, width), bf16)] * 4,
            scratch((experts * room, width), bf16),
            scratch((GROUP, count, width), bf16),
            scratch((GROUP, count, 3 * BLOCK), bf16),
            scratch((parts - 1, 2 * wide, span), bf16),
            scratch((parts - 1, 2 * wide, span), bf16),
            scratch((GROUP, count, w_qkv.shape[1]), bf16),
            scratch((GROUP - 1, count, width), bf16),
            scratch((GROUP - 1, count, width), bf16),
            DMA((14,)),
            DMA((2, experts - 1)),
            DMA((2, experts - 1)),
            DMA((2, experts - 1)),
            DMA((2, experts - 1)),
            DMA((4,)),
            DMA((4,)),
            DMA((parts - 1,)),
            DMA((parts - 1,)),
            DMA((3,)),
            DMA((3,)),
            DMA((2, 2)),
            DMA((2, 2)),
            DMA((2, fars)),
            DMA((2, fars)),
            DMA((8, fars)),
            *needs,
            *([scratch(grad.shape, bf16), DMA((1,)), DMA((1,))] if last else []),
        ],
        compiler_params=pltpu.CompilerParams(
            collective_id=layers + layer,
            has_side_effects=True,
            vmem_limit_bytes=(60 if parts <= 2 else 63) * 2**20,
        ),
        name="layer_backward",
    )(
        grad,
        saved.x,
        gain_attn,
        gain_moe,
        w_router,
        select,
        saved.chosen,
        bias,
        bias if bias_before is None else bias_before,
        saved.turned,
        saved.query,
        saved.pair,
        saved.merged,
        saved.log_total,
        saved.middle,
        saved.router,
        saved.picked,
        saved.arrived,
        saved.arrived_more,
        saved.before,
        w_qkv,
        w_output,
        w_in,
        w_out,
        *taken,
        *([x_last] if last else []),
    )
    own, sums = given[: len(own_gives)], given[len(own_gives) : len(own_gives) + len(gives)]
    return Own(*own), Given(*sums) if sums else None, given[-1]


def on_device(
    tokens,
    w_query,
    w_key,
    w_value,
    w_output,
    rel_bias,
    gain_attn,
    gain_moe,
    w_router,
    w_in,
    w_out,
    routes,
    kept,
    cotangent,
):
    experts = w_router.shape[2]
    layers = w_query.shape[0]
    parts = lax.axis_size("context")
    weights = (gain_attn, gain_moe, jnp.swapaxes(w_router, 1, 2), w_key, w_value, w_query, w_output, w_in, w_out)
    saved, going = [], None
    for layer in range(layers):
        begin = (tokens[0], cotangent[0], routes[:, 0, :, 0], kept[:, 0], rel_bias) if layer == 0 else None
        going = forward_layer(layer, layers, begin, going, weights)
        saved.append(going)
    grad, bias_grad = saved[0].grad, None
    left, lefts, sums = None, [], []
    for layer in reversed(range(layers)):
        x_last = going.x_next if layer == layers - 1 else None
        carried = left if parts == 2 else None
        own, done, swapped = backward_layer(layer, layers, grad, saved[layer], bias_grad, carried, weights, x_last, None if layer else rel_bias.shape[0])
        if x_last is not None:
            out = swapped[None]
        if done:
            sums.insert(0, done)
        grad, bias_grad = own.grad_next, own.bias
        left = own
        lefts.insert(0, left)
        if layer == 0:
            others = list(zip(lefts[1:], sums, strict=True)) if parts == 2 else ()
            done, d_tokens, finals = finish(left, rel_bias.shape[0], 2 * layers, grad, others)
            sums.insert(0, done)
        elif parts > 2:
            sums.insert(0, finish(left, None, 2 * layers + layer)[0])

    def experts_sum(own, from_across, from_beside):
        total = own.astype(f32) + from_across.astype(f32) + from_beside.astype(f32)
        if parts == 2:
            return total[0]
        groups = [[2 * far + level for far in range(parts // 2)] for level in range(2)]
        total = lax.psum_scatter(total.astype(bf16), "context", scatter_dimension=0, axis_index_groups=groups)
        return total.astype(f32)

    if finals:
        grad_in, grad_out = (item.astype(f32) for item in finals)
    else:
        grad_in = jnp.stack(
            [experts_sum(a.in_own, b.in_from_across, b.in_from_beside) for a, b in zip(lefts, sums)]
        )
        grad_out = jnp.stack(
            [experts_sum(a.out_own, b.out_from_across, b.out_from_beside) for a, b in zip(lefts, sums)]
        )
    rank = (lax.axis_index("dp") * parts + lax.axis_index("context")) * experts + lax.axis_index("expert")
    tall = sums[0].sums.shape[1]
    rows = jnp.stack([item.rows_sum for item in sums])
    rows = lax.dynamic_slice_in_dim(rows, rank * tall, tall, 2)
    key_out, value_out, query_out, output_out = (
        jnp.stack([item.sums[kind] for item in sums]) for kind in range(4)
    )
    return (
        out,
        d_tokens[None],
        query_out,
        key_out,
        value_out,
        output_out,
        sums[0].table_out[:, : rel_bias.shape[1]],
        rows[:, 5],
        rows[:, 4],
        jnp.swapaxes(rows[:, :experts], 1, 2),
        grad_in[:, None],
        grad_out[:, None],
    )


def solution(mesh):
    in_specs = (
        P("dp", ("context", "expert"), None),
        P(),
        P(),
        P(),
        P(),
        P(),
        P(),
        P(),
        P(),
        P(None, "expert", None, None),
        P(None, "expert", None, None),
        P(None, "dp", ("context", "expert"), None),
        P(None, "dp", ("context", "expert")),
        P("dp", ("context", "expert"), None),
    )
    out_specs = (
        P("dp", ("context", "expert"), None),
        P("dp", ("context", "expert"), None),
        P(None, ("dp", "context", "expert"), None),
        P(None, ("dp", "context", "expert"), None),
        P(None, ("dp", "context", "expert"), None),
        P(None, ("dp", "context", "expert"), None),
        P(),
        P(None, ("dp", "context", "expert")),
        P(None, ("dp", "context", "expert")),
        P(None, ("dp", "context", "expert"), None),
        P(None, "expert", ("dp", "context"), None),
        P(None, "expert", ("dp", "context"), None),
    )
    return jax.shard_map(
        on_device, mesh=mesh, in_specs=in_specs, out_specs=out_specs, check_vma=False
    )
```

```python
import functools
from typing import Any, NamedTuple

import jax
import jax.numpy as jnp
import numpy as np
from jax import lax
from jax.experimental import pallas as pl
from jax.experimental.pallas import tpu as pltpu
from jax.sharding import PartitionSpec as P

highest = lax.Precision.HIGHEST
epsilon = 1e-06
thresholds = (12, 16, 23, 32, 46, 64, 91)
MESH = pl.DeviceIdType.MESH
GROUP = 4
HEAD = 64
BLOCK = 128
FCHUNK = 512
f32, bf16 = jnp.float32, jnp.bfloat16


def div(a, b):
    return lax.div(a, jnp.int32(b))


def rem(a, b):
    return lax.rem(a, jnp.int32(b))


def turned_pair(index):
    return 2 * rem(index, 2) + div(index, 2)


class Place:
    def __init__(self, parts, experts):
        self.parts, self.experts = parts, experts
        self.dp = lax.axis_index("dp")
        self.context = lax.axis_index("context")
        self.expert = lax.axis_index("expert")
        self.core = rem(self.dp, 2)
        self.far = div(self.context, 2)
        self.block = 2 * rem(self.context, 2) + div(self.dp, 2)
        self.part = 2 * self.far + self.core

    def flipped(self, flip):
        low = rem(rem(self.block, 2) + flip % 2, 2)
        high = rem(div(self.block, 2) + flip // 2, 2)
        return 2 * high + low

    def group_device(self, block):
        return {"dp": 2 * rem(block, 2) + self.core, "context": 2 * self.far + div(block, 2)}

    def part_other(self, step):
        return rem(self.part + step, self.parts)

    def part_device(self, part):
        return {
            "dp": self.dp - self.core + rem(part, 2),
            "context": 2 * div(part, 2) + rem(self.context, 2),
        }

    def expert_other(self, step):
        return rem(self.expert + step, self.experts)

    def offset(self, part, block, query_block):
        across = 4 * (block // 2 - div(query_block, 2)) + (block % 2 - rem(query_block, 2))
        part = jnp.int32(part)
        return 8 * (div(part, 2) - self.far) + across + 2 * (rem(part, 2) - self.core)

    def bias_index(self, part, block, query_block):
        offset = self.offset(part, block, query_block)
        return jnp.minimum(jnp.maximum(offset, -2), 2) + 2

    def core_device(self):
        return {"dp": self.dp + 1 - 2 * self.core}

    def plane_others(self):
        made = []
        for step in range(self.parts // 2):
            far = rem(self.far + step, self.parts // 2)
            for flip in range(GROUP):
                if step or flip:
                    other = self.flipped(flip)
                    device = {"dp": 2 * rem(other, 2) + self.core, "context": 2 * far + div(other, 2)}
                    made.append((step, flip, far, other, device))
        return made

    def is_swapped(self):
        return self.dp != turned_pair(self.expert)

    def swap_device(self):
        return {"dp": turned_pair(self.expert), "expert": turned_pair(self.dp)}

    def greet(self, plane=False, swap=False):
        if plane:
            partners = [item[-1] for item in self.plane_others()]
            partners += [{**device, "dp": device.get("dp") + 1 - 2 * self.core} for device in partners]
            partners += [self.core_device()]
        else:
            partners = [self.group_device(self.flipped(flip)) for flip in (1, 2, 3)]
            partners += [self.part_device(self.part_other(step)) for step in range(1, self.parts)]
        partners += [{"expert": self.expert_other(step)} for step in range(1, self.experts)]
        barrier = pltpu.get_barrier_semaphore()
        for partner in partners:
            pl.semaphore_signal(barrier, inc=1, device_id=partner, device_id_type=MESH)
        if swap:

            @pl.when(self.is_swapped())
            def _():
                pl.semaphore_signal(barrier, inc=1, device_id=self.swap_device(), device_id_type=MESH)

        def wait():
            if swap:

                @pl.when(self.is_swapped())
                def _():
                    pl.semaphore_wait(barrier, len(partners) + 1)

                @pl.when(jnp.logical_not(self.is_swapped()))
                def _():
                    pl.semaphore_wait(barrier, len(partners))

            else:
                pl.semaphore_wait(barrier, len(partners))

        return wait


def remote(source, target, send, receive, device):
    return pltpu.make_async_remote_copy(
        src_ref=source,
        dst_ref=target,
        send_sem=send,
        recv_sem=receive,
        device_id=device,
        device_id_type=MESH,
    )


def dot(a, b):
    return jnp.dot(a, b, preferred_element_type=f32)


def dot_nt(a, b):
    return lax.dot_general(a, b, (((1,), (1,)), ((), ())), preferred_element_type=f32)


def dot_tn(a, b):
    return lax.dot_general(a, b, (((0,), (0,)), ((), ())), preferred_element_type=f32)


def root_scale(value):
    return lax.rsqrt(jnp.mean(value * value, axis=-1, keepdims=True) + epsilon)


def lanes(rows, width):
    return lax.broadcasted_iota(jnp.int32, (rows, width), 1)


def gelu_parts(value):
    scale = 0.7978845608028654
    square = value * value
    inner = jnp.tanh(scale * (value + 0.044715 * (square * value)))
    half = 0.5 * (1.0 + inner)
    slope = half + 0.5 * value * (1.0 - inner * inner) * (scale * (1.0 + 3 * 0.044715 * square))
    return value * half, slope


def gelu(value):
    scale = 0.7978845608028654
    return value * (0.5 * (1.0 + jnp.tanh(scale * (value + 0.044715 * (value * value * value)))))


class Swap:
    def __init__(self, here, pairs, send, recv):
        self.here, self.pairs, self.send, self.recv = here, pairs, send, recv

    def copies(self, which):
        made = []
        for index in which:
            source, target = self.pairs[index]
            made.append(remote(source, target, self.send.at[index], self.recv.at[index], self.here.swap_device()))
        return made

    def start(self, which):
        @pl.when(self.here.is_swapped())
        def _():
            for copy in self.copies(which):
                copy.start()

        @pl.when(jnp.logical_not(self.here.is_swapped()))
        def _():
            for index in which:
                source, target = self.pairs[index]
                target[...] = source[...]

    def wait(self, which):
        @pl.when(self.here.is_swapped())
        def _():
            for copy in self.copies(which):
                copy.wait_recv()

    def drain(self):
        @pl.when(self.here.is_swapped())
        def _():
            for copy in self.copies(range(len(self.pairs))):
                copy.wait_send()


def route_tokens(marks, layer, layers, select, chosen):
    experts, room, count = select.shape
    route = marks[layer : layer + 1, :]
    live = marks[layers + layer : layers + layer + 1, :] > 0
    named = lax.broadcasted_iota(jnp.int32, (8, count), 0) == route
    before = lax.broadcasted_iota(jnp.int32, (count, count), 0)
    after = lax.broadcasted_iota(jnp.int32, (count, count), 1)
    named = named.astype(f32)
    ahead = dot(named.astype(bf16), (before < after).astype(f32).astype(bf16))
    rank = jnp.sum(named * ahead, axis=0, keepdims=True)
    slot = lax.broadcasted_iota(jnp.int32, (room, count), 0).astype(f32)
    for expert in range(experts):
        select[expert] = ((slot == rank) & (route == expert) & live).astype(f32).astype(bf16)
    chosen[...] = ((before == route) & live).astype(f32).T


def bucket_block(place, half):
    row = lax.broadcasted_iota(jnp.int32, (BLOCK, BLOCK), 0)
    column = lax.broadcasted_iota(jnp.int32, (BLOCK, BLOCK), 1)
    offset = (place - 2) * BLOCK + column - row
    distance = jnp.abs(offset)
    beyond = 8 + sum((distance >= limit).astype(jnp.int32) for limit in thresholds)
    return jnp.where(distance < 8, distance, beyond) + jnp.where(offset > 0, half, 0)


def bucket_range(place, half):
    return (half, 2 * half) if place == 3 else (0, half if place == 1 else 2 * half)


def make_bias(bias, rel_bias, first):
    half = rel_bias.shape[0] // 2
    for head in range(3):
        bias[head, 0] = jnp.full((BLOCK, BLOCK), rel_bias[half - 1, first + head], f32)
        bias[head, 4] = jnp.full((BLOCK, BLOCK), rel_bias[2 * half - 1, first + head], f32)
    for place in (1, 2, 3):
        buckets = bucket_block(place, half)
        for head in range(3):

            def one(bucket, made, buckets=buckets, head=head):
                return jnp.where(buckets == bucket, rel_bias[bucket, first + head], made)

            bias[head, place] = lax.fori_loop(*bucket_range(place, half), one, jnp.zeros((BLOCK, BLOCK), f32))


def pack_weights(w_qkv, slabs, block):
    wide = 3 * HEAD
    shape = (slabs.shape[1], w_qkv.shape[1])
    row = lax.broadcasted_iota(jnp.int32, shape, 0)
    column = lax.broadcasted_iota(jnp.int32, shape, 1)
    head, inside = column // BLOCK, column % BLOCK
    kind = inside // HEAD
    source = jnp.where(
        column < 2 * wide, 2 * BLOCK * kind + HEAD * head + inside % HEAD, 4 * BLOCK + column - 2 * wide
    )
    source = source + HEAD * rem(block, 2)
    move = ((row == source) & (column < 3 * wide)).astype(f32).astype(bf16)
    w_qkv[...] = dot(slabs[...], move).astype(bf16)


def ones_where(condition):
    return condition.astype(f32).astype(bf16)


def query_spread(rows, columns):
    row = lax.broadcasted_iota(jnp.int32, (rows, columns), 0)
    column = lax.broadcasted_iota(jnp.int32, (rows, columns), 1)
    return ones_where((column % BLOCK < HEAD) & (row == HEAD * (column // BLOCK) + column % BLOCK))


def half_select(rows, columns, half):
    row = lax.broadcasted_iota(jnp.int32, (rows, columns), 0)
    column = lax.broadcasted_iota(jnp.int32, (rows, columns), 1)
    return ones_where((row == BLOCK * (column // HEAD) + HEAD * half + column % HEAD) & (column < 3 * HEAD))


def forward_kernel(layer, layers, parts, experts, first, *refs):
    if first:
        tokens, cotangent, routes, kept, rel_bias, *refs = refs
    else:
        x, marks, bias, *refs = refs
    (
        gain_attn,
        gain_moe,
        w_router,
        w_key_hbm,
        w_value_hbm,
        w_query_hbm,
        w_output_hbm,
        w_in_hbm,
        w_out_hbm,
        *refs,
    ) = refs
    if first:
        x, grad, marks, bias, *refs = refs
    forward_body(
        layer,
        layers,
        parts,
        experts,
        (tokens, cotangent, routes, kept, rel_bias, grad) if first else None,
        x,
        marks,
        bias,
        gain_attn,
        gain_moe,
        w_router,
        w_key_hbm,
        w_value_hbm,
        w_query_hbm,
        w_output_hbm,
        w_in_hbm,
        w_out_hbm,
        *refs,
    )


def widened(w_router, layer):
    rows = w_router[layer]
    return jnp.concatenate([rows, jnp.zeros((BLOCK - rows.shape[0], rows.shape[1]), f32)], axis=0)


def gathering(here, blocks, send, recv, straight):
    half = blocks.shape[1] // 2

    def gather(flip, source):
        device = here.group_device(here.flipped(flip))
        return remote(blocks.at[source], blocks.at[source], send.at[flip - 1], recv.at[flip - 1], device)

    def relay(flip, source):
        rows = blocks.at[source, (flip - 1) * half : flip * half]
        device = here.group_device(here.flipped(3 if straight else 3 - flip))
        return remote(rows, rows, send.at[flip + 1], recv.at[flip + 1], device)

    return gather, relay


def halves(arrays):
    first = arrays[0].shape[1]
    return (0, first), (first, first + arrays[1].shape[1])


def joined(slots):
    return jnp.concatenate([slots[index].astype(f32) for index in range(slots.shape[0])], axis=0).astype(bf16)


def forward_body(
    layer,
    layers,
    parts,
    experts,
    begin,
    x,
    marks,
    bias,
    gain_attn,
    gain_moe,
    w_router,
    w_key_hbm,
    w_value_hbm,
    w_query_hbm,
    w_output_hbm,
    w_in_hbm,
    w_out_hbm,
    select,
    chosen,
    w_qkv_out,
    turned_out,
    query_out,
    pair_out,
    merged_out,
    log_total_out,
    middle,
    router,
    picked,
    arrived,
    arrived_more,
    before_out,
    x_next,
    w_qkv,
    turned,
    query,
    pair,
    merged,
    log_total,
    merged_low,
    before,
    normed,
    slabs,
    w_output,
    w_in,
    w_out,
    scores,
    merged_mine,
    slots,
    slots_more,
    total,
    answer,
    answer_more,
    returned,
    returned_more,
    load_sem,
    store_sem,
    group_send,
    group_recv,
    part_send,
    part_recv,
    merge_send,
    merge_recv,
    slot_send,
    slot_recv,
    back_send,
    back_recv,
    tokens_came=None,
    marks_here=None,
    swap_send=None,
    swap_recv=None,
):
    here = Place(parts, experts)
    heads = 3
    wide = heads * HEAD
    block = here.block
    if begin:
        tokens, cotangent, routes, kept, rel_bias, grad = begin
        all_here = here.greet(swap=True)
        marks_here[...] = jnp.zeros_like(marks_here)
        marks_here[:layers, :] = routes[...]
        marks_here[layers : 2 * layers, :] = kept[...]
        all_here()
        pairs = [(marks_here, marks), (tokens, tokens_came), (cotangent, grad)]
        swap = Swap(here, pairs, swap_send, swap_recv)
        swap.start((0, 1))
    else:
        all_here = here.greet()
    stores = [
        pltpu.make_async_copy(source, target, store_sem.at[index])
        for index, (source, target) in enumerate(
            (
                (w_qkv, w_qkv_out),
                (turned, turned_out),
                (query, query_out),
                (pair, pair_out),
                (merged, merged_out),
                (log_total, log_total_out),
                (before, before_out),
            )
        )
    ]
    slab = pl.ds(pl.multiple_of(BLOCK * div(3 * block, 2), BLOCK), 2 * BLOCK)
    loads = []
    for kind, source in enumerate((w_key_hbm, w_value_hbm, w_query_hbm)):
        target = slabs.at[:, kind * 2 * BLOCK : (kind + 1) * 2 * BLOCK]
        loads.append(pltpu.make_async_copy(source.at[layer, :, slab], target, load_sem.at[kind]))
    loads += [
        pltpu.make_async_copy(w_output_hbm.at[layer], w_output, load_sem.at[3]),
        pltpu.make_async_copy(w_in_hbm.at[layer, 0], w_in, load_sem.at[4]),
        pltpu.make_async_copy(w_out_hbm.at[layer, 0], w_out, load_sem.at[5]),
    ]
    for load in loads:
        load.start()
    if begin:
        for load in loads[:3]:
            load.wait()
        pack_weights(w_qkv, slabs, block)
        swap.wait((0, 1))
        value = tokens_came[...].astype(f32)
        x[...] = value
    else:
        value = x[...]
    normed[block] = (value * root_scale(value) * gain_attn[layer : layer + 1, :]).astype(bf16)
    if not begin:
        all_here()

    gather, relay = gathering(here, normed, group_send, group_recv, True)
    for flip in (1, 2):
        gather(flip, block).start()
    for flip in (1, 2):
        relay(flip, block).start()

    def hand_pair(step, part, of_block):
        return remote(
            pair.at[part, of_block],
            pair.at[part, of_block],
            part_send.at[step - 1, of_block],
            part_recv.at[step - 1, of_block],
            here.part_device(here.part_other(step)),
        )

    def project(of_block):
        made = dot(normed[of_block], w_qkv[...]).astype(bf16)
        pair[here.part, of_block] = made[:, : 2 * wide]
        query[of_block] = dot(made[:, 2 * wide :], query_spread(2 * BLOCK, 3 * BLOCK)).astype(bf16)
        for step in range(1, parts):
            hand_pair(step, here.part, of_block).start()
        columns = pl.ds(pl.multiple_of(of_block * BLOCK, BLOCK), BLOCK)
        turned[:, columns] = normed[of_block].astype(f32).T.astype(bf16)

    if begin:
        swap.start((2,))
    else:
        for load in loads[:3]:
            load.wait()
        pack_weights(w_qkv, slabs, block)
    project(block)
    route_tokens(marks, layer, layers, select, chosen)
    if begin:
        make_bias(bias, rel_bias, heads * block)
    for flip in (1, 2):
        gather(flip, here.flipped(flip)).wait_recv()
        project(here.flipped(flip))
    for flip in (1, 2):
        relay(flip, here.flipped(3)).wait_recv()
    project(here.flipped(3))
    for store in stores[:3]:
        store.start()
    lane_log = lanes(BLOCK, BLOCK)

    def hand_merged(flip, source):
        return remote(
            merged_mine.at[here.flipped(flip)],
            merged_low.at[source],
            merge_send.at[flip - 1],
            merge_recv.at[flip - 1],
            here.group_device(here.flipped(flip)),
        )

    for flip in (3, 1, 2, 0):
        mine = here.flipped(flip)
        logs = jnp.zeros((BLOCK, BLOCK), f32)
        for head in range(heads):
            columns = slice(head * BLOCK, (head + 1) * BLOCK)
            top = jnp.full((BLOCK, 1), -1e30, f32)
            for turn in range(parts):
                part = rem(here.part + turn, parts)
                if turn == 1 and flip == 3 and head == 0:
                    for step in range(1, parts):
                        source = rem(here.part + parts - step, parts)
                        for of_block in range(GROUP):
                            hand_pair(step, source, of_block).wait_recv()
                    stores[3].start()
                both = pair[part, :, :, columns].reshape(GROUP * BLOCK, BLOCK)
                raw = dot_nt(query[mine, :, columns], both)
                for of_block in range(GROUP):
                    piece = (
                        raw[:, of_block * BLOCK : (of_block + 1) * BLOCK]
                        + bias[head, here.bias_index(part, of_block, mine)]
                    )
                    scores[turn * GROUP + of_block] = piece
                    top = jnp.maximum(top, jnp.max(piece, axis=-1, keepdims=True))
            summed = jnp.zeros((BLOCK, 1), f32)
            out = jnp.zeros((BLOCK, BLOCK), f32)
            for turn in range(parts):
                part = rem(here.part + turn, parts)
                pieces = []
                for of_block in range(GROUP):
                    weight = jnp.exp(scores[turn * GROUP + of_block] - top)
                    summed = summed + jnp.sum(weight, axis=-1, keepdims=True)
                    pieces.append(weight.astype(bf16))
                both = pair[part, :, :, columns].reshape(GROUP * BLOCK, BLOCK)
                out = out + dot(jnp.concatenate(pieces, axis=1), both)
            merged[mine, :, columns] = jnp.where(lane_log >= HEAD, out / summed, 0.0)
            logs = jnp.where(lane_log == head, top + jnp.log(summed), logs)
        final = dot(merged[mine].astype(bf16), half_select(3 * BLOCK, wide, 1))
        log_total[mine] = logs
        if flip:
            merged_mine[mine] = final.astype(bf16)
            hand_merged(flip, block).start()
        else:
            merged_low[block] = final.astype(bf16)

    for store in stores[4:6]:
        store.start()
    for flip in (1, 2, 3):
        hand_merged(flip, here.flipped(flip)).wait_recv()
    loads[3].wait()
    mid = value
    for of_block in range(GROUP):
        mid = mid + dot(merged_low[of_block], w_output[of_block * wide : (of_block + 1) * wide, :])
    middle[...] = mid
    moe_in = mid * root_scale(mid) * gain_moe[layer : layer + 1, :]
    moe_low = moe_in.astype(bf16)

    slots, arrived = (slots, slots_more), (arrived, arrived_more)
    answer, returned = (answer, answer_more), (returned, returned_more)
    spans = halves(arrived)

    def hand_slots(half, step, source):
        return remote(
            slots[half].at[here.expert_other(step)],
            arrived[half].at[source],
            slot_send.at[half, step - 1],
            slot_recv.at[half, step - 1],
            {"expert": here.expert_other(step)},
        )

    for half, (low, high) in enumerate(spans):
        for expert in range(experts):
            slots[half][expert] = dot(select[expert, low:high], moe_low).astype(bf16)
        for step in range(1, experts):
            hand_slots(half, step, here.expert).start()
        arrived[half][here.expert] = slots[half][here.expert]
    logits = lax.dot_general(
        moe_in, widened(w_router, layer), (((1,), (1,)), ((), ())), precision=highest, preferred_element_type=f32
    )
    logits = jnp.where(lane_log < experts, logits, -1e30)
    raised = jnp.exp(logits - jnp.max(logits, axis=-1, keepdims=True))
    chances = raised / jnp.sum(raised, axis=-1, keepdims=True)
    router[...] = chances
    gate = jnp.sum(chances * chosen[...], axis=-1, keepdims=True)
    total[...] = jnp.zeros_like(total)
    loads[4].wait()
    loads[5].wait()

    def hand_answer(half, step, source):
        return remote(
            answer[half].at[here.expert_other(step)],
            returned[half].at[source],
            back_send.at[half, step - 1],
            back_recv.at[half, step - 1],
            {"expert": here.expert_other(step)},
        )

    for half, (low, high) in enumerate(spans):
        for step in range(1, experts):
            hand_slots(half, step, rem(here.expert + experts - step, experts)).wait_recv()
        given = joined(arrived[half])
        rows = slice(experts * low, experts * high)

        @pl.loop(0, w_in.shape[1] // FCHUNK)
        def _(index, given=given, rows=rows):
            columns = pl.ds(pl.multiple_of(index * FCHUNK, FCHUNK), FCHUNK)
            first = dot(given, w_in[:, columns])
            before[rows, columns] = first
            total[rows, :] += dot(gelu(first).astype(bf16), w_out[columns, :])

        for expert in range(experts):
            first = experts * low + expert * (high - low)
            answer[half][expert] = total[first : first + high - low, :].astype(bf16)
        for step in range(1, experts):
            hand_answer(half, step, here.expert).start()
        returned[half][here.expert] = answer[half][here.expert]
    stores[6].start()
    back = jnp.zeros_like(value)
    for half, (low, high) in enumerate(spans):
        for step in range(1, experts):
            hand_answer(half, step, rem(here.expert + experts - step, experts)).wait_recv()
        for expert in range(experts):
            back = back + dot_tn(select[expert, low:high], returned[half][expert])
    picked[...] = back.astype(bf16)
    x_next[...] = mid + gate * back
    for store in stores:
        store.wait()
    if begin:
        swap.wait((2,))
        swap.drain()
    for flip in (1, 2):
        gather(flip, block).wait_send()
        relay(flip, here.flipped(flip)).wait_send()
    for flip in (1, 2, 3):
        hand_merged(flip, block).wait_send()
    for step in range(1, parts):
        for of_block in range(GROUP):
            hand_pair(step, here.part, of_block).wait_send()
    for step in range(1, experts):
        for half in range(2):
            hand_slots(half, step, here.expert).wait_send()
            hand_answer(half, step, here.expert).wait_send()


def table_sum(table, grads, block):
    marks = lanes(table, 128)
    row = lax.broadcasted_iota(jnp.int32, marks.shape, 0)
    half = table // 2
    total = jnp.zeros(marks.shape, f32)
    for head in range(3):
        made = jnp.zeros(marks.shape, f32)
        for place, bucket in ((0, half - 1), (4, 2 * half - 1)):
            line = jnp.sum(grads[head, place], axis=0, keepdims=True)
            made = made + jnp.where(row == bucket, line, 0.0)
        for place in (1, 2, 3):
            buckets = bucket_block(place, half)

            def one(bucket, made, buckets=buckets, place=place, head=head):
                found = jnp.where(buckets == bucket, grads[head, place], 0.0)
                return made + jnp.where(row == bucket, jnp.sum(found, axis=0, keepdims=True), 0.0)

            made = lax.fori_loop(*bucket_range(place, half), one, made)
        column = jnp.sum(made, axis=-1, keepdims=True)
        total = total + jnp.where(marks == 3 * block + head, column, 0.0)
    return total


class Saved(NamedTuple):
    x: Any
    grad: Any
    marks: Any
    bias: Any
    select: Any
    chosen: Any
    w_qkv: Any
    turned: Any
    query: Any
    pair: Any
    merged: Any
    log_total: Any
    middle: Any
    router: Any
    picked: Any
    arrived: Any
    arrived_more: Any
    before: Any
    x_next: Any


class Own(NamedTuple):
    grad_next: Any
    in_across: Any
    in_beside: Any
    in_own: Any
    out_across: Any
    out_beside: Any
    out_own: Any
    qkv: Any
    output: Any
    bias: Any
    rows: Any


class Taken(NamedTuple):
    in_across: Any
    in_beside: Any
    out_across: Any
    out_beside: Any
    qkv: Any
    output: Any
    rows: Any
    table_part: Any = None


class Given(NamedTuple):
    in_from_across: Any
    in_from_beside: Any
    out_from_across: Any
    out_from_beside: Any
    sums: Any
    rows_sum: Any
    table_out: Any = None


class Needed(NamedTuple):
    small: Any
    qkv_core: Any
    output_core: Any
    small_core: Any
    qkv_line: Any
    output_line: Any
    small_line: Any
    qkv_came: Any
    output_came: Any
    small_came: Any
    qkv_plane: Any
    output_plane: Any
    small_plane: Any
    qkv_last: Any
    output_last: Any
    small_last: Any
    expert_send: Any
    expert_recv: Any
    core_send: Any
    core_recv: Any
    line_send: Any
    line_recv: Any
    plane_send: Any
    plane_recv: Any
    output_send: Any
    output_recv: Any


def present(items):
    return [item for item in items if item is not None]


def taken_from(own, table):
    return Taken(
        own.in_across,
        own.in_beside,
        own.out_across,
        own.out_beside,
        own.qkv,
        own.output,
        own.rows,
        own.bias if table else None,
    )


class Earlier:
    def __init__(self, parts, experts, table, taken, given, needed):
        self.parts, self.experts, self.table, self.fars = parts, experts, table, parts // 2
        for refs in (Taken(*taken), Given(*given), Needed(*needed)):
            self.__dict__.update(refs._asdict())

    def expert_copies(self, which=(0, 1, 2, 3)):
        here, made = self.here, []
        across, beside = here.group_device(here.flipped(1)), here.group_device(here.flipped(2))
        for kind, (source, target, device) in enumerate(
            (
                (self.in_across, self.in_from_across, across),
                (self.out_beside, self.out_from_beside, beside),
                (self.in_beside, self.in_from_beside, beside),
                (self.out_across, self.out_from_across, across),
            )
        ):
            half = source.shape[2] // 2
            for turn in range(2):
                if kind // 2 * 2 + turn in which:
                    columns = slice(turn * half, (turn + 1) * half)
                    sems = self.expert_send.at[kind, turn], self.expert_recv.at[kind, turn]
                    made.append(remote(source.at[:, :, columns], target.at[:, :, columns], *sems, device))
        return made

    def core_copies(self):
        here, made = self.here, []
        device = here.core_device()
        for at in range(2):
            sems = self.core_send.at[at], self.core_recv.at[at]
            made.append(remote(self.qkv.at[2 * at + 1 - here.core], self.qkv_core.at[at], *sems, device))
        sems = self.core_send.at[2], self.core_recv.at[2]
        made.append(remote(self.output.at[1 - here.core], self.output_core, *sems, device))
        sems = self.core_send.at[3], self.core_recv.at[3]
        made.append(remote(self.small, self.small_core, *sems, device))
        return made

    def line_copies(self, step, source):
        here = self.here
        target = here.expert_other(step)
        device = {"expert": target}
        sems = [(self.line_send.at[kind, step - 1], self.line_recv.at[kind, step - 1]) for kind in range(3)]
        return [
            remote(self.qkv_line.at[target], self.qkv_came.at[source], *sems[0], device),
            remote(self.output_line.at[target], self.output_came.at[source], *sems[1], device),
            remote(self.small_line, self.small_came.at[source], *sems[2], device),
        ]

    def plane_copies(self):
        here, made = self.here, []
        for step, flip, far, other, device in here.plane_others():
            sems = [(self.plane_send.at[kind, step, flip], self.plane_recv.at[kind, step, flip]) for kind in range(2)]
            source = self.qkv_plane.at[rem(other, 2), 2 * far + div(other, 2)]
            made.append(remote(source, self.qkv_last.at[here.block, here.far], *sems[0], device))
            made.append(remote(self.small_plane, self.small_last.at[here.block, here.far], *sems[1], device))
        return made

    def output_copy(self, context):
        here = self.here
        return remote(
            self.output_plane.at[context],
            self.output_last.at[here.core, here.far],
            self.output_send.at[context],
            self.output_recv.at[here.core, here.far],
            {"dp": here.block, "context": jnp.int32(context)},
        )

    def is_here(self, context):
        return (self.here.block == self.here.dp) & (self.here.context == context)

    def begin(self, here, which=(0, 1, 2, 3)):
        self.here = here
        for copy in self.expert_copies(which):
            copy.start()
        pieces = self.rows.shape[1] // 128
        for piece in range(pieces):
            self.small[8 * piece : 8 * piece + 8, :] = self.rows[:, piece * 128 : (piece + 1) * 128]
        for copy in self.core_copies()[:3]:
            copy.start()
        if self.table:
            self.small[8 * pieces :, :] = self.table_part[...]
        self.core_copies()[3].start()

    def pass_line(self):
        here = self.here
        for copy in self.core_copies():
            copy.wait_recv()
        for expert in range(self.experts):
            for context in range(self.parts):
                for at in range(2):
                    self.qkv_line[expert, at, context] = (
                        self.qkv[2 * at + here.core, context, expert].astype(f32)
                        + self.qkv_core[at, context, expert].astype(f32)
                    ).astype(bf16)
                self.output_line[expert, context] = (
                    self.output[here.core, context, expert].astype(f32)
                    + self.output_core[context, expert].astype(f32)
                ).astype(bf16)
        self.small_line[...] = self.small[...] + self.small_core[...]
        for step in range(1, self.experts):
            for copy in self.line_copies(step, here.expert):
                copy.start()

    def pass_plane(self, which=()):
        here = self.here
        for step in range(1, self.experts):
            for copy in self.line_copies(step, rem(here.expert + self.experts - step, self.experts)):
                copy.wait_recv()
        sources = [rem(here.expert + step, self.experts) for step in range(1, self.experts)]
        for context in range(self.parts):
            for at in range(2):
                total = self.qkv_line[here.expert, at, context].astype(f32)
                for source in sources:
                    total = total + self.qkv_came[source, at, context].astype(f32)
                self.qkv_plane[at, context] = total.astype(bf16)
            total = self.output_line[here.expert, context].astype(f32)
            for source in sources:
                total = total + self.output_came[source, context].astype(f32)
            self.output_plane[context] = total.astype(bf16)
        total = self.small_line[...]
        for source in sources:
            total = total + self.small_came[source]
        self.small_plane[...] = total
        for copy in self.plane_copies():
            copy.start()
        for context in range(self.parts):

            @pl.when(jnp.logical_not(self.is_here(context)))
            def _():
                self.output_copy(context).start()

            @pl.when(self.is_here(context))
            def _():
                self.output_last[here.core, here.far] = self.output_plane[context]

        for copy in self.expert_copies(which):
            copy.start()
        self.qkv_last[here.block, here.far] = self.qkv_plane[div(here.dp, 2), here.context]
        self.small_last[here.block, here.far] = self.small_plane[...]

    def finish(self):
        here = self.here
        for copy in self.plane_copies():
            copy.wait_recv()
        for core in range(2):
            for far in range(self.fars):
                source_dp = 2 * here.core + core
                source_context = 2 * far + div(here.dp, 2)

                @pl.when(jnp.logical_not((source_dp == here.dp) & (source_context == here.context)))
                def _():
                    remote(
                        self.output_plane.at[0],
                        self.output_last.at[core, far],
                        self.output_send.at[0],
                        self.output_recv.at[core, far],
                        here.core_device(),
                    ).wait_recv()

        wide = 3 * HEAD
        total = jnp.zeros(self.small_plane.shape, f32)
        for block in range(GROUP):
            made = jnp.zeros(self.qkv_last.shape[2:], f32)
            for far in range(self.fars):
                total = total + self.small_last[block, far]
                made = made + self.qkv_last[block, far].astype(f32)
            columns = slice(block * wide, (block + 1) * wide)
            for head in range(3):
                part = slice(block * wide + head * HEAD, block * wide + (head + 1) * HEAD)
                for kind in range(2):
                    first = head * BLOCK + kind * HEAD
                    self.sums[kind, :, part] = made[:, first : first + HEAD]
            self.sums[2, :, columns] = made[:, 2 * wide : 3 * wide]
        half = self.output_last.shape[3]
        for core in range(2):
            made = self.output_last[core, 0].astype(f32)
            for far in range(1, self.fars):
                made = made + self.output_last[core, far].astype(f32)
            self.sums[3, :, core * half : (core + 1) * half] = made
        pieces = self.rows.shape[1] // 128
        for piece in range(pieces):
            self.rows_sum[:, piece * 128 : (piece + 1) * 128] = total[8 * piece : 8 * piece + 8, :]
        if self.table:
            self.table_out[...] = total[8 * pieces :, :]
        for copy in self.expert_copies():
            copy.wait()
        for copy in self.core_copies() + self.plane_copies():
            copy.wait_send()
        for step in range(1, self.experts):
            for copy in self.line_copies(step, here.expert):
                copy.wait_send()
        for context in range(self.parts):

            @pl.when(jnp.logical_not(self.is_here(context)))
            def _():
                self.output_copy(context).wait_send()


def earlier_call(parts, experts, left, table):
    tall, packed = left.qkv.shape[3:]
    half = left.output.shape[4]
    fars = parts // 2
    small = 8 * (2 * half // 128) + (table or 0)
    shape, scratch = jax.ShapeDtypeStruct, pltpu.VMEM
    specs = [ANY] * 4 + [VMEM] * (4 if table else 3)
    gives = Given(
        shape(left.in_across.shape, bf16),
        shape(left.in_across.shape, bf16),
        shape(left.out_across.shape, bf16),
        shape(left.out_across.shape, bf16),
        shape((4, tall, 2 * half), f32),
        shape((8, 2 * half), f32),
        shape((table, 128), f32) if table else None,
    )
    needs = Needed(
        small=scratch((small, 128), f32),
        qkv_core=scratch((2, parts, experts, tall, packed), bf16),
        output_core=scratch((parts, experts, tall, half), bf16),
        small_core=scratch((small, 128), f32),
        qkv_line=scratch((experts, 2, parts, tall, packed), bf16),
        output_line=scratch((experts, parts, tall, half), bf16),
        small_line=scratch((small, 128), f32),
        qkv_came=scratch((experts, 2, parts, tall, packed), bf16),
        output_came=scratch((experts, parts, tall, half), bf16),
        small_came=scratch((experts, small, 128), f32),
        qkv_plane=scratch((2, parts, tall, packed), bf16),
        output_plane=scratch((parts, tall, half), bf16),
        small_plane=scratch((small, 128), f32),
        qkv_last=scratch((GROUP, fars, tall, packed), bf16),
        output_last=scratch((2, fars, tall, half), bf16),
        small_last=scratch((GROUP, fars, small, 128), f32),
        expert_send=DMA((4, 2)),
        expert_recv=DMA((4, 2)),
        core_send=DMA((4,)),
        core_recv=DMA((4,)),
        line_send=DMA((3, experts - 1)),
        line_recv=DMA((3, experts - 1)),
        plane_send=DMA((2, fars, GROUP)),
        plane_recv=DMA((2, fars, GROUP)),
        output_send=DMA((parts,)),
        output_recv=DMA((2, fars)),
    )
    given_specs = [ANY] * 4 + [VMEM] * (3 if table else 2)
    return specs, gives, given_specs, needs


def finish_kernel(parts, experts, table, last, others, *refs):
    here = Place(parts, experts)
    swap = None
    if last:
        grad, *refs = refs
        *refs, grad_low, grad_came, send, recv = refs
    takes = 8 if table else 7
    taken, refs = refs[:takes], refs[takes:]
    if others:
        loads_from, refs = refs[: 2 + 6 * others], refs[2 + 6 * others :]
    if last:
        d_tokens, *refs = refs
        swap = Swap(here, [(grad_low, grad_came)], send, recv)
    if others:
        sums, rows_sum, table_out, final_in, final_out, *refs = refs
        *refs, in_part, in_whole, out_whole, out_part = refs
        *refs, load_sem = refs
        refs, loads_to = refs[: -2 - 6 * others], refs[-2 - 6 * others :]
        given = [in_part, in_whole, out_whole, out_part, sums, rows_sum, table_out]
        loads = [
            pltpu.make_async_copy(source, target, load_sem.at[index])
            for index, (source, target) in enumerate(zip(loads_from, loads_to, strict=True))
        ]
        for load in loads:
            load.start()
    else:
        given, refs = refs[: takes - 1], refs[takes - 1 :]
    earlier = Earlier(parts, experts, table, taken, given, refs)
    all_here = here.greet(plane=True, swap=last)
    if last:
        grad_low[...] = grad[...].astype(bf16)
    all_here()
    earlier.begin(here, (0, 1, 2))
    if last:
        swap.start((0,))
    earlier.pass_line()

    def total(target, own, one, other):
        made = own[0].astype(f32) + one[0].astype(f32) + other[0].astype(f32)
        target[...] = made.astype(bf16)

    if others:
        for load in loads:
            load.wait()
        for layer in range(others):
            own_in, part_in, whole_in, own_out, part_out, whole_out = loads_to[2 + 6 * layer : 8 + 6 * layer]
            total(final_in.at[1 + layer], own_in, part_in, whole_in)
            total(final_out.at[1 + layer], own_out, part_out, whole_out)
    earlier.pass_plane((3,))
    earlier.finish()
    if others:
        total(final_in.at[0], loads_to[0], in_part, in_whole)
        total(final_out.at[0], loads_to[1], out_part, out_whole)
    if last:
        swap.wait((0,))
        d_tokens[...] = grad_came[...].astype(f32)
        swap.drain()


def finish(left, table, number, grad=None, others=()):
    parts, experts = lax.axis_size("context"), lax.axis_size("expert")
    specs, gives, given_specs, needs = earlier_call(parts, experts, left, table)
    last = grad is not None
    shape, scratch = jax.ShapeDtypeStruct, pltpu.VMEM
    loaded, more_scratch, finals = [], [], []
    if others:
        loaded = [left.in_own, left.out_own]
        for own, done in others:
            loaded += [own.in_own, done.in_from_across, done.in_from_beside]
            loaded += [own.out_own, done.out_from_beside, done.out_from_across]
        more_scratch = [scratch(item.shape, bf16) for item in loaded] + [DMA((len(loaded),))]
        more_scratch += [scratch(item.shape, bf16) for item in gives[:4]]
        finals = [shape((1 + len(others),) + item.shape[1:], bf16) for item in loaded[:2]]
        gives, given_specs = gives[4:], given_specs[4:]
    given = pl.pallas_call(
        functools.partial(finish_kernel, parts, experts, table, last, len(others)),
        out_shape=([shape(grad.shape, f32)] if last else []) + present(gives) + finals,
        in_specs=[VMEM] * last + specs + [ANY] * len(loaded),
        out_specs=[VMEM] * last + given_specs + [VMEM] * len(finals),
        scratch_shapes=list(needs)
        + more_scratch
        + ([scratch(grad.shape, bf16)] * 2 + [DMA((1,)), DMA((1,))] if last else []),
        compiler_params=pltpu.CompilerParams(
            collective_id=number, has_side_effects=True, vmem_limit_bytes=60 * 2**20
        ),
        name="finish",
    )(*([grad] if last else []), *present(taken_from(left, table)), *loaded)
    if others:
        return Given(None, None, None, None, *given[1:4]), given[0], given[4:]
    return Given(*given[last:]), given[0], None


def backward_and_earlier(layer, parts, experts, counts, earlier_bias, table, *refs):
    own_in, takes, own_out, gives, needs, last = counts
    own_scratch = len(refs) - own_in - takes - own_out - gives - needs - 5 * last
    cuts = np.cumsum([0, own_in, takes, last, own_out, gives, last, own_scratch, needs, 3 * last])
    pieces = [refs[a:b] for a, b in zip(cuts[:-1], cuts[1:], strict=True)]
    earlier = Earlier(parts, experts, None, pieces[1], pieces[4], pieces[7]) if takes else None
    backward_kernel(
        layer,
        parts,
        experts,
        *pieces[0],
        *pieces[3],
        *pieces[6],
        earlier=earlier,
        earlier_bias=earlier_bias,
        table=table,
        last=pieces[2] + pieces[5] + pieces[8] if last else None,
    )


def backward_kernel(
    layer,
    parts,
    experts,
    grad,
    x,
    gain_attn,
    gain_moe,
    w_router,
    select,
    chosen,
    bias_hbm,
    bias_before,
    turned_hbm,
    query_hbm,
    pair_hbm,
    merged_hbm,
    log_total_hbm,
    middle,
    router,
    picked,
    arrived,
    arrived_more,
    before_hbm,
    w_qkv_hbm,
    w_output_hbm,
    w_in_hbm,
    w_out_hbm,
    grad_next,
    in_across,
    in_beside,
    in_own,
    out_across,
    out_beside,
    out_own,
    grad_qkv_out,
    grad_output,
    grad_bias_out,
    grad_rows,
    bias,
    turned,
    query,
    pair,
    merged,
    log_total,
    grad_qkv,
    grad_bias,
    grad_in,
    grad_out,
    core_in,
    core_out,
    second_in,
    second_out,
    output_sum,
    w_qkv,
    w_output,
    slots,
    slots_more,
    arrived_grad,
    arrived_grad_more,
    answer,
    answer_more,
    returned,
    returned_more,
    given_grad,
    branches,
    query_grad,
    pair_sent,
    pair_recv,
    made_grad,
    normed_sent,
    normed_recv,
    load_sem,
    slot_send,
    slot_recv,
    back_send,
    back_recv,
    group_send,
    group_recv,
    part_send,
    part_recv,
    merge_send,
    merge_recv,
    core_send,
    core_recv,
    second_send,
    second_recv,
    store_sem,
    earlier=None,
    earlier_bias=False,
    last=None,
    table=None,
):
    here = Place(parts, experts)
    heads = 3
    wide = heads * HEAD
    block = here.block
    fars = parts // 2
    side, level = div(here.dp, 2), rem(here.context, 2)
    across, beside = here.group_device(here.flipped(1)), here.group_device(here.flipped(2))
    own_in, own_out = grad_in.at[2 * side + here.core], grad_out.at[2 * side + here.core]

    def to_core(turns=(0, 1)):
        made = []
        for at in turns:
            there = 2 * at + 1 - here.core
            for kind, (source, target) in enumerate(((grad_in, core_in), (grad_out, core_out))):
                sems = core_send.at[kind, at], core_recv.at[kind, at]
                made.append(remote(source.at[there], target.at[at], *sems, here.core_device()))
        return made

    def second():
        made = []
        for far in range(fars):
            sems = second_send.at[0, far], second_recv.at[0, far]
            source = grad_in.at[2 * (1 - side) + here.core, 2 * far + 1 - level]
            made.append(remote(source, second_in.at[far], *sems, across))
            sems = second_send.at[1, far], second_recv.at[1, far]
            source = grad_out.at[2 * (1 - side) + here.core, 2 * far + 1 - level]
            made.append(remote(source, second_out.at[far], *sems, beside))
        return made

    def stores(kinds):
        made = []
        there = 2 * (1 - side) + here.core
        for far in range(fars):
            for kind, (source, target) in enumerate(
                (
                    (grad_in.at[there, 2 * far + level], in_across),
                    (own_in.at[2 * far + 1 - level], in_beside),
                    (own_in.at[2 * far + level], in_own),
                    (grad_out.at[there, 2 * far + level], out_across),
                    (own_out.at[2 * far + 1 - level], out_beside),
                    (own_out.at[2 * far + level], out_own),
                )
            ):
                if kind in kinds:
                    made.append(pltpu.make_async_copy(source, target.at[far], store_sem.at[kind, far]))
        return made

    def add(target, source):
        target[...] = (target[...].astype(f32) + source[...].astype(f32)).astype(bf16)
    later = [
        pltpu.make_async_copy(source, target, load_sem.at[6 + index])
        for index, (source, target) in enumerate(
            (
                (w_qkv_hbm, w_qkv),
                (turned_hbm, turned),
                (query_hbm, query),
                (pair_hbm, pair),
                (merged_hbm, merged),
                (log_total_hbm, log_total),
                (bias_hbm, bias),
                (bias_before, grad_bias),
            )[: 8 if earlier_bias else 7]
        )
    ]
    for head in range(heads):
        rows = pl.ds(pl.multiple_of(block * wide + head * HEAD, HEAD), HEAD)
        target = w_output.at[head * BLOCK + HEAD : (head + 1) * BLOCK]
        later.append(pltpu.make_async_copy(w_output_hbm.at[layer, rows], target, load_sem.at[3 + head]))

    all_here = here.greet(plane=earlier is not None, swap=last is not None)
    slots, arrived_grad = (slots, slots_more), (arrived_grad, arrived_grad_more)
    answer, returned = (answer, answer_more), (returned, returned_more)
    spans = halves((arrived, arrived_more))

    def hand_slots(half, step, source):
        return remote(
            slots[half].at[here.expert_other(step)],
            arrived_grad[half].at[source],
            slot_send.at[half, step - 1],
            slot_recv.at[half, step - 1],
            {"expert": here.expert_other(step)},
        )

    def hand_answer(half, step, source):
        return remote(
            answer[half].at[here.expert_other(step)],
            returned[half].at[source],
            back_send.at[half, step - 1],
            back_recv.at[half, step - 1],
            {"expert": here.expert_other(step)},
        )

    if last:
        x_last, out, out_low, send, recv = last
        out_low[...] = x_last[...].astype(bf16)
        swap = Swap(here, [(out_low, out)], send, recv)

    def experts_phase(w_in, w_out, hidden, slope, before_grad, total, turned_given):
        loads = [
            pltpu.make_async_copy(before_hbm, slope, load_sem.at[2]),
            pltpu.make_async_copy(w_out_hbm.at[layer, 0], w_out, load_sem.at[0]),
            pltpu.make_async_copy(w_in_hbm.at[layer, 0], w_in, load_sem.at[1]),
        ]
        for load in loads + later:
            load.start()
        for head in range(heads):
            w_output[head * BLOCK : head * BLOCK + HEAD, :] = jnp.zeros((HEAD, w_output.shape[1]), bf16)
        came = grad[...].astype(f32)
        chances = router[...]
        gate = jnp.sum(chances * chosen[...], axis=-1, keepdims=True)
        gate_grad = jnp.sum(came * picked[...].astype(f32), axis=-1, keepdims=True)
        answer_grad = (gate * came).astype(bf16)
        for half, (low, high) in enumerate(spans):
            for expert in range(experts):
                slots[half][expert] = dot(select[expert, low:high], answer_grad).astype(bf16)
        all_here()
        if earlier:
            earlier.begin(here)

        for half in range(2):
            for step in range(1, experts):
                hand_slots(half, step, here.expert).start()
            arrived_grad[half][here.expert] = slots[half][here.expert]
        hidden_width = w_in.shape[1]

        loads[0].wait()

        @pl.loop(0, hidden_width // FCHUNK)
        def _(index):
            columns = pl.ds(pl.multiple_of(index * FCHUNK, FCHUNK), FCHUNK)
            made, steep = gelu_parts(slope[:, columns])
            hidden[:, columns] = made.astype(bf16)
            slope[:, columns] = steep

        mid = middle[...]
        scale = root_scale(mid)
        unit = mid * scale
        moe_in = unit * gain_moe[layer : layer + 1, :]
        chance_grad = chosen[...] * gate_grad
        logit_grad = chances * (chance_grad - jnp.sum(chances * chance_grad, axis=-1, keepdims=True))
        router_grad = lax.dot_general(
            logit_grad, moe_in, (((0,), (0,)), ((), ())), precision=highest, preferred_element_type=f32
        )
        grad_rows[...] = router_grad[:8, :]
        moe_part = jnp.dot(
            logit_grad, widened(w_router, layer), precision=highest, preferred_element_type=f32
        )
        given = jnp.concatenate([joined(arrived), joined(arrived_more)], axis=0)
        turned_given[...] = given.astype(f32).T.astype(bf16)
        total[...] = jnp.zeros_like(total)
        loads[1].wait()
        loads[2].wait()
        for half, (low, high) in enumerate(spans):
            for step in range(1, experts):
                hand_slots(half, step, rem(here.expert + experts - step, experts)).wait_recv()
            rows = slice(experts * low, experts * high)
            given_grad[rows, :] = joined(arrived_grad[half])

            @pl.loop(0, hidden_width // FCHUNK)
            def _(index, rows=rows):
                columns = pl.ds(pl.multiple_of(index * FCHUNK, FCHUNK), FCHUNK)
                hidden_grad = dot_nt(given_grad[rows, :], w_out[columns, :])
                low_grad = (hidden_grad * slope[rows, columns]).astype(bf16)
                before_grad[rows, columns] = low_grad
                total[rows, :] += dot_nt(low_grad, w_in[:, columns])

            for expert in range(experts):
                first = experts * low + expert * (high - low)
                answer[half][expert] = total[first : first + high - low, :].astype(bf16)
            for step in range(1, experts):
                hand_answer(half, step, here.expert).start()
            returned[half][here.expert] = answer[half][here.expert]
        if last:
            swap.start((0,))
        rows_in, rows_out = grad_in.shape[2], grad_out.shape[2]
        columns_in = grad_in.shape[3] // GROUP
        for turn in range(4):
            there = 2 * (turn % 2) + (1 - here.core if turn < 2 else here.core)
            rows = pl.ds(pl.multiple_of(there * (parts * rows_in), parts * rows_in), parts * rows_in)
            for piece in range(GROUP):
                columns = slice(piece * columns_in, (piece + 1) * columns_in)
                made = dot(turned_given[rows, :], before_grad[:, columns])
                for at in range(parts):
                    grad_in[there, at, :, columns] = made[at * rows_in : (at + 1) * rows_in, :].astype(bf16)
            columns = pl.ds(pl.multiple_of(there * (parts * rows_out), parts * rows_out), parts * rows_out)
            made = dot_tn(hidden[:, columns], given_grad[...])
            for at in range(parts):
                grad_out[there, at] = made[at * rows_out : (at + 1) * rows_out, :].astype(bf16)
            if turn < 2:
                for copy in to_core((turn,)):
                    copy.start()

        moe_grad = moe_part
        for half, (low, high) in enumerate(spans):
            for step in range(1, experts):
                hand_answer(half, step, rem(here.expert + experts - step, experts)).wait_recv()
            for expert in range(experts):
                moe_grad = moe_grad + dot_tn(select[expert, low:high], returned[half][expert])
        grad_rows[4:5, :] = jnp.sum(moe_grad * unit, axis=0, keepdims=True)
        scaled = moe_grad * gain_moe[layer : layer + 1, :]
        mid_grad = came + scale * (scaled - unit * jnp.mean(unit * scaled, axis=-1, keepdims=True))
        branches[block] = mid_grad.astype(bf16)
        return mid_grad

    slot_rows = given_grad.shape[0]
    mid_grad = pl.run_scoped(
        experts_phase,
        pltpu.VMEM(w_in_hbm.shape[2:], bf16),
        pltpu.VMEM(w_out_hbm.shape[2:], bf16),
        pltpu.VMEM(before_hbm.shape, bf16),
        pltpu.VMEM(before_hbm.shape, f32),
        pltpu.VMEM(before_hbm.shape, bf16),
        pltpu.VMEM((slot_rows, grad.shape[1]), f32),
        pltpu.VMEM((grad.shape[1], slot_rows), bf16),
    )

    gather, relay = gathering(here, branches, group_send, group_recv, earlier is None)
    for flip in (1, 2):
        gather(flip, block).start()
    if earlier is None:
        for flip in (1, 2):
            relay(flip, block).start()
    for turn in range(2):
        for copy in to_core((turn,)):
            copy.wait_recv()
        for at in range(parts):
            add(grad_in.at[2 * turn + here.core, at], core_in.at[turn, at])
            add(grad_out.at[2 * turn + here.core, at], core_out.at[turn, at])
    if earlier:
        for flip in (1, 2):
            gather(flip, here.flipped(flip)).wait_recv()
            relay(flip, here.flipped(flip)).start()
    for copy in second() + stores((0, 2, 4, 5)):
        copy.start()
    if earlier:
        earlier.pass_line()
    for load in later:
        load.wait()
    def hand_pair(step, source):
        return remote(
            pair_sent.at[step - 1],
            pair_recv.at[step - 1],
            part_send.at[step - 1],
            part_recv.at[step - 1],
            here.part_device(here.part_other(step)),
        )

    def attention_phase(pair_grad):
        lane = lanes(BLOCK, BLOCK)
        if not earlier_bias:
            grad_bias[...] = jnp.zeros_like(grad_bias)
        for flip in range(GROUP):
            mine = here.flipped(flip)
            if flip == 3:
                for other in (1, 2):
                    relay(other, mine).wait_recv()
            elif flip and earlier is None:
                gather(flip, mine).wait_recv()
            wanted = dot_nt(branches[mine], w_output[...])
            wanted_low = wanted.astype(bf16)
            wanted = wanted_low.astype(f32)
            turned_rows = jnp.concatenate([query[mine].astype(f32).T, wanted.T], axis=1).astype(bf16)
            products = wanted * merged[mine]
            for head in range(heads):
                columns = slice(head * BLOCK, (head + 1) * BLOCK)
                rows = jnp.concatenate([query[mine, :, columns], wanted_low[:, columns]], axis=0)
                delta = jnp.sum(products[:, columns], axis=-1, keepdims=True)
                log_sum = log_total[mine][:, head : head + 1]
                gathered = jnp.zeros((BLOCK, BLOCK), f32)
                for part in range(parts):
                    both = pair[part, :, :, columns].reshape(GROUP * BLOCK, BLOCK)
                    raw = dot_nt(rows, both)
                    upper, lower = [], []
                    for of_block in range(GROUP):
                        inside = slice(of_block * BLOCK, (of_block + 1) * BLOCK)
                        place = here.bias_index(part, of_block, mine)
                        weight = jnp.exp(raw[:BLOCK, inside] + (bias[head, place] - log_sum))
                        score_grad = weight * (raw[BLOCK:, inside] - delta)
                        grad_bias[head, place] += score_grad
                        upper.append(score_grad.astype(bf16))
                        lower.append(weight.astype(bf16))
                    upper = jnp.concatenate(upper, axis=1)
                    stacked = jnp.concatenate([upper, jnp.concatenate(lower, axis=1)], axis=0)
                    gathered = gathered + dot(upper, both)
                    more = dot(turned_rows[columns], stacked)
                    if flip:
                        pair_grad[part, columns, :] += more
                    else:
                        pair_grad[part, columns, :] = more
                query_grad[mine, :, columns] = jnp.where(lane < HEAD, gathered, 0.0).astype(bf16)
        for step in range(1, parts):
            pair_sent[step - 1] = pair_grad[here.part_other(step)].astype(bf16)
            hand_pair(step, 0).start()
        summed = pair_grad[here.part]
        for step in range(1, parts):
            hand_pair(step, 0).wait_recv()
            summed = summed + pair_recv[step - 1].astype(f32)
        summed = summed.T.astype(bf16)
        for of_block in range(GROUP):
            made_grad[of_block, :, : 2 * wide] = summed[of_block * BLOCK : (of_block + 1) * BLOCK, :]
            made_grad[of_block, :, 2 * wide :] = dot(
                query_grad[of_block], half_select(3 * BLOCK, 2 * BLOCK, 0)
            ).astype(bf16)

    pl.run_scoped(attention_phase, pltpu.VMEM((parts, 2 * wide, GROUP * BLOCK), f32))

    def hand_normed(flip):
        return remote(
            normed_sent.at[flip - 1],
            normed_recv.at[flip - 1],
            merge_send.at[flip - 1],
            merge_recv.at[flip - 1],
            here.group_device(here.flipped(flip)),
        )

    for flip in (3, 1, 2):
        normed_sent[flip - 1] = dot_nt(made_grad[here.flipped(flip)], w_qkv[...]).astype(bf16)
        hand_normed(flip).start()
    normed_grad = dot_nt(made_grad[block], w_qkv[...])
    if earlier:
        earlier.pass_plane()
    both = made_grad[...].reshape(GROUP * BLOCK, made_grad.shape[2])
    rows = turned.shape[0] // GROUP
    tall = grad_qkv.shape[3]
    for there in range(GROUP):
        made = dot(turned[there * rows : (there + 1) * rows, :], both)
        for at in range(parts):
            for expert in range(experts):
                first = (at * experts + expert) * tall
                grad_qkv[there, at, expert] = made[first : first + tall, :].astype(bf16)
    made = dot_tn(
        merged[...].reshape(GROUP * BLOCK, 3 * BLOCK).astype(bf16),
        branches[...].reshape(GROUP * BLOCK, branches.shape[2]),
    )
    for head in range(heads):
        output_sum[head * HEAD : (head + 1) * HEAD, :] = made[head * BLOCK + HEAD : (head + 1) * BLOCK, :]
    stores_late = [pltpu.make_async_copy(grad_qkv, grad_qkv_out, store_sem.at[6, 0])]
    if table:
        grad_bias_out[...] = table_sum(table, grad_bias, here.block)
    else:
        stores_late.append(pltpu.make_async_copy(grad_bias, grad_bias_out, store_sem.at[7, 0]))
    for store in stores_late:
        store.start()
    half = grad_output.shape[4]
    for at in range(parts):
        for expert in range(experts):
            first = (at * experts + expert) * tall
            for turn in range(2):
                piece = output_sum[first : first + tall, turn * half : (turn + 1) * half]
                grad_output[turn, at, expert] = piece.astype(bf16)
    for copy in second():
        copy.wait_recv()
    for far in range(fars):
        add(own_in.at[2 * far + 1 - level], second_in.at[far])
        add(grad_out.at[2 * (1 - side) + here.core, 2 * far + level], second_out.at[far])
    for copy in stores((1, 3)):
        copy.start()
    value = x[...]
    scale = root_scale(value)
    unit = value * scale
    for flip in (1, 2, 3):
        hand_normed(flip).wait_recv()
        normed_grad = normed_grad + normed_recv[flip - 1].astype(f32)
    grad_rows[5:6, :] = jnp.sum(normed_grad * unit, axis=0, keepdims=True)
    scaled = normed_grad * gain_attn[layer : layer + 1, :]
    grad_next[...] = mid_grad + scale * (scaled - unit * jnp.mean(unit * scaled, axis=-1, keepdims=True))
    if earlier:
        earlier.finish()
    if last:
        swap.wait((0,))
        swap.drain()
    for copy in stores(range(6)) + stores_late:
        copy.wait()
    for copy in to_core() + second():
        copy.wait_send()
    for flip in (1, 2):
        gather(flip, block).wait_send()
        relay(flip, here.flipped(flip)).wait_send()
    for flip in (1, 2, 3):
        hand_normed(flip).wait_send()
    for step in range(1, parts):
        hand_pair(step, 0).wait_send()
    for step in range(1, experts):
        for half in range(2):
            hand_slots(half, step, here.expert).wait_send()
            hand_answer(half, step, here.expert).wait_send()


VMEM = pl.BlockSpec(memory_space=pltpu.VMEM)
ANY = pl.BlockSpec(memory_space=pl.ANY)
DMA = pltpu.SemaphoreType.DMA


def forward_layer(layer, layers, begin, going, weights):
    parts, experts = lax.axis_size("context"), lax.axis_size("expert")
    w_in = weights[7]
    width, hidden = w_in.shape[2:]
    count = BLOCK
    wide, packed = 3 * HEAD, 5 * BLOCK
    room = count * 5 // (4 * experts)
    cut = room // 32 * 16
    shape, scratch = jax.ShapeDtypeStruct, pltpu.VMEM
    first = begin is not None
    gives = Saved(
        x=shape((count, width), f32),
        grad=shape((count, width), bf16),
        marks=shape((8, count), jnp.int32),
        bias=shape((3, 5, BLOCK, BLOCK), f32),
        select=shape((experts, room, count), bf16),
        chosen=shape((count, BLOCK), f32),
        w_qkv=shape((width, packed), bf16),
        turned=shape((width, GROUP * count), bf16),
        query=shape((GROUP, count, 3 * BLOCK), bf16),
        pair=shape((parts, GROUP, count, 2 * wide), bf16),
        merged=shape((GROUP, count, 3 * BLOCK), f32),
        log_total=shape((GROUP, count, BLOCK), f32),
        middle=shape((count, width), f32),
        router=shape((count, BLOCK), f32),
        picked=shape((count, width), bf16),
        arrived=shape((experts, cut, width), bf16),
        arrived_more=shape((experts, room - cut, width), bf16),
        before=shape((experts * room, hidden), f32),
        x_next=shape((count, width), f32),
    )
    far = Saved(*[VMEM] * len(gives))._replace(
        w_qkv=ANY, turned=ANY, query=ANY, pair=ANY, merged=ANY, log_total=ANY, before=ANY
    )
    skipped = 0 if first else 4
    start = list(begin) if first else [going.x_next, going.marks, going.bias]
    start_specs = [VMEM] * 4 + [pl.BlockSpec(memory_space=pltpu.SMEM)] if first else [VMEM] * 3
    made = pl.pallas_call(
        functools.partial(forward_kernel, layer, layers, parts, experts, first),
        out_shape=list(gives[skipped:]),
        in_specs=start_specs + [VMEM] * 3 + [ANY] * 6,
        out_specs=list(far[skipped:]),
        scratch_shapes=[
            scratch((width, packed), bf16),
            scratch((width, GROUP * count), bf16),
            scratch((GROUP, count, 3 * BLOCK), bf16),
            scratch((parts, GROUP, count, 2 * wide), bf16),
            scratch((GROUP, count, 3 * BLOCK), f32),
            scratch((GROUP, count, BLOCK), f32),
            scratch((GROUP, count, wide), bf16),
            scratch((experts * room, hidden), f32),
            scratch((GROUP, count, width), bf16),
            scratch((width, 6 * BLOCK), bf16),
            scratch((width, width), bf16),
            scratch((width, hidden), bf16),
            scratch((hidden, width), bf16),
            scratch((parts * GROUP, count, BLOCK), f32),
            scratch((GROUP, count, wide), bf16),
            scratch((experts, cut, width), bf16),
            scratch((experts, room - cut, width), bf16),
            scratch((experts * room, width), f32),
            *[scratch((experts, cut, width), bf16), scratch((experts, room - cut, width), bf16)] * 2,
            DMA((6,)),
            DMA((7,)),
            DMA((4,)),
            DMA((4,)),
            DMA((parts - 1, GROUP)),
            DMA((parts - 1, GROUP)),
            DMA((3,)),
            DMA((3,)),
            DMA((2, experts - 1)),
            DMA((2, experts - 1)),
            DMA((2, experts - 1)),
            DMA((2, experts - 1)),
        ]
        + ([scratch((count, width), bf16), scratch((8, count), jnp.int32), DMA((3,)), DMA((3,))] if first else []),
        compiler_params=pltpu.CompilerParams(
            collective_id=layer, has_side_effects=True, vmem_limit_bytes=60 * 2**20
        ),
        name="layer_forward",
    )(*start, *weights)
    return Saved(*([] if first else [going.x_next, going.grad, going.marks, going.bias]), *made)


def backward_layer(layer, layers, grad, saved, bias_before, left, weights, x_last, table):
    gain_attn, gain_moe, w_router, _, _, _, w_output, w_in, w_out = weights
    w_qkv, select, bias = saved.w_qkv, saved.select, saved.bias
    count, width = grad.shape
    parts, experts = lax.axis_size("context"), lax.axis_size("expert")
    wide = 3 * HEAD
    room = select.shape[1]
    hidden = w_in.shape[3]
    shape = jax.ShapeDtypeStruct
    scratch = pltpu.VMEM
    span = GROUP * count
    rows_in, rows_out = width // (GROUP * parts), hidden // (GROUP * parts)
    tall = rows_in // experts
    fars = parts // 2
    specs, gives, given_specs, needs = earlier_call(parts, experts, left, None) if left else ([], [], [], [])
    taken = present(taken_from(left, None)) if left else []
    gives = present(gives)
    cut = saved.arrived.shape[1]
    own_gives = Own(
        grad_next=shape((count, width), f32),
        in_across=shape((fars, rows_in, hidden), bf16),
        in_beside=shape((fars, rows_in, hidden), bf16),
        in_own=shape((fars, rows_in, hidden), bf16),
        out_across=shape((fars, rows_out, width), bf16),
        out_beside=shape((fars, rows_out, width), bf16),
        out_own=shape((fars, rows_out, width), bf16),
        qkv=shape((GROUP, parts, experts, tall, w_qkv.shape[1]), bf16),
        output=shape((2, parts, experts, tall, width // 2), bf16),
        bias=shape((table, 128) if table else bias.shape, f32),
        rows=shape((8, width), f32),
    )
    own_specs = [VMEM] + [ANY] * 7 + [VMEM, VMEM if table else ANY, VMEM]
    last = int(x_last is not None)
    counts = (24, len(taken), len(own_gives), len(gives), len(needs), last)
    given = pl.pallas_call(
        functools.partial(backward_and_earlier, layer, parts, experts, counts, bias_before is not None, table),
        out_shape=[*own_gives, *gives] + [shape(grad.shape, bf16)] * last,
        in_specs=[VMEM] * 7 + [ANY] * 7 + [VMEM] * 5 + [ANY] * 5 + specs + [VMEM] * last,
        out_specs=own_specs + given_specs + [VMEM] * last,
        scratch_shapes=[
            scratch(bias.shape, f32),
            scratch(saved.turned.shape, bf16),
            scratch(saved.query.shape, bf16),
            scratch(saved.pair.shape, bf16),
            scratch(saved.merged.shape, f32),
            scratch(saved.log_total.shape, f32),
            scratch((GROUP, parts, experts, tall, w_qkv.shape[1]), bf16),
            scratch(bias.shape, f32),
            scratch((GROUP, parts, rows_in, hidden), bf16),
            scratch((GROUP, parts, rows_out, width), bf16),
            scratch((2, parts, rows_in, hidden), bf16),
            scratch((2, parts, rows_out, width), bf16),
            scratch((fars, rows_in, hidden), bf16),
            scratch((fars, rows_out, width), bf16),
            scratch((wide, width), f32),
            scratch((width, w_qkv.shape[1]), bf16),
            scratch((3 * BLOCK, width), bf16),
            *[scratch((experts, cut, width), bf16), scratch((experts, room - cut, width), bf16)] * 4,
            scratch((experts * room, width), bf16),
            scratch((GROUP, count, width), bf16),
            scratch((GROUP, count, 3 * BLOCK), bf16),
            scratch((parts - 1, 2 * wide, span), bf16),
            scratch((parts - 1, 2 * wide, span), bf16),
            scratch((GROUP, count, w_qkv.shape[1]), bf16),
            scratch((GROUP - 1, count, width), bf16),
            scratch((GROUP - 1, count, width), bf16),
            DMA((14,)),
            DMA((2, experts - 1)),
            DMA((2, experts - 1)),
            DMA((2, experts - 1)),
            DMA((2, experts - 1)),
            DMA((4,)),
            DMA((4,)),
            DMA((parts - 1,)),
            DMA((parts - 1,)),
            DMA((3,)),
            DMA((3,)),
            DMA((2, 2)),
            DMA((2, 2)),
            DMA((2, fars)),
            DMA((2, fars)),
            DMA((8, fars)),
            *needs,
            *([scratch(grad.shape, bf16), DMA((1,)), DMA((1,))] if last else []),
        ],
        compiler_params=pltpu.CompilerParams(
            collective_id=layers + layer,
            has_side_effects=True,
            vmem_limit_bytes=(60 if parts <= 2 else 63) * 2**20,
        ),
        name="layer_backward",
    )(
        grad,
        saved.x,
        gain_attn,
        gain_moe,
        w_router,
        select,
        saved.chosen,
        bias,
        bias if bias_before is None else bias_before,
        saved.turned,
        saved.query,
        saved.pair,
        saved.merged,
        saved.log_total,
        saved.middle,
        saved.router,
        saved.picked,
        saved.arrived,
        saved.arrived_more,
        saved.before,
        w_qkv,
        w_output,
        w_in,
        w_out,
        *taken,
        *([x_last] if last else []),
    )
    own, sums = given[: len(own_gives)], given[len(own_gives) : len(own_gives) + len(gives)]
    return Own(*own), Given(*sums) if sums else None, given[-1]


def on_device(
    tokens,
    w_query,
    w_key,
    w_value,
    w_output,
    rel_bias,
    gain_attn,
    gain_moe,
    w_router,
    w_in,
    w_out,
    routes,
    kept,
    cotangent,
):
    experts = w_router.shape[2]
    layers = w_query.shape[0]
    parts = lax.axis_size("context")
    weights = (gain_attn, gain_moe, jnp.swapaxes(w_router, 1, 2), w_key, w_value, w_query, w_output, w_in, w_out)
    saved, going = [], None
    for layer in range(layers):
        begin = (tokens[0], cotangent[0], routes[:, 0, :, 0], kept[:, 0], rel_bias) if layer == 0 else None
        going = forward_layer(layer, layers, begin, going, weights)
        saved.append(going)
    grad, bias_grad = saved[0].grad, None
    left, lefts, sums = None, [], []
    for layer in reversed(range(layers)):
        x_last = going.x_next if layer == layers - 1 else None
        carried = left if parts == 2 else None
        own, done, swapped = backward_layer(layer, layers, grad, saved[layer], bias_grad, carried, weights, x_last, None if layer else rel_bias.shape[0])
        if x_last is not None:
            out = swapped[None]
        if done:
            sums.insert(0, done)
        grad, bias_grad = own.grad_next, own.bias
        left = own
        lefts.insert(0, left)
        if layer == 0:
            others = list(zip(lefts[1:], sums, strict=True)) if parts == 2 else ()
            done, d_tokens, finals = finish(left, rel_bias.shape[0], 2 * layers, grad, others)
            sums.insert(0, done)
        elif parts > 2:
            sums.insert(0, finish(left, None, 2 * layers + layer)[0])

    def experts_sum(own, from_across, from_beside):
        total = own.astype(f32) + from_across.astype(f32) + from_beside.astype(f32)
        if parts == 2:
            return total[0]
        groups = [[2 * far + level for far in range(parts // 2)] for level in range(2)]
        total = lax.psum_scatter(total.astype(bf16), "context", scatter_dimension=0, axis_index_groups=groups)
        return total.astype(f32)

    if finals:
        grad_in, grad_out = (item.astype(f32) for item in finals)
    else:
        grad_in = jnp.stack(
            [experts_sum(a.in_own, b.in_from_across, b.in_from_beside) for a, b in zip(lefts, sums)]
        )
        grad_out = jnp.stack(
            [experts_sum(a.out_own, b.out_from_across, b.out_from_beside) for a, b in zip(lefts, sums)]
        )
    rank = (lax.axis_index("dp") * parts + lax.axis_index("context")) * experts + lax.axis_index("expert")
    tall = sums[0].sums.shape[1]
    rows = jnp.stack([item.rows_sum for item in sums])
    rows = lax.dynamic_slice_in_dim(rows, rank * tall, tall, 2)
    key_out, value_out, query_out, output_out = (
        jnp.stack([item.sums[kind] for item in sums]) for kind in range(4)
    )
    return (
        out,
        d_tokens[None],
        query_out,
        key_out,
        value_out,
        output_out,
        sums[0].table_out[:, : rel_bias.shape[1]],
        rows[:, 5],
        rows[:, 4],
        jnp.swapaxes(rows[:, :experts], 1, 2),
        grad_in[:, None],
        grad_out[:, None],
    )


def solution(mesh):
    in_specs = (
        P("dp", ("context", "expert"), None),
        P(),
        P(),
        P(),
        P(),
        P(),
        P(),
        P(),
        P(),
        P(None, "expert", None, None),
        P(None, "expert", None, None),
        P(None, "dp", ("context", "expert"), None),
        P(None, "dp", ("context", "expert")),
        P("dp", ("context", "expert"), None),
    )
    out_specs = (
        P("dp", ("context", "expert"), None),
        P("dp", ("context", "expert"), None),
        P(None, ("dp", "context", "expert"), None),
        P(None, ("dp", "context", "expert"), None),
        P(None, ("dp", "context", "expert"), None),
        P(None, ("dp", "context", "expert"), None),
        P(),
        P(None, ("dp", "context", "expert")),
        P(None, ("dp", "context", "expert")),
        P(None, ("dp", "context", "expert"), None),
        P(None, "expert", ("dp", "context"), None),
        P(None, "expert", ("dp", "context"), None),
    )
    return jax.shard_map(
        on_device, mesh=mesh, in_specs=in_specs, out_specs=out_specs, check_vma=False
    )
```

```python
import functools
from typing import Any, NamedTuple

import jax
import jax.numpy as jnp
import numpy as np
from jax import lax
from jax.experimental import pallas as pl
from jax.experimental.pallas import tpu as pltpu
from jax.sharding import PartitionSpec as P

highest = lax.Precision.HIGHEST
epsilon = 1e-06
thresholds = (12, 16, 23, 32, 46, 64, 91)
MESH = pl.DeviceIdType.MESH
GROUP = 4
HEAD = 64
BLOCK = 128
FCHUNK = 512
f32, bf16 = jnp.float32, jnp.bfloat16


def div(a, b):
    return lax.div(a, jnp.int32(b))


def rem(a, b):
    return lax.rem(a, jnp.int32(b))


def turned_pair(index):
    return 2 * rem(index, 2) + div(index, 2)


class Place:
    def __init__(self, parts, experts):
        self.parts, self.experts = parts, experts
        self.dp = lax.axis_index("dp")
        self.context = lax.axis_index("context")
        self.expert = lax.axis_index("expert")
        self.core = rem(self.dp, 2)
        self.far = div(self.context, 2)
        self.block = 2 * rem(self.context, 2) + div(self.dp, 2)
        self.part = 2 * self.far + self.core

    def flipped(self, flip):
        low = rem(rem(self.block, 2) + flip % 2, 2)
        high = rem(div(self.block, 2) + flip // 2, 2)
        return 2 * high + low

    def group_device(self, block):
        return {"dp": 2 * rem(block, 2) + self.core, "context": 2 * self.far + div(block, 2)}

    def part_other(self, step):
        return rem(self.part + step, self.parts)

    def part_device(self, part):
        return {
            "dp": self.dp - self.core + rem(part, 2),
            "context": 2 * div(part, 2) + rem(self.context, 2),
        }

    def expert_other(self, step):
        return rem(self.expert + step, self.experts)

    def offset(self, part, block, query_block):
        across = 4 * (block // 2 - div(query_block, 2)) + (block % 2 - rem(query_block, 2))
        part = jnp.int32(part)
        return 8 * (div(part, 2) - self.far) + across + 2 * (rem(part, 2) - self.core)

    def bias_index(self, part, block, query_block):
        offset = self.offset(part, block, query_block)
        return jnp.minimum(jnp.maximum(offset, -2), 2) + 2

    def core_device(self):
        return {"dp": self.dp + 1 - 2 * self.core}

    def plane_others(self):
        made = []
        for step in range(self.parts // 2):
            far = rem(self.far + step, self.parts // 2)
            for flip in range(GROUP):
                if step or flip:
                    other = self.flipped(flip)
                    device = {"dp": 2 * rem(other, 2) + self.core, "context": 2 * far + div(other, 2)}
                    made.append((step, flip, far, other, device))
        return made

    def is_swapped(self):
        return self.dp != turned_pair(self.expert)

    def swap_device(self):
        return {"dp": turned_pair(self.expert), "expert": turned_pair(self.dp)}

    def greet(self, plane=False, swap=False):
        if plane:
            partners = [item[-1] for item in self.plane_others()]
            partners += [{**device, "dp": device.get("dp") + 1 - 2 * self.core} for device in partners]
            partners += [self.core_device()]
        else:
            partners = [self.group_device(self.flipped(flip)) for flip in (1, 2, 3)]
            partners += [self.part_device(self.part_other(step)) for step in range(1, self.parts)]
        partners += [{"expert": self.expert_other(step)} for step in range(1, self.experts)]
        barrier = pltpu.get_barrier_semaphore()
        for partner in partners:
            pl.semaphore_signal(barrier, inc=1, device_id=partner, device_id_type=MESH)
        if swap:

            @pl.when(self.is_swapped())
            def _():
                pl.semaphore_signal(barrier, inc=1, device_id=self.swap_device(), device_id_type=MESH)

        def wait():
            if swap:

                @pl.when(self.is_swapped())
                def _():
                    pl.semaphore_wait(barrier, len(partners) + 1)

                @pl.when(jnp.logical_not(self.is_swapped()))
                def _():
                    pl.semaphore_wait(barrier, len(partners))

            else:
                pl.semaphore_wait(barrier, len(partners))

        return wait


def remote(source, target, send, receive, device):
    return pltpu.make_async_remote_copy(
        src_ref=source,
        dst_ref=target,
        send_sem=send,
        recv_sem=receive,
        device_id=device,
        device_id_type=MESH,
    )


def dot(a, b):
    return jnp.dot(a, b, preferred_element_type=f32)


def dot_nt(a, b):
    return lax.dot_general(a, b, (((1,), (1,)), ((), ())), preferred_element_type=f32)


def dot_tn(a, b):
    return lax.dot_general(a, b, (((0,), (0,)), ((), ())), preferred_element_type=f32)


def root_scale(value):
    return lax.rsqrt(jnp.mean(value * value, axis=-1, keepdims=True) + epsilon)


def lanes(rows, width):
    return lax.broadcasted_iota(jnp.int32, (rows, width), 1)


def gelu_parts(value):
    scale = 0.7978845608028654
    square = value * value
    inner = jnp.tanh(scale * (value + 0.044715 * (square * value)))
    half = 0.5 * (1.0 + inner)
    slope = half + 0.5 * value * (1.0 - inner * inner) * (scale * (1.0 + 3 * 0.044715 * square))
    return value * half, slope


def gelu(value):
    scale = 0.7978845608028654
    return value * (0.5 * (1.0 + jnp.tanh(scale * (value + 0.044715 * (value * value * value)))))


class Swap:
    def __init__(self, here, pairs, send, recv):
        self.here, self.pairs, self.send, self.recv = here, pairs, send, recv

    def copies(self, which):
        made = []
        for index in which:
            source, target = self.pairs[index]
            made.append(remote(source, target, self.send.at[index], self.recv.at[index], self.here.swap_device()))
        return made

    def start(self, which):
        @pl.when(self.here.is_swapped())
        def _():
            for copy in self.copies(which):
                copy.start()

        @pl.when(jnp.logical_not(self.here.is_swapped()))
        def _():
            for index in which:
                source, target = self.pairs[index]
                target[...] = source[...]

    def wait(self, which):
        @pl.when(self.here.is_swapped())
        def _():
            for copy in self.copies(which):
                copy.wait_recv()

    def drain(self):
        @pl.when(self.here.is_swapped())
        def _():
            for copy in self.copies(range(len(self.pairs))):
                copy.wait_send()


def route_tokens(marks, layer, layers, select, chosen):
    experts, room, count = select.shape
    route = marks[layer : layer + 1, :]
    live = marks[layers + layer : layers + layer + 1, :] > 0
    named = lax.broadcasted_iota(jnp.int32, (8, count), 0) == route
    before = lax.broadcasted_iota(jnp.int32, (count, count), 0)
    after = lax.broadcasted_iota(jnp.int32, (count, count), 1)
    named = named.astype(f32)
    ahead = dot(named.astype(bf16), (before < after).astype(f32).astype(bf16))
    rank = jnp.sum(named * ahead, axis=0, keepdims=True)
    slot = lax.broadcasted_iota(jnp.int32, (room, count), 0).astype(f32)
    for expert in range(experts):
        select[expert] = ((slot == rank) & (route == expert) & live).astype(f32).astype(bf16)
    chosen[...] = ((before == route) & live).astype(f32).T


def bucket_block(place, half):
    row = lax.broadcasted_iota(jnp.int32, (BLOCK, BLOCK), 0)
    column = lax.broadcasted_iota(jnp.int32, (BLOCK, BLOCK), 1)
    offset = (place - 2) * BLOCK + column - row
    distance = jnp.abs(offset)
    beyond = 8 + sum((distance >= limit).astype(jnp.int32) for limit in thresholds)
    return jnp.where(distance < 8, distance, beyond) + jnp.where(offset > 0, half, 0)


def bucket_range(place, half):
    return (half, 2 * half) if place == 3 else (0, half if place == 1 else 2 * half)


def make_bias(bias, rel_bias, first):
    half = rel_bias.shape[0] // 2
    for head in range(3):
        bias[head, 0] = jnp.full((BLOCK, BLOCK), rel_bias[half - 1, first + head], f32)
        bias[head, 4] = jnp.full((BLOCK, BLOCK), rel_bias[2 * half - 1, first + head], f32)
    for place in (1, 2, 3):
        buckets = bucket_block(place, half)
        for head in range(3):

            def one(bucket, made, buckets=buckets, head=head):
                return jnp.where(buckets == bucket, rel_bias[bucket, first + head], made)

            bias[head, place] = lax.fori_loop(*bucket_range(place, half), one, jnp.zeros((BLOCK, BLOCK), f32))


def pack_weights(w_qkv, slabs, block):
    wide = 3 * HEAD
    shape = (slabs.shape[1], w_qkv.shape[1])
    row = lax.broadcasted_iota(jnp.int32, shape, 0)
    column = lax.broadcasted_iota(jnp.int32, shape, 1)
    head, inside = column // BLOCK, column % BLOCK
    kind = inside // HEAD
    source = jnp.where(
        column < 2 * wide, 2 * BLOCK * kind + HEAD * head + inside % HEAD, 4 * BLOCK + column - 2 * wide
    )
    source = source + HEAD * rem(block, 2)
    move = ((row == source) & (column < 3 * wide)).astype(f32).astype(bf16)
    w_qkv[...] = dot(slabs[...], move).astype(bf16)


def ones_where(condition):
    return condition.astype(f32).astype(bf16)


def query_spread(rows, columns):
    row = lax.broadcasted_iota(jnp.int32, (rows, columns), 0)
    column = lax.broadcasted_iota(jnp.int32, (rows, columns), 1)
    return ones_where((column % BLOCK < HEAD) & (row == HEAD * (column // BLOCK) + column % BLOCK))


def half_select(rows, columns, half):
    row = lax.broadcasted_iota(jnp.int32, (rows, columns), 0)
    column = lax.broadcasted_iota(jnp.int32, (rows, columns), 1)
    return ones_where((row == BLOCK * (column // HEAD) + HEAD * half + column % HEAD) & (column < 3 * HEAD))


def forward_kernel(layer, layers, parts, experts, first, *refs):
    if first:
        tokens, cotangent, routes, kept, rel_bias, *refs = refs
    else:
        x, marks, bias, *refs = refs
    (
        gain_attn,
        gain_moe,
        w_router,
        w_key_hbm,
        w_value_hbm,
        w_query_hbm,
        w_output_hbm,
        w_in_hbm,
        w_out_hbm,
        *refs,
    ) = refs
    if first:
        x, grad, marks, bias, *refs = refs
    forward_body(
        layer,
        layers,
        parts,
        experts,
        (tokens, cotangent, routes, kept, rel_bias, grad) if first else None,
        x,
        marks,
        bias,
        gain_attn,
        gain_moe,
        w_router,
        w_key_hbm,
        w_value_hbm,
        w_query_hbm,
        w_output_hbm,
        w_in_hbm,
        w_out_hbm,
        *refs,
    )


def widened(w_router, layer):
    rows = w_router[layer]
    return jnp.concatenate([rows, jnp.zeros((BLOCK - rows.shape[0], rows.shape[1]), f32)], axis=0)


def gathering(here, blocks, send, recv, straight):
    half = blocks.shape[1] // 2

    def gather(flip, source):
        device = here.group_device(here.flipped(flip))
        return remote(blocks.at[source], blocks.at[source], send.at[flip - 1], recv.at[flip - 1], device)

    def relay(flip, source):
        rows = blocks.at[source, (flip - 1) * half : flip * half]
        device = here.group_device(here.flipped(3 if straight else 3 - flip))
        return remote(rows, rows, send.at[flip + 1], recv.at[flip + 1], device)

    return gather, relay


def halves(arrays):
    first = arrays[0].shape[1]
    return (0, first), (first, first + arrays[1].shape[1])


def joined(slots):
    return jnp.concatenate([slots[index].astype(f32) for index in range(slots.shape[0])], axis=0).astype(bf16)


def forward_body(
    layer,
    layers,
    parts,
    experts,
    begin,
    x,
    marks,
    bias,
    gain_attn,
    gain_moe,
    w_router,
    w_key_hbm,
    w_value_hbm,
    w_query_hbm,
    w_output_hbm,
    w_in_hbm,
    w_out_hbm,
    select,
    chosen,
    w_qkv_out,
    turned_out,
    query_out,
    pair_out,
    merged_out,
    log_total_out,
    middle,
    router,
    picked,
    arrived,
    arrived_more,
    before_out,
    x_next,
    w_qkv,
    turned,
    query,
    pair,
    merged,
    log_total,
    merged_low,
    before,
    normed,
    slabs,
    w_output,
    w_in,
    w_out,
    scores,
    merged_mine,
    slots,
    slots_more,
    total,
    answer,
    answer_more,
    returned,
    returned_more,
    load_sem,
    store_sem,
    group_send,
    group_recv,
    part_send,
    part_recv,
    merge_send,
    merge_recv,
    slot_send,
    slot_recv,
    back_send,
    back_recv,
    tokens_came=None,
    marks_here=None,
    swap_send=None,
    swap_recv=None,
):
    here = Place(parts, experts)
    chunk = FCHUNK if parts > 2 else 2 * FCHUNK
    heads = 3
    wide = heads * HEAD
    block = here.block
    if begin:
        tokens, cotangent, routes, kept, rel_bias, grad = begin
        all_here = here.greet(swap=True)
        marks_here[...] = jnp.zeros_like(marks_here)
        marks_here[:layers, :] = routes[...]
        marks_here[layers : 2 * layers, :] = kept[...]
        all_here()
        pairs = [(marks_here, marks), (tokens, tokens_came), (cotangent, grad)]
        swap = Swap(here, pairs, swap_send, swap_recv)
        swap.start((0, 1))
    else:
        all_here = here.greet()
    stores = [
        pltpu.make_async_copy(source, target, store_sem.at[index])
        for index, (source, target) in enumerate(
            (
                (w_qkv, w_qkv_out),
                (turned, turned_out),
                (query, query_out),
                (pair, pair_out),
                (merged, merged_out),
                (log_total, log_total_out),
                (before, before_out),
            )
        )
    ]
    slab = pl.ds(pl.multiple_of(BLOCK * div(3 * block, 2), BLOCK), 2 * BLOCK)
    loads = []
    for kind, source in enumerate((w_key_hbm, w_value_hbm, w_query_hbm)):
        target = slabs.at[:, kind * 2 * BLOCK : (kind + 1) * 2 * BLOCK]
        loads.append(pltpu.make_async_copy(source.at[layer, :, slab], target, load_sem.at[kind]))
    loads += [
        pltpu.make_async_copy(w_output_hbm.at[layer], w_output, load_sem.at[3]),
        pltpu.make_async_copy(w_in_hbm.at[layer, 0], w_in, load_sem.at[4]),
        pltpu.make_async_copy(w_out_hbm.at[layer, 0], w_out, load_sem.at[5]),
    ]
    for load in loads:
        load.start()
    if begin:
        for load in loads[:3]:
            load.wait()
        pack_weights(w_qkv, slabs, block)
        swap.wait((0, 1))
        value = tokens_came[...].astype(f32)
        x[...] = value
    else:
        value = x[...]
    normed[block] = (value * root_scale(value) * gain_attn[layer : layer + 1, :]).astype(bf16)
    if not begin:
        all_here()

    gather, relay = gathering(here, normed, group_send, group_recv, True)
    for flip in (1, 2):
        gather(flip, block).start()
    for flip in (1, 2):
        relay(flip, block).start()

    def hand_pair(step, part, of_block):
        return remote(
            pair.at[part, of_block],
            pair.at[part, of_block],
            part_send.at[step - 1, of_block],
            part_recv.at[step - 1, of_block],
            here.part_device(here.part_other(step)),
        )

    def project(of_block):
        made = dot(normed[of_block], w_qkv[...]).astype(bf16)
        pair[here.part, of_block] = made[:, : 2 * wide]
        query[of_block] = dot(made[:, 2 * wide :], query_spread(2 * BLOCK, 3 * BLOCK)).astype(bf16)
        for step in range(1, parts):
            hand_pair(step, here.part, of_block).start()
        columns = pl.ds(pl.multiple_of(of_block * BLOCK, BLOCK), BLOCK)
        turned[:, columns] = normed[of_block].astype(f32).T.astype(bf16)

    if begin:
        swap.start((2,))
    else:
        for load in loads[:3]:
            load.wait()
        pack_weights(w_qkv, slabs, block)
    project(block)
    route_tokens(marks, layer, layers, select, chosen)
    if begin:
        make_bias(bias, rel_bias, heads * block)
    for flip in (1, 2):
        gather(flip, here.flipped(flip)).wait_recv()
        project(here.flipped(flip))
    for flip in (1, 2):
        relay(flip, here.flipped(3)).wait_recv()
    project(here.flipped(3))
    for store in stores[:3]:
        store.start()
    lane_log = lanes(BLOCK, BLOCK)

    def hand_merged(flip, source):
        return remote(
            merged_mine.at[here.flipped(flip)],
            merged_low.at[source],
            merge_send.at[flip - 1],
            merge_recv.at[flip - 1],
            here.group_device(here.flipped(flip)),
        )

    for flip in (3, 1, 2, 0):
        mine = here.flipped(flip)
        logs = jnp.zeros((BLOCK, BLOCK), f32)
        for head in range(heads):
            columns = slice(head * BLOCK, (head + 1) * BLOCK)
            top = jnp.full((BLOCK, 1), -1e30, f32)
            for turn in range(parts):
                part = rem(here.part + turn, parts)
                if turn == 1 and flip == 3 and head == 0:
                    for step in range(1, parts):
                        source = rem(here.part + parts - step, parts)
                        for of_block in range(GROUP):
                            hand_pair(step, source, of_block).wait_recv()
                    stores[3].start()
                both = pair[part, :, :, columns].reshape(GROUP * BLOCK, BLOCK)
                raw = dot_nt(query[mine, :, columns], both)
                for of_block in range(GROUP):
                    piece = (
                        raw[:, of_block * BLOCK : (of_block + 1) * BLOCK]
                        + bias[head, here.bias_index(part, of_block, mine)]
                    )
                    scores[turn * GROUP + of_block] = piece
                    top = jnp.maximum(top, jnp.max(piece, axis=-1, keepdims=True))
            summed = jnp.zeros((BLOCK, 1), f32)
            out = jnp.zeros((BLOCK, BLOCK), f32)
            for turn in range(parts):
                part = rem(here.part + turn, parts)
                pieces = []
                for of_block in range(GROUP):
                    weight = jnp.exp(scores[turn * GROUP + of_block] - top)
                    summed = summed + jnp.sum(weight, axis=-1, keepdims=True)
                    pieces.append(weight.astype(bf16))
                both = pair[part, :, :, columns].reshape(GROUP * BLOCK, BLOCK)
                out = out + dot(jnp.concatenate(pieces, axis=1), both)
            merged[mine, :, columns] = jnp.where(lane_log >= HEAD, out / summed, 0.0)
            logs = jnp.where(lane_log == head, top + jnp.log(summed), logs)
        final = dot(merged[mine].astype(bf16), half_select(3 * BLOCK, wide, 1))
        log_total[mine] = logs
        if flip:
            merged_mine[mine] = final.astype(bf16)
            hand_merged(flip, block).start()
        else:
            merged_low[block] = final.astype(bf16)

    for store in stores[4:6]:
        store.start()
    for flip in (1, 2, 3):
        hand_merged(flip, here.flipped(flip)).wait_recv()
    loads[3].wait()
    mid = value
    for of_block in range(GROUP):
        mid = mid + dot(merged_low[of_block], w_output[of_block * wide : (of_block + 1) * wide, :])
    middle[...] = mid
    moe_in = mid * root_scale(mid) * gain_moe[layer : layer + 1, :]
    moe_low = moe_in.astype(bf16)

    slots, arrived = (slots, slots_more), (arrived, arrived_more)
    answer, returned = (answer, answer_more), (returned, returned_more)
    spans = halves(arrived)

    def hand_slots(half, step, source):
        return remote(
            slots[half].at[here.expert_other(step)],
            arrived[half].at[source],
            slot_send.at[half, step - 1],
            slot_recv.at[half, step - 1],
            {"expert": here.expert_other(step)},
        )

    for half, (low, high) in enumerate(spans):
        for expert in range(experts):
            slots[half][expert] = dot(select[expert, low:high], moe_low).astype(bf16)
        for step in range(1, experts):
            hand_slots(half, step, here.expert).start()
        arrived[half][here.expert] = slots[half][here.expert]
    logits = lax.dot_general(
        moe_in, widened(w_router, layer), (((1,), (1,)), ((), ())), precision=highest, preferred_element_type=f32
    )
    logits = jnp.where(lane_log < experts, logits, -1e30)
    raised = jnp.exp(logits - jnp.max(logits, axis=-1, keepdims=True))
    chances = raised / jnp.sum(raised, axis=-1, keepdims=True)
    router[...] = chances
    gate = jnp.sum(chances * chosen[...], axis=-1, keepdims=True)
    total[...] = jnp.zeros_like(total)
    loads[4].wait()
    loads[5].wait()

    def hand_answer(half, step, source):
        return remote(
            answer[half].at[here.expert_other(step)],
            returned[half].at[source],
            back_send.at[half, step - 1],
            back_recv.at[half, step - 1],
            {"expert": here.expert_other(step)},
        )

    for half, (low, high) in enumerate(spans):
        for step in range(1, experts):
            hand_slots(half, step, rem(here.expert + experts - step, experts)).wait_recv()
        given = joined(arrived[half])
        rows = slice(experts * low, experts * high)

        @pl.loop(0, w_in.shape[1] // chunk)
        def _(index, given=given, rows=rows):
            columns = pl.ds(pl.multiple_of(index * chunk, chunk), chunk)
            first = dot(given, w_in[:, columns])
            before[rows, columns] = first
            total[rows, :] += dot(gelu(first).astype(bf16), w_out[columns, :])

        for expert in range(experts):
            first = experts * low + expert * (high - low)
            answer[half][expert] = total[first : first + high - low, :].astype(bf16)
        for step in range(1, experts):
            hand_answer(half, step, here.expert).start()
        returned[half][here.expert] = answer[half][here.expert]
    stores[6].start()
    back = jnp.zeros_like(value)
    for half, (low, high) in enumerate(spans):
        for step in range(1, experts):
            hand_answer(half, step, rem(here.expert + experts - step, experts)).wait_recv()
        for expert in range(experts):
            back = back + dot_tn(select[expert, low:high], returned[half][expert])
    picked[...] = back.astype(bf16)
    x_next[...] = mid + gate * back
    for store in stores:
        store.wait()
    if begin:
        swap.wait((2,))
        swap.drain()
    for flip in (1, 2):
        gather(flip, block).wait_send()
        relay(flip, here.flipped(flip)).wait_send()
    for flip in (1, 2, 3):
        hand_merged(flip, block).wait_send()
    for step in range(1, parts):
        for of_block in range(GROUP):
            hand_pair(step, here.part, of_block).wait_send()
    for step in range(1, experts):
        for half in range(2):
            hand_slots(half, step, here.expert).wait_send()
            hand_answer(half, step, here.expert).wait_send()


def table_sum(table, grads, block):
    marks = lanes(table, 128)
    row = lax.broadcasted_iota(jnp.int32, marks.shape, 0)
    half = table // 2
    total = jnp.zeros(marks.shape, f32)
    for head in range(3):
        made = jnp.zeros(marks.shape, f32)
        for place, bucket in ((0, half - 1), (4, 2 * half - 1)):
            line = jnp.sum(grads[head, place], axis=0, keepdims=True)
            made = made + jnp.where(row == bucket, line, 0.0)
        for place in (1, 2, 3):
            buckets = bucket_block(place, half)

            def one(bucket, made, buckets=buckets, place=place, head=head):
                found = jnp.where(buckets == bucket, grads[head, place], 0.0)
                return made + jnp.where(row == bucket, jnp.sum(found, axis=0, keepdims=True), 0.0)

            made = lax.fori_loop(*bucket_range(place, half), one, made)
        column = jnp.sum(made, axis=-1, keepdims=True)
        total = total + jnp.where(marks == 3 * block + head, column, 0.0)
    return total


class Saved(NamedTuple):
    x: Any
    grad: Any
    marks: Any
    bias: Any
    select: Any
    chosen: Any
    w_qkv: Any
    turned: Any
    query: Any
    pair: Any
    merged: Any
    log_total: Any
    middle: Any
    router: Any
    picked: Any
    arrived: Any
    arrived_more: Any
    before: Any
    x_next: Any


class Own(NamedTuple):
    grad_next: Any
    in_across: Any
    in_beside: Any
    in_own: Any
    out_across: Any
    out_beside: Any
    out_own: Any
    qkv: Any
    output: Any
    bias: Any
    rows: Any


class Taken(NamedTuple):
    in_across: Any
    in_beside: Any
    out_across: Any
    out_beside: Any
    qkv: Any
    output: Any
    rows: Any
    table_part: Any = None


class Given(NamedTuple):
    in_from_across: Any
    in_from_beside: Any
    out_from_across: Any
    out_from_beside: Any
    sums: Any
    rows_sum: Any
    table_out: Any = None


class Needed(NamedTuple):
    small: Any
    qkv_core: Any
    output_core: Any
    small_core: Any
    qkv_line: Any
    output_line: Any
    small_line: Any
    qkv_came: Any
    output_came: Any
    small_came: Any
    qkv_plane: Any
    output_plane: Any
    small_plane: Any
    qkv_last: Any
    output_last: Any
    small_last: Any
    expert_send: Any
    expert_recv: Any
    core_send: Any
    core_recv: Any
    line_send: Any
    line_recv: Any
    plane_send: Any
    plane_recv: Any
    output_send: Any
    output_recv: Any


def present(items):
    return [item for item in items if item is not None]


def taken_from(own, table):
    return Taken(
        own.in_across,
        own.in_beside,
        own.out_across,
        own.out_beside,
        own.qkv,
        own.output,
        own.rows,
        own.bias if table else None,
    )


class Earlier:
    def __init__(self, parts, experts, table, taken, given, needed):
        self.parts, self.experts, self.table, self.fars = parts, experts, table, parts // 2
        for refs in (Taken(*taken), Given(*given), Needed(*needed)):
            self.__dict__.update(refs._asdict())

    def expert_copies(self, which=(0, 1, 2, 3)):
        here, made = self.here, []
        across, beside = here.group_device(here.flipped(1)), here.group_device(here.flipped(2))
        for kind, (source, target, device) in enumerate(
            (
                (self.in_across, self.in_from_across, across),
                (self.out_beside, self.out_from_beside, beside),
                (self.in_beside, self.in_from_beside, beside),
                (self.out_across, self.out_from_across, across),
            )
        ):
            half = source.shape[2] // 2
            for turn in range(2):
                if kind // 2 * 2 + turn in which:
                    columns = slice(turn * half, (turn + 1) * half)
                    sems = self.expert_send.at[kind, turn], self.expert_recv.at[kind, turn]
                    made.append(remote(source.at[:, :, columns], target.at[:, :, columns], *sems, device))
        return made

    def core_copies(self):
        here, made = self.here, []
        device = here.core_device()
        for at in range(2):
            sems = self.core_send.at[at], self.core_recv.at[at]
            made.append(remote(self.qkv.at[2 * at + 1 - here.core], self.qkv_core.at[at], *sems, device))
        sems = self.core_send.at[2], self.core_recv.at[2]
        made.append(remote(self.output.at[1 - here.core], self.output_core, *sems, device))
        sems = self.core_send.at[3], self.core_recv.at[3]
        made.append(remote(self.small, self.small_core, *sems, device))
        return made

    def line_copies(self, step, source):
        here = self.here
        target = here.expert_other(step)
        device = {"expert": target}
        sems = [(self.line_send.at[kind, step - 1], self.line_recv.at[kind, step - 1]) for kind in range(3)]
        return [
            remote(self.qkv_line.at[target], self.qkv_came.at[source], *sems[0], device),
            remote(self.output_line.at[target], self.output_came.at[source], *sems[1], device),
            remote(self.small_line, self.small_came.at[source], *sems[2], device),
        ]

    def plane_copies(self):
        here, made = self.here, []
        for step, flip, far, other, device in here.plane_others():
            sems = [(self.plane_send.at[kind, step, flip], self.plane_recv.at[kind, step, flip]) for kind in range(2)]
            source = self.qkv_plane.at[rem(other, 2), 2 * far + div(other, 2)]
            made.append(remote(source, self.qkv_last.at[here.block, here.far], *sems[0], device))
            made.append(remote(self.small_plane, self.small_last.at[here.block, here.far], *sems[1], device))
        return made

    def output_copy(self, context):
        here = self.here
        return remote(
            self.output_plane.at[context],
            self.output_last.at[here.core, here.far],
            self.output_send.at[context],
            self.output_recv.at[here.core, here.far],
            {"dp": here.block, "context": jnp.int32(context)},
        )

    def is_here(self, context):
        return (self.here.block == self.here.dp) & (self.here.context == context)

    def begin(self, here, which=(0, 1, 2, 3)):
        self.here = here
        for copy in self.expert_copies(which):
            copy.start()
        pieces = self.rows.shape[1] // 128
        for piece in range(pieces):
            self.small[8 * piece : 8 * piece + 8, :] = self.rows[:, piece * 128 : (piece + 1) * 128]
        for copy in self.core_copies()[:3]:
            copy.start()
        if self.table:
            self.small[8 * pieces :, :] = self.table_part[...]
        self.core_copies()[3].start()

    def pass_line(self):
        here = self.here
        for copy in self.core_copies():
            copy.wait_recv()
        for expert in range(self.experts):
            for context in range(self.parts):
                for at in range(2):
                    self.qkv_line[expert, at, context] = (
                        self.qkv[2 * at + here.core, context, expert].astype(f32)
                        + self.qkv_core[at, context, expert].astype(f32)
                    ).astype(bf16)
                self.output_line[expert, context] = (
                    self.output[here.core, context, expert].astype(f32)
                    + self.output_core[context, expert].astype(f32)
                ).astype(bf16)
        self.small_line[...] = self.small[...] + self.small_core[...]
        for step in range(1, self.experts):
            for copy in self.line_copies(step, here.expert):
                copy.start()

    def pass_plane(self, which=()):
        here = self.here
        for step in range(1, self.experts):
            for copy in self.line_copies(step, rem(here.expert + self.experts - step, self.experts)):
                copy.wait_recv()
        sources = [rem(here.expert + step, self.experts) for step in range(1, self.experts)]
        for context in range(self.parts):
            for at in range(2):
                total = self.qkv_line[here.expert, at, context].astype(f32)
                for source in sources:
                    total = total + self.qkv_came[source, at, context].astype(f32)
                self.qkv_plane[at, context] = total.astype(bf16)
            total = self.output_line[here.expert, context].astype(f32)
            for source in sources:
                total = total + self.output_came[source, context].astype(f32)
            self.output_plane[context] = total.astype(bf16)
        total = self.small_line[...]
        for source in sources:
            total = total + self.small_came[source]
        self.small_plane[...] = total
        for copy in self.plane_copies():
            copy.start()
        for context in range(self.parts):

            @pl.when(jnp.logical_not(self.is_here(context)))
            def _():
                self.output_copy(context).start()

            @pl.when(self.is_here(context))
            def _():
                self.output_last[here.core, here.far] = self.output_plane[context]

        for copy in self.expert_copies(which):
            copy.start()
        self.qkv_last[here.block, here.far] = self.qkv_plane[div(here.dp, 2), here.context]
        self.small_last[here.block, here.far] = self.small_plane[...]

    def finish(self):
        here = self.here
        for copy in self.plane_copies():
            copy.wait_recv()
        for core in range(2):
            for far in range(self.fars):
                source_dp = 2 * here.core + core
                source_context = 2 * far + div(here.dp, 2)

                @pl.when(jnp.logical_not((source_dp == here.dp) & (source_context == here.context)))
                def _():
                    remote(
                        self.output_plane.at[0],
                        self.output_last.at[core, far],
                        self.output_send.at[0],
                        self.output_recv.at[core, far],
                        here.core_device(),
                    ).wait_recv()

        wide = 3 * HEAD
        total = jnp.zeros(self.small_plane.shape, f32)
        for block in range(GROUP):
            made = jnp.zeros(self.qkv_last.shape[2:], f32)
            for far in range(self.fars):
                total = total + self.small_last[block, far]
                made = made + self.qkv_last[block, far].astype(f32)
            columns = slice(block * wide, (block + 1) * wide)
            for head in range(3):
                part = slice(block * wide + head * HEAD, block * wide + (head + 1) * HEAD)
                for kind in range(2):
                    first = head * BLOCK + kind * HEAD
                    self.sums[kind, :, part] = made[:, first : first + HEAD]
            self.sums[2, :, columns] = made[:, 2 * wide : 3 * wide]
        half = self.output_last.shape[3]
        for core in range(2):
            made = self.output_last[core, 0].astype(f32)
            for far in range(1, self.fars):
                made = made + self.output_last[core, far].astype(f32)
            self.sums[3, :, core * half : (core + 1) * half] = made
        pieces = self.rows.shape[1] // 128
        for piece in range(pieces):
            self.rows_sum[:, piece * 128 : (piece + 1) * 128] = total[8 * piece : 8 * piece + 8, :]
        if self.table:
            self.table_out[...] = total[8 * pieces :, :]
        for copy in self.expert_copies():
            copy.wait()
        for copy in self.core_copies() + self.plane_copies():
            copy.wait_send()
        for step in range(1, self.experts):
            for copy in self.line_copies(step, here.expert):
                copy.wait_send()
        for context in range(self.parts):

            @pl.when(jnp.logical_not(self.is_here(context)))
            def _():
                self.output_copy(context).wait_send()


def earlier_call(parts, experts, left, table):
    tall, packed = left.qkv.shape[3:]
    half = left.output.shape[4]
    fars = parts // 2
    small = 8 * (2 * half // 128) + (table or 0)
    shape, scratch = jax.ShapeDtypeStruct, pltpu.VMEM
    specs = [ANY] * 4 + [VMEM] * (4 if table else 3)
    gives = Given(
        shape(left.in_across.shape, bf16),
        shape(left.in_across.shape, bf16),
        shape(left.out_across.shape, bf16),
        shape(left.out_across.shape, bf16),
        shape((4, tall, 2 * half), f32),
        shape((8, 2 * half), f32),
        shape((table, 128), f32) if table else None,
    )
    needs = Needed(
        small=scratch((small, 128), f32),
        qkv_core=scratch((2, parts, experts, tall, packed), bf16),
        output_core=scratch((parts, experts, tall, half), bf16),
        small_core=scratch((small, 128), f32),
        qkv_line=scratch((experts, 2, parts, tall, packed), bf16),
        output_line=scratch((experts, parts, tall, half), bf16),
        small_line=scratch((small, 128), f32),
        qkv_came=scratch((experts, 2, parts, tall, packed), bf16),
        output_came=scratch((experts, parts, tall, half), bf16),
        small_came=scratch((experts, small, 128), f32),
        qkv_plane=scratch((2, parts, tall, packed), bf16),
        output_plane=scratch((parts, tall, half), bf16),
        small_plane=scratch((small, 128), f32),
        qkv_last=scratch((GROUP, fars, tall, packed), bf16),
        output_last=scratch((2, fars, tall, half), bf16),
        small_last=scratch((GROUP, fars, small, 128), f32),
        expert_send=DMA((4, 2)),
        expert_recv=DMA((4, 2)),
        core_send=DMA((4,)),
        core_recv=DMA((4,)),
        line_send=DMA((3, experts - 1)),
        line_recv=DMA((3, experts - 1)),
        plane_send=DMA((2, fars, GROUP)),
        plane_recv=DMA((2, fars, GROUP)),
        output_send=DMA((parts,)),
        output_recv=DMA((2, fars)),
    )
    given_specs = [ANY] * 4 + [VMEM] * (3 if table else 2)
    return specs, gives, given_specs, needs


def finish_kernel(parts, experts, table, last, others, *refs):
    here = Place(parts, experts)
    swap = None
    if last:
        grad, *refs = refs
        *refs, grad_low, grad_came, send, recv = refs
    takes = 8 if table else 7
    taken, refs = refs[:takes], refs[takes:]
    if others:
        loads_from, refs = refs[: 2 + 6 * others], refs[2 + 6 * others :]
    if last:
        d_tokens, *refs = refs
        swap = Swap(here, [(grad_low, grad_came)], send, recv)
    if others:
        sums, rows_sum, table_out, final_in, final_out, *refs = refs
        *refs, in_part, in_whole, out_whole, out_part = refs
        *refs, load_sem = refs
        refs, loads_to = refs[: -2 - 6 * others], refs[-2 - 6 * others :]
        given = [in_part, in_whole, out_whole, out_part, sums, rows_sum, table_out]
        loads = [
            pltpu.make_async_copy(source, target, load_sem.at[index])
            for index, (source, target) in enumerate(zip(loads_from, loads_to, strict=True))
        ]
        for load in loads:
            load.start()
    else:
        given, refs = refs[: takes - 1], refs[takes - 1 :]
    earlier = Earlier(parts, experts, table, taken, given, refs)
    all_here = here.greet(plane=True, swap=last)
    if last:
        grad_low[...] = grad[...].astype(bf16)
    all_here()
    earlier.begin(here, (0, 1, 2))
    if last:
        swap.start((0,))
    earlier.pass_line()

    def total(target, own, one, other):
        made = own[0].astype(f32) + one[0].astype(f32) + other[0].astype(f32)
        target[...] = made.astype(bf16)

    if others:
        for load in loads:
            load.wait()
        for layer in range(others):
            own_in, part_in, whole_in, own_out, part_out, whole_out = loads_to[2 + 6 * layer : 8 + 6 * layer]
            total(final_in.at[1 + layer], own_in, part_in, whole_in)
            total(final_out.at[1 + layer], own_out, part_out, whole_out)
    earlier.pass_plane((3,))
    earlier.finish()
    if others:
        total(final_in.at[0], loads_to[0], in_part, in_whole)
        total(final_out.at[0], loads_to[1], out_part, out_whole)
    if last:
        swap.wait((0,))
        d_tokens[...] = grad_came[...].astype(f32)
        swap.drain()


def finish(left, table, number, grad=None, others=()):
    parts, experts = lax.axis_size("context"), lax.axis_size("expert")
    specs, gives, given_specs, needs = earlier_call(parts, experts, left, table)
    last = grad is not None
    shape, scratch = jax.ShapeDtypeStruct, pltpu.VMEM
    loaded, more_scratch, finals = [], [], []
    if others:
        loaded = [left.in_own, left.out_own]
        for own, done in others:
            loaded += [own.in_own, done.in_from_across, done.in_from_beside]
            loaded += [own.out_own, done.out_from_beside, done.out_from_across]
        more_scratch = [scratch(item.shape, bf16) for item in loaded] + [DMA((len(loaded),))]
        more_scratch += [scratch(item.shape, bf16) for item in gives[:4]]
        finals = [shape((1 + len(others),) + item.shape[1:], bf16) for item in loaded[:2]]
        gives, given_specs = gives[4:], given_specs[4:]
    given = pl.pallas_call(
        functools.partial(finish_kernel, parts, experts, table, last, len(others)),
        out_shape=([shape(grad.shape, f32)] if last else []) + present(gives) + finals,
        in_specs=[VMEM] * last + specs + [ANY] * len(loaded),
        out_specs=[VMEM] * last + given_specs + [VMEM] * len(finals),
        scratch_shapes=list(needs)
        + more_scratch
        + ([scratch(grad.shape, bf16)] * 2 + [DMA((1,)), DMA((1,))] if last else []),
        compiler_params=pltpu.CompilerParams(
            collective_id=number, has_side_effects=True, vmem_limit_bytes=60 * 2**20
        ),
        name="finish",
    )(*([grad] if last else []), *present(taken_from(left, table)), *loaded)
    if others:
        return Given(None, None, None, None, *given[1:4]), given[0], given[4:]
    return Given(*given[last:]), given[0], None


def backward_and_earlier(layer, parts, experts, counts, earlier_bias, table, *refs):
    own_in, takes, own_out, gives, needs, last = counts
    own_scratch = len(refs) - own_in - takes - own_out - gives - needs - 5 * last
    cuts = np.cumsum([0, own_in, takes, last, own_out, gives, last, own_scratch, needs, 3 * last])
    pieces = [refs[a:b] for a, b in zip(cuts[:-1], cuts[1:], strict=True)]
    earlier = Earlier(parts, experts, None, pieces[1], pieces[4], pieces[7]) if takes else None
    backward_kernel(
        layer,
        parts,
        experts,
        *pieces[0],
        *pieces[3],
        *pieces[6],
        earlier=earlier,
        earlier_bias=earlier_bias,
        table=table,
        last=pieces[2] + pieces[5] + pieces[8] if last else None,
    )


def backward_kernel(
    layer,
    parts,
    experts,
    grad,
    x,
    gain_attn,
    gain_moe,
    w_router,
    select,
    chosen,
    bias_hbm,
    bias_before,
    turned_hbm,
    query_hbm,
    pair_hbm,
    merged_hbm,
    log_total_hbm,
    middle,
    router,
    picked,
    arrived,
    arrived_more,
    before_hbm,
    w_qkv_hbm,
    w_output_hbm,
    w_in_hbm,
    w_out_hbm,
    grad_next,
    in_across,
    in_beside,
    in_own,
    out_across,
    out_beside,
    out_own,
    grad_qkv_out,
    grad_output,
    grad_bias_out,
    grad_rows,
    bias,
    turned,
    query,
    pair,
    merged,
    log_total,
    grad_qkv,
    grad_bias,
    grad_in,
    grad_out,
    core_in,
    core_out,
    second_in,
    second_out,
    output_sum,
    w_qkv,
    w_output,
    slots,
    slots_more,
    arrived_grad,
    arrived_grad_more,
    answer,
    answer_more,
    returned,
    returned_more,
    given_grad,
    branches,
    query_grad,
    pair_sent,
    pair_recv,
    made_grad,
    normed_sent,
    normed_recv,
    load_sem,
    slot_send,
    slot_recv,
    back_send,
    back_recv,
    group_send,
    group_recv,
    part_send,
    part_recv,
    merge_send,
    merge_recv,
    core_send,
    core_recv,
    second_send,
    second_recv,
    store_sem,
    earlier=None,
    earlier_bias=False,
    last=None,
    table=None,
):
    here = Place(parts, experts)
    chunk = FCHUNK if parts > 2 else 2 * FCHUNK
    heads = 3
    wide = heads * HEAD
    block = here.block
    fars = parts // 2
    side, level = div(here.dp, 2), rem(here.context, 2)
    across, beside = here.group_device(here.flipped(1)), here.group_device(here.flipped(2))
    own_in, own_out = grad_in.at[2 * side + here.core], grad_out.at[2 * side + here.core]

    def to_core(turns=(0, 1)):
        made = []
        for at in turns:
            there = 2 * at + 1 - here.core
            for kind, (source, target) in enumerate(((grad_in, core_in), (grad_out, core_out))):
                sems = core_send.at[kind, at], core_recv.at[kind, at]
                made.append(remote(source.at[there], target.at[at], *sems, here.core_device()))
        return made

    def second():
        made = []
        for far in range(fars):
            sems = second_send.at[0, far], second_recv.at[0, far]
            source = grad_in.at[2 * (1 - side) + here.core, 2 * far + 1 - level]
            made.append(remote(source, second_in.at[far], *sems, across))
            sems = second_send.at[1, far], second_recv.at[1, far]
            source = grad_out.at[2 * (1 - side) + here.core, 2 * far + 1 - level]
            made.append(remote(source, second_out.at[far], *sems, beside))
        return made

    def stores(kinds):
        made = []
        there = 2 * (1 - side) + here.core
        for far in range(fars):
            for kind, (source, target) in enumerate(
                (
                    (grad_in.at[there, 2 * far + level], in_across),
                    (own_in.at[2 * far + 1 - level], in_beside),
                    (own_in.at[2 * far + level], in_own),
                    (grad_out.at[there, 2 * far + level], out_across),
                    (own_out.at[2 * far + 1 - level], out_beside),
                    (own_out.at[2 * far + level], out_own),
                )
            ):
                if kind in kinds:
                    made.append(pltpu.make_async_copy(source, target.at[far], store_sem.at[kind, far]))
        return made

    def add(target, source):
        target[...] = (target[...].astype(f32) + source[...].astype(f32)).astype(bf16)
    later = [
        pltpu.make_async_copy(source, target, load_sem.at[6 + index])
        for index, (source, target) in enumerate(
            (
                (w_qkv_hbm, w_qkv),
                (turned_hbm, turned),
                (query_hbm, query),
                (pair_hbm, pair),
                (merged_hbm, merged),
                (log_total_hbm, log_total),
                (bias_hbm, bias),
                (bias_before, grad_bias),
            )[: 8 if earlier_bias else 7]
        )
    ]
    for head in range(heads):
        rows = pl.ds(pl.multiple_of(block * wide + head * HEAD, HEAD), HEAD)
        target = w_output.at[head * BLOCK + HEAD : (head + 1) * BLOCK]
        later.append(pltpu.make_async_copy(w_output_hbm.at[layer, rows], target, load_sem.at[3 + head]))

    all_here = here.greet(plane=earlier is not None, swap=last is not None)
    slots, arrived_grad = (slots, slots_more), (arrived_grad, arrived_grad_more)
    answer, returned = (answer, answer_more), (returned, returned_more)
    spans = halves((arrived, arrived_more))

    def hand_slots(half, step, source):
        return remote(
            slots[half].at[here.expert_other(step)],
            arrived_grad[half].at[source],
            slot_send.at[half, step - 1],
            slot_recv.at[half, step - 1],
            {"expert": here.expert_other(step)},
        )

    def hand_answer(half, step, source):
        return remote(
            answer[half].at[here.expert_other(step)],
            returned[half].at[source],
            back_send.at[half, step - 1],
            back_recv.at[half, step - 1],
            {"expert": here.expert_other(step)},
        )

    if last:
        x_last, out, out_low, send, recv = last
        out_low[...] = x_last[...].astype(bf16)
        swap = Swap(here, [(out_low, out)], send, recv)

    def experts_phase(w_in, w_out, hidden, slope, before_grad, total, turned_given):
        loads = [
            pltpu.make_async_copy(before_hbm, slope, load_sem.at[2]),
            pltpu.make_async_copy(w_out_hbm.at[layer, 0], w_out, load_sem.at[0]),
            pltpu.make_async_copy(w_in_hbm.at[layer, 0], w_in, load_sem.at[1]),
        ]
        for load in loads + later:
            load.start()
        for head in range(heads):
            w_output[head * BLOCK : head * BLOCK + HEAD, :] = jnp.zeros((HEAD, w_output.shape[1]), bf16)
        came = grad[...].astype(f32)
        chances = router[...]
        gate = jnp.sum(chances * chosen[...], axis=-1, keepdims=True)
        gate_grad = jnp.sum(came * picked[...].astype(f32), axis=-1, keepdims=True)
        answer_grad = (gate * came).astype(bf16)
        for half, (low, high) in enumerate(spans):
            for expert in range(experts):
                slots[half][expert] = dot(select[expert, low:high], answer_grad).astype(bf16)
        all_here()
        if earlier:
            earlier.begin(here)

        for half in range(2):
            for step in range(1, experts):
                hand_slots(half, step, here.expert).start()
            arrived_grad[half][here.expert] = slots[half][here.expert]
        hidden_width = w_in.shape[1]

        loads[0].wait()

        @pl.loop(0, hidden_width // chunk)
        def _(index):
            columns = pl.ds(pl.multiple_of(index * chunk, chunk), chunk)
            made, steep = gelu_parts(slope[:, columns])
            hidden[:, columns] = made.astype(bf16)
            slope[:, columns] = steep

        mid = middle[...]
        scale = root_scale(mid)
        unit = mid * scale
        moe_in = unit * gain_moe[layer : layer + 1, :]
        chance_grad = chosen[...] * gate_grad
        logit_grad = chances * (chance_grad - jnp.sum(chances * chance_grad, axis=-1, keepdims=True))
        router_grad = lax.dot_general(
            logit_grad, moe_in, (((0,), (0,)), ((), ())), precision=highest, preferred_element_type=f32
        )
        grad_rows[...] = router_grad[:8, :]
        moe_part = jnp.dot(
            logit_grad, widened(w_router, layer), precision=highest, preferred_element_type=f32
        )
        given = jnp.concatenate([joined(arrived), joined(arrived_more)], axis=0)
        turned_given[...] = given.astype(f32).T.astype(bf16)
        total[...] = jnp.zeros_like(total)
        loads[1].wait()
        loads[2].wait()
        for half, (low, high) in enumerate(spans):
            for step in range(1, experts):
                hand_slots(half, step, rem(here.expert + experts - step, experts)).wait_recv()
            rows = slice(experts * low, experts * high)
            given_grad[rows, :] = joined(arrived_grad[half])

            @pl.loop(0, hidden_width // chunk)
            def _(index, rows=rows):
                columns = pl.ds(pl.multiple_of(index * chunk, chunk), chunk)
                hidden_grad = dot_nt(given_grad[rows, :], w_out[columns, :])
                low_grad = (hidden_grad * slope[rows, columns]).astype(bf16)
                before_grad[rows, columns] = low_grad
                total[rows, :] += dot_nt(low_grad, w_in[:, columns])

            for expert in range(experts):
                first = experts * low + expert * (high - low)
                answer[half][expert] = total[first : first + high - low, :].astype(bf16)
            for step in range(1, experts):
                hand_answer(half, step, here.expert).start()
            returned[half][here.expert] = answer[half][here.expert]
        if last:
            swap.start((0,))
        rows_in, rows_out = grad_in.shape[2], grad_out.shape[2]
        columns_in = grad_in.shape[3] // GROUP
        for turn in range(4):
            there = 2 * (turn % 2) + (1 - here.core if turn < 2 else here.core)
            rows = pl.ds(pl.multiple_of(there * (parts * rows_in), parts * rows_in), parts * rows_in)
            for piece in range(GROUP):
                columns = slice(piece * columns_in, (piece + 1) * columns_in)
                made = dot(turned_given[rows, :], before_grad[:, columns])
                for at in range(parts):
                    grad_in[there, at, :, columns] = made[at * rows_in : (at + 1) * rows_in, :].astype(bf16)
            columns = pl.ds(pl.multiple_of(there * (parts * rows_out), parts * rows_out), parts * rows_out)
            made = dot_tn(hidden[:, columns], given_grad[...])
            for at in range(parts):
                grad_out[there, at] = made[at * rows_out : (at + 1) * rows_out, :].astype(bf16)
            if turn < 2:
                for copy in to_core((turn,)):
                    copy.start()

        moe_grad = moe_part
        for half, (low, high) in enumerate(spans):
            for step in range(1, experts):
                hand_answer(half, step, rem(here.expert + experts - step, experts)).wait_recv()
            for expert in range(experts):
                moe_grad = moe_grad + dot_tn(select[expert, low:high], returned[half][expert])
        grad_rows[4:5, :] = jnp.sum(moe_grad * unit, axis=0, keepdims=True)
        scaled = moe_grad * gain_moe[layer : layer + 1, :]
        mid_grad = came + scale * (scaled - unit * jnp.mean(unit * scaled, axis=-1, keepdims=True))
        branches[block] = mid_grad.astype(bf16)
        return mid_grad

    slot_rows = given_grad.shape[0]
    mid_grad = pl.run_scoped(
        experts_phase,
        pltpu.VMEM(w_in_hbm.shape[2:], bf16),
        pltpu.VMEM(w_out_hbm.shape[2:], bf16),
        pltpu.VMEM(before_hbm.shape, bf16),
        pltpu.VMEM(before_hbm.shape, f32),
        pltpu.VMEM(before_hbm.shape, bf16),
        pltpu.VMEM((slot_rows, grad.shape[1]), f32),
        pltpu.VMEM((grad.shape[1], slot_rows), bf16),
    )

    gather, relay = gathering(here, branches, group_send, group_recv, earlier is None)
    for flip in (1, 2):
        gather(flip, block).start()
    if earlier is None:
        for flip in (1, 2):
            relay(flip, block).start()
    for turn in range(2):
        for copy in to_core((turn,)):
            copy.wait_recv()
        for at in range(parts):
            add(grad_in.at[2 * turn + here.core, at], core_in.at[turn, at])
            add(grad_out.at[2 * turn + here.core, at], core_out.at[turn, at])
    if earlier:
        for flip in (1, 2):
            gather(flip, here.flipped(flip)).wait_recv()
            relay(flip, here.flipped(flip)).start()
    for copy in second() + stores((0, 2, 4, 5)):
        copy.start()
    if earlier:
        earlier.pass_line()
    for load in later:
        load.wait()
    def hand_pair(step, source):
        return remote(
            pair_sent.at[step - 1],
            pair_recv.at[step - 1],
            part_send.at[step - 1],
            part_recv.at[step - 1],
            here.part_device(here.part_other(step)),
        )

    def attention_phase(pair_grad):
        lane = lanes(BLOCK, BLOCK)
        if not earlier_bias:
            grad_bias[...] = jnp.zeros_like(grad_bias)
        for flip in range(GROUP):
            mine = here.flipped(flip)
            if flip == 3:
                for other in (1, 2):
                    relay(other, mine).wait_recv()
            elif flip and earlier is None:
                gather(flip, mine).wait_recv()
            wanted = dot_nt(branches[mine], w_output[...])
            wanted_low = wanted.astype(bf16)
            wanted = wanted_low.astype(f32)
            turned_rows = jnp.concatenate([query[mine].astype(f32).T, wanted.T], axis=1).astype(bf16)
            products = wanted * merged[mine]
            for head in range(heads):
                columns = slice(head * BLOCK, (head + 1) * BLOCK)
                rows = jnp.concatenate([query[mine, :, columns], wanted_low[:, columns]], axis=0)
                delta = jnp.sum(products[:, columns], axis=-1, keepdims=True)
                log_sum = log_total[mine][:, head : head + 1]
                gathered = jnp.zeros((BLOCK, BLOCK), f32)
                for part in range(parts):
                    both = pair[part, :, :, columns].reshape(GROUP * BLOCK, BLOCK)
                    raw = dot_nt(rows, both)
                    upper, lower = [], []
                    for of_block in range(GROUP):
                        inside = slice(of_block * BLOCK, (of_block + 1) * BLOCK)
                        place = here.bias_index(part, of_block, mine)
                        weight = jnp.exp(raw[:BLOCK, inside] + (bias[head, place] - log_sum))
                        score_grad = weight * (raw[BLOCK:, inside] - delta)
                        grad_bias[head, place] += score_grad
                        upper.append(score_grad.astype(bf16))
                        lower.append(weight.astype(bf16))
                    upper = jnp.concatenate(upper, axis=1)
                    stacked = jnp.concatenate([upper, jnp.concatenate(lower, axis=1)], axis=0)
                    gathered = gathered + dot(upper, both)
                    more = dot(turned_rows[columns], stacked)
                    if flip:
                        pair_grad[part, columns, :] += more
                    else:
                        pair_grad[part, columns, :] = more
                query_grad[mine, :, columns] = jnp.where(lane < HEAD, gathered, 0.0).astype(bf16)
        for step in range(1, parts):
            pair_sent[step - 1] = pair_grad[here.part_other(step)].astype(bf16)
            hand_pair(step, 0).start()
        summed = pair_grad[here.part]
        for step in range(1, parts):
            hand_pair(step, 0).wait_recv()
            summed = summed + pair_recv[step - 1].astype(f32)
        summed = summed.T.astype(bf16)
        for of_block in range(GROUP):
            made_grad[of_block, :, : 2 * wide] = summed[of_block * BLOCK : (of_block + 1) * BLOCK, :]
            made_grad[of_block, :, 2 * wide :] = dot(
                query_grad[of_block], half_select(3 * BLOCK, 2 * BLOCK, 0)
            ).astype(bf16)

    pl.run_scoped(attention_phase, pltpu.VMEM((parts, 2 * wide, GROUP * BLOCK), f32))

    def hand_normed(flip):
        return remote(
            normed_sent.at[flip - 1],
            normed_recv.at[flip - 1],
            merge_send.at[flip - 1],
            merge_recv.at[flip - 1],
            here.group_device(here.flipped(flip)),
        )

    for flip in (3, 1, 2):
        normed_sent[flip - 1] = dot_nt(made_grad[here.flipped(flip)], w_qkv[...]).astype(bf16)
        hand_normed(flip).start()
    normed_grad = dot_nt(made_grad[block], w_qkv[...])
    if earlier:
        earlier.pass_plane()
    both = made_grad[...].reshape(GROUP * BLOCK, made_grad.shape[2])
    rows = turned.shape[0] // GROUP
    tall = grad_qkv.shape[3]
    for there in range(GROUP):
        made = dot(turned[there * rows : (there + 1) * rows, :], both)
        for at in range(parts):
            for expert in range(experts):
                first = (at * experts + expert) * tall
                grad_qkv[there, at, expert] = made[first : first + tall, :].astype(bf16)
    made = dot_tn(
        merged[...].reshape(GROUP * BLOCK, 3 * BLOCK).astype(bf16),
        branches[...].reshape(GROUP * BLOCK, branches.shape[2]),
    )
    for head in range(heads):
        output_sum[head * HEAD : (head + 1) * HEAD, :] = made[head * BLOCK + HEAD : (head + 1) * BLOCK, :]
    stores_late = [pltpu.make_async_copy(grad_qkv, grad_qkv_out, store_sem.at[6, 0])]
    if table:
        grad_bias_out[...] = table_sum(table, grad_bias, here.block)
    else:
        stores_late.append(pltpu.make_async_copy(grad_bias, grad_bias_out, store_sem.at[7, 0]))
    for store in stores_late:
        store.start()
    half = grad_output.shape[4]
    for at in range(parts):
        for expert in range(experts):
            first = (at * experts + expert) * tall
            for turn in range(2):
                piece = output_sum[first : first + tall, turn * half : (turn + 1) * half]
                grad_output[turn, at, expert] = piece.astype(bf16)
    for copy in second():
        copy.wait_recv()
    for far in range(fars):
        add(own_in.at[2 * far + 1 - level], second_in.at[far])
        add(grad_out.at[2 * (1 - side) + here.core, 2 * far + level], second_out.at[far])
    for copy in stores((1, 3)):
        copy.start()
    value = x[...]
    scale = root_scale(value)
    unit = value * scale
    for flip in (1, 2, 3):
        hand_normed(flip).wait_recv()
        normed_grad = normed_grad + normed_recv[flip - 1].astype(f32)
    grad_rows[5:6, :] = jnp.sum(normed_grad * unit, axis=0, keepdims=True)
    scaled = normed_grad * gain_attn[layer : layer + 1, :]
    grad_next[...] = mid_grad + scale * (scaled - unit * jnp.mean(unit * scaled, axis=-1, keepdims=True))
    if earlier:
        earlier.finish()
    if last:
        swap.wait((0,))
        swap.drain()
    for copy in stores(range(6)) + stores_late:
        copy.wait()
    for copy in to_core() + second():
        copy.wait_send()
    for flip in (1, 2):
        gather(flip, block).wait_send()
        relay(flip, here.flipped(flip)).wait_send()
    for flip in (1, 2, 3):
        hand_normed(flip).wait_send()
    for step in range(1, parts):
        hand_pair(step, 0).wait_send()
    for step in range(1, experts):
        for half in range(2):
            hand_slots(half, step, here.expert).wait_send()
            hand_answer(half, step, here.expert).wait_send()


VMEM = pl.BlockSpec(memory_space=pltpu.VMEM)
ANY = pl.BlockSpec(memory_space=pl.ANY)
DMA = pltpu.SemaphoreType.DMA


def forward_layer(layer, layers, begin, going, weights):
    parts, experts = lax.axis_size("context"), lax.axis_size("expert")
    w_in = weights[7]
    width, hidden = w_in.shape[2:]
    count = BLOCK
    wide, packed = 3 * HEAD, 5 * BLOCK
    room = count * 5 // (4 * experts)
    cut = room // 32 * 16
    shape, scratch = jax.ShapeDtypeStruct, pltpu.VMEM
    first = begin is not None
    gives = Saved(
        x=shape((count, width), f32),
        grad=shape((count, width), bf16),
        marks=shape((8, count), jnp.int32),
        bias=shape((3, 5, BLOCK, BLOCK), f32),
        select=shape((experts, room, count), bf16),
        chosen=shape((count, BLOCK), f32),
        w_qkv=shape((width, packed), bf16),
        turned=shape((width, GROUP * count), bf16),
        query=shape((GROUP, count, 3 * BLOCK), bf16),
        pair=shape((parts, GROUP, count, 2 * wide), bf16),
        merged=shape((GROUP, count, 3 * BLOCK), f32),
        log_total=shape((GROUP, count, BLOCK), f32),
        middle=shape((count, width), f32),
        router=shape((count, BLOCK), f32),
        picked=shape((count, width), bf16),
        arrived=shape((experts, cut, width), bf16),
        arrived_more=shape((experts, room - cut, width), bf16),
        before=shape((experts * room, hidden), f32),
        x_next=shape((count, width), f32),
    )
    far = Saved(*[VMEM] * len(gives))._replace(
        w_qkv=ANY, turned=ANY, query=ANY, pair=ANY, merged=ANY, log_total=ANY, before=ANY
    )
    skipped = 0 if first else 4
    start = list(begin) if first else [going.x_next, going.marks, going.bias]
    start_specs = [VMEM] * 4 + [pl.BlockSpec(memory_space=pltpu.SMEM)] if first else [VMEM] * 3
    made = pl.pallas_call(
        functools.partial(forward_kernel, layer, layers, parts, experts, first),
        out_shape=list(gives[skipped:]),
        in_specs=start_specs + [VMEM] * 3 + [ANY] * 6,
        out_specs=list(far[skipped:]),
        scratch_shapes=[
            scratch((width, packed), bf16),
            scratch((width, GROUP * count), bf16),
            scratch((GROUP, count, 3 * BLOCK), bf16),
            scratch((parts, GROUP, count, 2 * wide), bf16),
            scratch((GROUP, count, 3 * BLOCK), f32),
            scratch((GROUP, count, BLOCK), f32),
            scratch((GROUP, count, wide), bf16),
            scratch((experts * room, hidden), f32),
            scratch((GROUP, count, width), bf16),
            scratch((width, 6 * BLOCK), bf16),
            scratch((width, width), bf16),
            scratch((width, hidden), bf16),
            scratch((hidden, width), bf16),
            scratch((parts * GROUP, count, BLOCK), f32),
            scratch((GROUP, count, wide), bf16),
            scratch((experts, cut, width), bf16),
            scratch((experts, room - cut, width), bf16),
            scratch((experts * room, width), f32),
            *[scratch((experts, cut, width), bf16), scratch((experts, room - cut, width), bf16)] * 2,
            DMA((6,)),
            DMA((7,)),
            DMA((4,)),
            DMA((4,)),
            DMA((parts - 1, GROUP)),
            DMA((parts - 1, GROUP)),
            DMA((3,)),
            DMA((3,)),
            DMA((2, experts - 1)),
            DMA((2, experts - 1)),
            DMA((2, experts - 1)),
            DMA((2, experts - 1)),
        ]
        + ([scratch((count, width), bf16), scratch((8, count), jnp.int32), DMA((3,)), DMA((3,))] if first else []),
        compiler_params=pltpu.CompilerParams(
            collective_id=layer, has_side_effects=True, vmem_limit_bytes=60 * 2**20
        ),
        name="layer_forward",
    )(*start, *weights)
    return Saved(*([] if first else [going.x_next, going.grad, going.marks, going.bias]), *made)


def backward_layer(layer, layers, grad, saved, bias_before, left, weights, x_last, table):
    gain_attn, gain_moe, w_router, _, _, _, w_output, w_in, w_out = weights
    w_qkv, select, bias = saved.w_qkv, saved.select, saved.bias
    count, width = grad.shape
    parts, experts = lax.axis_size("context"), lax.axis_size("expert")
    wide = 3 * HEAD
    room = select.shape[1]
    hidden = w_in.shape[3]
    shape = jax.ShapeDtypeStruct
    scratch = pltpu.VMEM
    span = GROUP * count
    rows_in, rows_out = width // (GROUP * parts), hidden // (GROUP * parts)
    tall = rows_in // experts
    fars = parts // 2
    specs, gives, given_specs, needs = earlier_call(parts, experts, left, None) if left else ([], [], [], [])
    taken = present(taken_from(left, None)) if left else []
    gives = present(gives)
    cut = saved.arrived.shape[1]
    own_gives = Own(
        grad_next=shape((count, width), f32),
        in_across=shape((fars, rows_in, hidden), bf16),
        in_beside=shape((fars, rows_in, hidden), bf16),
        in_own=shape((fars, rows_in, hidden), bf16),
        out_across=shape((fars, rows_out, width), bf16),
        out_beside=shape((fars, rows_out, width), bf16),
        out_own=shape((fars, rows_out, width), bf16),
        qkv=shape((GROUP, parts, experts, tall, w_qkv.shape[1]), bf16),
        output=shape((2, parts, experts, tall, width // 2), bf16),
        bias=shape((table, 128) if table else bias.shape, f32),
        rows=shape((8, width), f32),
    )
    own_specs = [VMEM] + [ANY] * 7 + [VMEM, VMEM if table else ANY, VMEM]
    last = int(x_last is not None)
    counts = (24, len(taken), len(own_gives), len(gives), len(needs), last)
    given = pl.pallas_call(
        functools.partial(backward_and_earlier, layer, parts, experts, counts, bias_before is not None, table),
        out_shape=[*own_gives, *gives] + [shape(grad.shape, bf16)] * last,
        in_specs=[VMEM] * 7 + [ANY] * 7 + [VMEM] * 5 + [ANY] * 5 + specs + [VMEM] * last,
        out_specs=own_specs + given_specs + [VMEM] * last,
        scratch_shapes=[
            scratch(bias.shape, f32),
            scratch(saved.turned.shape, bf16),
            scratch(saved.query.shape, bf16),
            scratch(saved.pair.shape, bf16),
            scratch(saved.merged.shape, f32),
            scratch(saved.log_total.shape, f32),
            scratch((GROUP, parts, experts, tall, w_qkv.shape[1]), bf16),
            scratch(bias.shape, f32),
            scratch((GROUP, parts, rows_in, hidden), bf16),
            scratch((GROUP, parts, rows_out, width), bf16),
            scratch((2, parts, rows_in, hidden), bf16),
            scratch((2, parts, rows_out, width), bf16),
            scratch((fars, rows_in, hidden), bf16),
            scratch((fars, rows_out, width), bf16),
            scratch((wide, width), f32),
            scratch((width, w_qkv.shape[1]), bf16),
            scratch((3 * BLOCK, width), bf16),
            *[scratch((experts, cut, width), bf16), scratch((experts, room - cut, width), bf16)] * 4,
            scratch((experts * room, width), bf16),
            scratch((GROUP, count, width), bf16),
            scratch((GROUP, count, 3 * BLOCK), bf16),
            scratch((parts - 1, 2 * wide, span), bf16),
            scratch((parts - 1, 2 * wide, span), bf16),
            scratch((GROUP, count, w_qkv.shape[1]), bf16),
            scratch((GROUP - 1, count, width), bf16),
            scratch((GROUP - 1, count, width), bf16),
            DMA((14,)),
            DMA((2, experts - 1)),
            DMA((2, experts - 1)),
            DMA((2, experts - 1)),
            DMA((2, experts - 1)),
            DMA((4,)),
            DMA((4,)),
            DMA((parts - 1,)),
            DMA((parts - 1,)),
            DMA((3,)),
            DMA((3,)),
            DMA((2, 2)),
            DMA((2, 2)),
            DMA((2, fars)),
            DMA((2, fars)),
            DMA((8, fars)),
            *needs,
            *([scratch(grad.shape, bf16), DMA((1,)), DMA((1,))] if last else []),
        ],
        compiler_params=pltpu.CompilerParams(
            collective_id=layers + layer,
            has_side_effects=True,
            vmem_limit_bytes=(60 if parts <= 2 else 63) * 2**20,
        ),
        name="layer_backward",
    )(
        grad,
        saved.x,
        gain_attn,
        gain_moe,
        w_router,
        select,
        saved.chosen,
        bias,
        bias if bias_before is None else bias_before,
        saved.turned,
        saved.query,
        saved.pair,
        saved.merged,
        saved.log_total,
        saved.middle,
        saved.router,
        saved.picked,
        saved.arrived,
        saved.arrived_more,
        saved.before,
        w_qkv,
        w_output,
        w_in,
        w_out,
        *taken,
        *([x_last] if last else []),
    )
    own, sums = given[: len(own_gives)], given[len(own_gives) : len(own_gives) + len(gives)]
    return Own(*own), Given(*sums) if sums else None, given[-1]


def on_device(
    tokens,
    w_query,
    w_key,
    w_value,
    w_output,
    rel_bias,
    gain_attn,
    gain_moe,
    w_router,
    w_in,
    w_out,
    routes,
    kept,
    cotangent,
):
    experts = w_router.shape[2]
    layers = w_query.shape[0]
    parts = lax.axis_size("context")
    weights = (gain_attn, gain_moe, jnp.swapaxes(w_router, 1, 2), w_key, w_value, w_query, w_output, w_in, w_out)
    saved, going = [], None
    for layer in range(layers):
        begin = (tokens[0], cotangent[0], routes[:, 0, :, 0], kept[:, 0], rel_bias) if layer == 0 else None
        going = forward_layer(layer, layers, begin, going, weights)
        saved.append(going)
    grad, bias_grad = saved[0].grad, None
    left, lefts, sums = None, [], []
    for layer in reversed(range(layers)):
        x_last = going.x_next if layer == layers - 1 else None
        carried = left if parts == 2 else None
        own, done, swapped = backward_layer(layer, layers, grad, saved[layer], bias_grad, carried, weights, x_last, None if layer else rel_bias.shape[0])
        if x_last is not None:
            out = swapped[None]
        if done:
            sums.insert(0, done)
        grad, bias_grad = own.grad_next, own.bias
        left = own
        lefts.insert(0, left)
        if layer == 0:
            others = list(zip(lefts[1:], sums, strict=True)) if parts == 2 else ()
            done, d_tokens, finals = finish(left, rel_bias.shape[0], 2 * layers, grad, others)
            sums.insert(0, done)
        elif parts > 2:
            sums.insert(0, finish(left, None, 2 * layers + layer)[0])

    def experts_sum(own, from_across, from_beside):
        total = own.astype(f32) + from_across.astype(f32) + from_beside.astype(f32)
        if parts == 2:
            return total[0]
        groups = [[2 * far + level for far in range(parts // 2)] for level in range(2)]
        total = lax.psum_scatter(total.astype(bf16), "context", scatter_dimension=0, axis_index_groups=groups)
        return total.astype(f32)

    if finals:
        grad_in, grad_out = (item.astype(f32) for item in finals)
    else:
        grad_in = jnp.stack(
            [experts_sum(a.in_own, b.in_from_across, b.in_from_beside) for a, b in zip(lefts, sums)]
        )
        grad_out = jnp.stack(
            [experts_sum(a.out_own, b.out_from_across, b.out_from_beside) for a, b in zip(lefts, sums)]
        )
    rank = (lax.axis_index("dp") * parts + lax.axis_index("context")) * experts + lax.axis_index("expert")
    tall = sums[0].sums.shape[1]
    rows = jnp.stack([item.rows_sum for item in sums])
    rows = lax.dynamic_slice_in_dim(rows, rank * tall, tall, 2)
    key_out, value_out, query_out, output_out = (
        jnp.stack([item.sums[kind] for item in sums]) for kind in range(4)
    )
    return (
        out,
        d_tokens[None],
        query_out,
        key_out,
        value_out,
        output_out,
        sums[0].table_out[:, : rel_bias.shape[1]],
        rows[:, 5],
        rows[:, 4],
        jnp.swapaxes(rows[:, :experts], 1, 2),
        grad_in[:, None],
        grad_out[:, None],
    )


def solution(mesh):
    in_specs = (
        P("dp", ("context", "expert"), None),
        P(),
        P(),
        P(),
        P(),
        P(),
        P(),
        P(),
        P(),
        P(None, "expert", None, None),
        P(None, "expert", None, None),
        P(None, "dp", ("context", "expert"), None),
        P(None, "dp", ("context", "expert")),
        P("dp", ("context", "expert"), None),
    )
    out_specs = (
        P("dp", ("context", "expert"), None),
        P("dp", ("context", "expert"), None),
        P(None, ("dp", "context", "expert"), None),
        P(None, ("dp", "context", "expert"), None),
        P(None, ("dp", "context", "expert"), None),
        P(None, ("dp", "context", "expert"), None),
        P(),
        P(None, ("dp", "context", "expert")),
        P(None, ("dp", "context", "expert")),
        P(None, ("dp", "context", "expert"), None),
        P(None, "expert", ("dp", "context"), None),
        P(None, "expert", ("dp", "context"), None),
    )
    return jax.shard_map(
        on_device, mesh=mesh, in_specs=in_specs, out_specs=out_specs, check_vma=False
    )
```
